32 devices in a mesh: ctx: 16 (over z, y, core), ch: 2 (over x).
Axes of the slice: x: 2, y: 2, z: 4, core: 2. Of those that a mesh axis runs over, the one named last changes fastest.
Arguments:
- query_proj: bfloat16 [2048, 4096], P('ctx', 'ch'), may hold values from -6 to 6
- key_proj: bfloat16 [2048, 4096], P('ctx', 'ch'), may hold values from -6 to 6
- value_proj: bfloat16 [2048, 4096], P('ctx', 'ch'), may hold values from -6 to 6
- output_grad: bfloat16 [2048, 4096], P('ctx', 'ch'), may hold values from -6 to 6
- residue: float32 [4096, 16], P(('ch', 'ctx')), may hold values from -5 to 5
- decay_rate: float32 [4096, 16], P(('ch', 'ctx')), may hold values from 4.8828126e-05 to 0.0625
Outputs:
- query_grad: bfloat16 [2048, 4096], P('ctx', 'ch')
- key_grad: bfloat16 [2048, 4096], P('ctx', 'ch')
- value_grad: bfloat16 [2048, 4096], P('ctx', 'ch')
- residue_grad: float32 [4096, 16], P(('ch', 'ctx'))
- log_rate_grad: float32 [4096, 16], P(('ch', 'ctx'))
The draws below stay inside these ranges and needn't reach their ends.
All inputs are finite; a program needn't handle non-finite values.
Results may differ from the reference program's by a relative error of at most 0.0085.
Values may be sent and summed in bfloat16 or wider, within the bound.
No kernel may reach another device: no remote copies, remote signals or barrier semaphores. Data moves between devices by JAX's collectives and lax.ppermute only.
A program may use at most 64 MiB of HBM per device.

```python
import math
import jax
import jax.numpy as jnp
from jax import lax

C = 4096
MODES = 16
TOKENS = 2048


def shard_levels(key, extent, pieces, smallest, top_value):
    def one(position, blocks):
        draws = jax.random.uniform(jax.random.fold_in(jax.random.fold_in(key, 6), position), (blocks,), jnp.float32, smallest / len(pieces), top_value / len(pieces))
        return jnp.repeat(jnp.exp(draws), extent[position] // blocks).reshape((-1,) + (1,) * (len(extent) - position - 1))

    gain = one(*pieces[0])
    for cut in pieces[1:]:
        gain = gain * one(*cut)
    return gain


def centred(stream_key, dims, scale, bound, cuts=(), kind=jnp.bfloat16):
    result = scale * jax.random.normal(stream_key, dims, jnp.float32)
    if cuts:
        result = result * shard_levels(stream_key, dims, cuts, -0.22, 0.18)
    return jnp.clip(result, -bound, bound).astype(kind)


def setup_inputs(seed: int = 0) -> dict:
    splits = jax.random.split(jax.random.key(seed), 7)
    query_proj = centred(splits[0], (TOKENS, C), 1.0, 6.0, ((0, 16), (1, 2)))
    key_proj = centred(splits[1], (TOKENS, C), 1.0, 6.0, ((0, 16), (1, 2)))
    value_proj = centred(splits[2], (TOKENS, C), 1.0, 6.0, ((0, 16), (1, 2)))
    output_grad = centred(splits[3], (TOKENS, C), 1.0, 6.0, ((0, 16), (1, 2)))
    residue = centred(splits[4], (C, MODES), 0.35, 5.0, ((0, 32),), jnp.float32)
    decay_rate = jnp.clip(jnp.exp(math.log(0.0625) - 7.1546153 * jax.random.uniform(splits[5], (C, MODES), jnp.float32) ** shard_levels(splits[5], (C, MODES), ((0, 32),), -0.2, 0.2)), 4.882812572759576e-05, 0.0625)
    return dict(query_proj=query_proj, key_proj=key_proj, value_proj=value_proj, output_grad=output_grad, residue=residue, decay_rate=decay_rate)


def filter_bank(residue, decay_rate):
    positions = jnp.arange(TOKENS, dtype=jnp.float32)[None, :]
    filters = jnp.zeros((residue.shape[0], TOKENS), jnp.float32)
    for mode_index in range(MODES):
        rate = decay_rate[:, mode_index:mode_index + 1]
        filters = filters + residue[:, mode_index:mode_index + 1] * (jnp.sqrt(rate) * jnp.exp(-rate * positions))
    return filters

def parameter_grads(lag_grad, residue, decay_rate):
    positions = jnp.arange(TOKENS, dtype=jnp.float32)[None, :]
    residue_cols = []
    log_cols = []
    for mode_index in range(MODES):
        rate = decay_rate[:, mode_index:mode_index + 1]
        basis = jnp.sqrt(rate) * jnp.exp(-rate * positions)
        residue_cols.append(lax.optimization_barrier(jnp.sum(lag_grad * basis, axis=1)))
        log_cols.append(lax.optimization_barrier(jnp.sum(lag_grad * basis * (0.5 - rate * positions), axis=1)) * residue[:, mode_index])
    return (jnp.stack(residue_cols, axis=1), jnp.stack(log_cols, axis=1))

def reference(query_proj, key_proj, value_proj, output_grad, residue, decay_rate):
    length = 2 * TOKENS
    block_width = min(C, 256)
    blocks = C // block_width

    def regroup(whole):
        return whole.reshape(TOKENS, blocks, block_width).transpose(1, 0, 2)

    def one_block(block):
        query_rows, key_rows, value_rows, upstream, residue_rows, rate_rows = block
        filters = filter_bank(residue_rows, rate_rows)
        filter_spec = jnp.fft.rfft(filters, n=length, axis=1)
        gated = (key_rows.astype(jnp.float32) * value_rows.astype(jnp.float32)).astype(jnp.bfloat16)
        gate_grad = (upstream.astype(jnp.float32) * query_rows.astype(jnp.float32)).astype(jnp.bfloat16)
        gate_spec = jnp.fft.rfft(gated.astype(jnp.float32).T, n=length, axis=1)
        grad_spec = jnp.fft.rfft(gate_grad.astype(jnp.float32).T, n=length, axis=1)
        conv_out = jnp.fft.irfft(filter_spec * gate_spec, n=length, axis=1)[:, :TOKENS].astype(jnp.bfloat16).T
        conv_grad = jnp.fft.irfft(jnp.conj(filter_spec) * grad_spec, n=length, axis=1)[:, :TOKENS].astype(jnp.bfloat16).T
        lag_grad = jnp.fft.irfft(jnp.conj(gate_spec) * grad_spec, n=length, axis=1)[:, :TOKENS]
        query_grad = (upstream.astype(jnp.float32) * conv_out.astype(jnp.float32)).astype(jnp.bfloat16)
        key_grad = (conv_grad.astype(jnp.float32) * value_rows.astype(jnp.float32)).astype(jnp.bfloat16)
        value_grad = (conv_grad.astype(jnp.float32) * key_rows.astype(jnp.float32)).astype(jnp.bfloat16)
        residue_grad, log_rate_grad = parameter_grads(lag_grad, residue_rows, rate_rows)
        return (query_grad, key_grad, value_grad, residue_grad, log_rate_grad)
    outs = lax.map(one_block, (regroup(query_proj), regroup(key_proj), regroup(value_proj), regroup(output_grad), residue.reshape(blocks, block_width, MODES), decay_rate.reshape(blocks, block_width, MODES)))

    def ungroup(parts):
        return parts.transpose(1, 0, 2).reshape(TOKENS, C)
    scale = TOKENS ** (-0.5)
    return (ungroup(outs[0]), ungroup(outs[1]), ungroup(outs[2]), outs[3].reshape(C, MODES) * scale, outs[4].reshape(C, MODES) * scale)
```

```python
import functools

import jax
import jax.numpy as jnp
from jax import lax
from jax.experimental import pallas as pl
from jax.experimental.pallas import tpu as pltpu
from jax.sharding import PartitionSpec as P

LANES = 128
SETS = 2
F32 = jnp.float32
BF16 = jnp.bfloat16


def load_rows(ref, start, size, stride):
    return ref[pl.ds(start, size, stride=stride), :]


def gate_kernel(q_ref, k_ref, v_ref, u_ref, x_ref, g_ref, *, groups):
    tokens = q_ref.shape[0]
    members = groups // SETS

    def body(tile, _):
        rows = pl.ds(pl.multiple_of(tile * 16, 16), 16)
        for group in range(groups):
            member, which = group // SETS, group % SETS
            cols = slice(group * LANES, (group + 1) * LANES)
            x = (k_ref[rows, cols].astype(F32) * v_ref[rows, cols].astype(F32)).astype(BF16).astype(F32)
            g = (u_ref[rows, cols].astype(F32) * q_ref[rows, cols].astype(F32)).astype(BF16).astype(F32)
            for half in range(2):
                where = pl.ds((tile * 16 + half * 8) * members + member, 8, stride=members)
                x_ref[which, where, :] = x[half * 8 : half * 8 + 8]
                g_ref[which, where, :] = g[half * 8 : half * 8 + 8]
        return 0

    lax.fori_loop(0, tokens // 16, body, 0)


def param_rows(par_ref, which, param, mode, modes, members):
    return load_rows(par_ref, (which * 2 + param) * modes + mode, members, SETS * 2 * modes)


def state_kernel(x_ref, g_ref, par_ref, s_ref, k_ref, *, tokens, modes, members, unroll):
    for which in range(SETS):
        w = [jnp.exp(-param_rows(par_ref, which, 0, m, modes, members)) for m in range(modes)]

        def step(t, carry):
            s, k = carry
            x = x_ref[which, pl.ds(t * members, members), :]
            g = g_ref[which, pl.ds((tokens - 1 - t) * members, members), :]
            return (
                tuple(w[m] * s[m] + x for m in range(modes)),
                tuple(w[m] * k[m] + g for m in range(modes)),
            )

        zero = tuple(jnp.zeros((members, LANES), F32) for _ in range(modes))
        s, k = lax.fori_loop(0, tokens, step, (zero, zero), unroll=unroll)
        for m in range(modes):
            s_ref[which, pl.ds(m, members, stride=modes), :] = s[m]
            k_ref[which, pl.ds(m, members, stride=modes), :] = k[m]


def local_kernel(x_ref, g_ref, par_ref, y_ref, z_ref, r_ref, d_ref, sd_ref, kd_ref, *, tokens, modes, members, unroll, part):
    for which in range(SETS):
        for first in range(0, modes, part):
            rate = [param_rows(par_ref, which, 0, first + m, modes, members) for m in range(part)]
            w = [jnp.exp(-rate[m]) for m in range(part)]
            amp = [param_rows(par_ref, which, 1, first + m, modes, members) * jnp.sqrt(rate[m]) for m in range(part)]
            zero = tuple(jnp.zeros((members, LANES), F32) for _ in range(part))

            def forward(t, carry):
                h, hd, r, d = carry
                at = pl.ds(t * members, members)
                x = x_ref[which, at, :]
                g = g_ref[which, at, :]
                hd = tuple(w[m] * (hd[m] + h[m]) for m in range(part))
                h = tuple(w[m] * h[m] + x for m in range(part))
                r = tuple(r[m] + g * h[m] for m in range(part))
                d = tuple(d[m] + g * hd[m] for m in range(part))
                y = functools.reduce(jnp.add, [amp[m] * h[m] for m in range(part)])
                if first:
                    y = y + y_ref[which, at, :]
                y_ref[which, at, :] = y
                return h, hd, r, d

            h, hd, r, d = lax.fori_loop(0, tokens, forward, (zero, zero, zero, zero), unroll=unroll)

            def backward(step, carry):
                k, kd = carry
                at = pl.ds((tokens - 1 - step) * members, members)
                g = g_ref[which, at, :]
                kd = tuple(w[m] * (kd[m] + k[m]) for m in range(part))
                k = tuple(w[m] * k[m] + g for m in range(part))
                z = functools.reduce(jnp.add, [amp[m] * k[m] for m in range(part)])
                if first:
                    z = z + z_ref[which, at, :]
                z_ref[which, at, :] = z
                return k, kd

            k, kd = lax.fori_loop(0, tokens, backward, (zero, zero), unroll=unroll)
            for m in range(part):
                at = pl.ds(first + m, members, stride=modes)
                r_ref[which, at, :] = r[m]
                d_ref[which, at, :] = d[m]
                sd_ref[which, at, :] = hd[m]
                kd_ref[which, at, :] = kd[m]


def finish_kernel(
    y_ref, z_ref, par_ref, hin_ref, kin_ref, k_ref, v_ref, u_ref, dq_ref, dk_ref, dv_ref, yo_ref, zo_ref,
    *, tokens, modes, members, unroll,
):
    groups = members * SETS
    for which in range(SETS):
        rate = [param_rows(par_ref, which, 0, m, modes, members) for m in range(modes)]
        w = [jnp.exp(-rate[m]) for m in range(modes)]
        amp = [param_rows(par_ref, which, 1, m, modes, members) * jnp.sqrt(rate[m]) * w[m] for m in range(modes)]
        p = tuple(amp[m] * hin_ref[which, pl.ds(m, members, stride=modes), :] for m in range(modes))
        q = tuple(amp[m] * kin_ref[which, pl.ds(m, members, stride=modes), :] for m in range(modes))

        def step(t, carry):
            p, q = carry
            at = pl.ds(t * members, members)
            back = pl.ds((tokens - 1 - t) * members, members)
            yo_ref[which, at, :] = y_ref[which, at, :] + functools.reduce(jnp.add, p)
            zo_ref[which, back, :] = z_ref[which, back, :] + functools.reduce(jnp.add, q)
            return tuple(w[m] * p[m] for m in range(modes)), tuple(w[m] * q[m] for m in range(modes))

        lax.fori_loop(0, tokens, step, (p, q), unroll=unroll)

    def body(tile, _):
        rows = pl.ds(pl.multiple_of(tile * 16, 16), 16)
        for group in range(groups):
            member, which = group // SETS, group % SETS
            cols = slice(group * LANES, (group + 1) * LANES)
            halves = [pl.ds((tile * 16 + half * 8) * members + member, 8, stride=members) for half in range(2)]
            y = jnp.concatenate([yo_ref[which, at, :] for at in halves], axis=0).astype(BF16).astype(F32)
            z = jnp.concatenate([zo_ref[which, at, :] for at in halves], axis=0).astype(BF16).astype(F32)
            dq_ref[rows, cols] = (u_ref[rows, cols].astype(F32) * y).astype(BF16)
            dk_ref[rows, cols] = (z * v_ref[rows, cols].astype(F32)).astype(BF16)
            dv_ref[rows, cols] = (z * k_ref[rows, cols].astype(F32)).astype(BF16)
        return 0

    lax.fori_loop(0, tokens // 16, body, 0)


def call(body, out_shape, n_in, flops, scratch=()):
    whole = pl.BlockSpec(memory_space=pltpu.VMEM)
    return pl.pallas_call(
        body,
        out_shape=out_shape,
        in_specs=[whole] * n_in,
        out_specs=jax.tree.map(lambda _: whole, out_shape),
        scratch_shapes=scratch,
        compiler_params=pltpu.CompilerParams(vmem_limit_bytes=32 * 1024 * 1024),
        cost_estimate=pl.CostEstimate(flops=flops, bytes_accessed=4 * 1024 * 1024, transcendentals=0),
    )


def exchange(value, distance, count):
    return lax.ppermute(value, "ctx", [(i, i ^ distance) for i in range(count)])


def gather_params(own, count):
    me = lax.axis_index("ctx")
    value, distance, axis = own, count // 2, 0
    while distance:
        other = exchange(value, distance, count)
        upper = (me // distance) % 2 == 1
        value = jnp.stack([jnp.where(upper, other, value), jnp.where(upper, value, other)], axis=axis)
        distance //= 2
        axis += 1
    return value.reshape((count,) + own.shape)


def scan_states(s, k, rate, count, tokens):
    me = lax.axis_index("ctx")
    core = me % 2
    other = 1 - core

    def fade(rate, chunks):
        return jnp.exp(rate * (-float(tokens) * jnp.asarray(chunks).astype(F32)))

    both = jnp.stack([s, k])
    mine = lax.dynamic_index_in_dim(both, core, 1, keepdims=False)
    theirs = exchange(lax.dynamic_index_in_dim(both, other, 1, keepdims=False).astype(BF16), 1, count).astype(F32)
    rate = lax.dynamic_index_in_dim(rate, core, 0, keepdims=False)
    fade_one = fade(rate, 1)
    first = jnp.where(core == 0, mine, theirs)
    last = jnp.where(core == 0, theirs, mine)
    s_sum = fade_one * first[0] + last[0]
    k_sum = first[1] + fade_one * last[1]
    before = jnp.zeros_like(s_sum)
    after = jnp.zeros_like(s_sum)
    span = 2
    pair = me // 2
    while span < count:
        ways = 4 if span * 4 == count else 2
        place = (me // span) % ways
        inside = 2 * (pair % (span // 2))
        total_s, total_k = s_sum, k_sum
        for hop in range(1, ways):
            partner = place ^ hop
            earlier = partner < place
            if span * ways == count:
                got = exchange(jnp.where(earlier, k_sum, s_sum).astype(BF16), hop * span, count).astype(F32)
                got_s = got_k = got
            else:
                got_s, got_k = exchange(jnp.stack([s_sum, k_sum]).astype(BF16), hop * span, count).astype(F32)
                far = fade(rate, span)
                total_s = jnp.where(earlier, far * got_s + s_sum, far * s_sum + got_s)
                total_k = jnp.where(earlier, got_k + far * k_sum, k_sum + far * got_k)
            gap_before = span * (place - partner - 1) + inside
            gap_after = span * (partner - place - 1) + (span - 2 - inside)
            weight = fade(rate, jnp.where(earlier, gap_before, gap_after))
            before = before + jnp.where(earlier, weight * got_s, 0.0)
            after = after + jnp.where(earlier, 0.0, weight * got_k)
        s_sum, k_sum = total_s, total_k
        span *= ways
    enter_first = jnp.stack([before, last[1] + fade_one * after])
    enter_last = jnp.stack([first[0] + fade_one * before, after])
    keep = jnp.where(core == 0, enter_first, enter_last)
    send = jnp.where(core == 0, enter_last, enter_first)
    got = exchange(send.astype(BF16), 1, count).astype(F32)
    whole = jnp.where(core == 0, jnp.stack([keep, got], 1), jnp.stack([got, keep], 1))
    return whole[0], whole[1]


def local(query_proj, key_proj, value_proj, output_grad, residue, decay_rate):
    tokens, channels = query_proj.shape
    own_channels, modes = residue.shape
    count = lax.axis_size("ctx")
    total_tokens = tokens * count
    groups = channels // LANES
    members = groups // SETS
    sizes = dict(tokens=tokens, modes=modes, members=members)
    work = tokens * channels * modes

    own = jnp.stack([decay_rate.T, residue.T])
    params = gather_params(own, count)
    if own_channels != LANES:
        params = params.transpose(1, 2, 0, 3).reshape(2, modes, groups, LANES).transpose(2, 0, 1, 3)
    rows = params.reshape(groups * 2 * modes, LANES)

    big = jax.ShapeDtypeStruct((SETS, tokens * members, LANES), F32)
    small = jax.ShapeDtypeStruct((SETS, members * modes, LANES), F32)
    gated, gate_grad = call(functools.partial(gate_kernel, groups=groups), (big, big), 4, work)(
        query_proj, key_proj, value_proj, output_grad
    )
    s, k = call(functools.partial(state_kernel, unroll=4, **sizes), (small, small), 3, work * 4)(gated, gate_grad, rows)
    y, z, r, d, s_d, k_d = call(
        functools.partial(local_kernel, unroll=2, part=min(8, modes), **sizes), (big, big) + (small,) * 4, 3, work * 16
    )(gated, gate_grad, rows)

    shape = (SETS, members, modes, LANES)
    s, k, r, d, s_d, k_d = (a.reshape(shape) for a in (s, k, r, d, s_d, k_d))
    rate = params[:, 0].reshape(members, SETS, modes, LANES).transpose(1, 0, 2, 3)
    h_in, k_in = scan_states(s, k, rate, count, tokens)
    w = jnp.exp(-rate)
    r_part = r + w * h_in * k
    d_part = d + w * (h_in * k_d + k_in * (s_d + s)) + float(tokens) * jnp.exp(-rate * float(tokens + 1)) * h_in * k_in

    dq, dk, dv = call(
        functools.partial(finish_kernel, unroll=2, **sizes),
        (jax.ShapeDtypeStruct((tokens, channels), BF16),) * 3,
        8,
        work * 4,
        (pltpu.VMEM(big.shape, F32), pltpu.VMEM(big.shape, F32)),
    )(y, z, rows, h_in.reshape(small.shape), k_in.reshape(small.shape), key_proj, value_proj, output_grad)

    parts = jnp.stack([r_part, d_part], axis=2).transpose(1, 0, 2, 3, 4).reshape(groups, 2, modes, LANES)
    if own_channels != LANES:
        parts = parts.transpose(1, 2, 0, 3).reshape(2, modes, count, own_channels).transpose(2, 0, 1, 3)
    sums = lax.all_to_all(parts, "ctx", split_axis=0, concat_axis=0, tiled=True).sum(axis=0)
    scale = float(total_tokens) ** (-0.5)
    root = jnp.sqrt(decay_rate)
    r_own, d_own = sums[0].T, sums[1].T
    residue_grad = scale * root * r_own
    log_grad = scale * residue * root * (0.5 * r_own - decay_rate * d_own)
    return dq, dk, dv, residue_grad, log_grad


def solution(mesh):
    in_specs = (P("ctx", "ch"),) * 4 + (P(("ch", "ctx"), None),) * 2
    out_specs = (P("ctx", "ch"),) * 3 + (P(("ch", "ctx"), None),) * 2
    return jax.shard_map(local, mesh=mesh, in_specs=in_specs, out_specs=out_specs, check_vma=False)
```

```python
import functools

import jax
import jax.numpy as jnp
from jax import lax
from jax.experimental import pallas as pl
from jax.experimental.pallas import tpu as pltpu
from jax.sharding import PartitionSpec as P

LANES = 128
SETS = 2
STRETCH = 8
F32 = jnp.float32
BF16 = jnp.bfloat16
VMEM = pl.BlockSpec(memory_space=pltpu.VMEM)
SMEM = pl.BlockSpec(memory_space=pltpu.SMEM)
ANY = pl.BlockSpec(memory_space=pl.ANY)
HBM = pl.BlockSpec(memory_space=pltpu.HBM)


def total(terms):
    terms = list(terms)
    while len(terms) > 1:
        terms = [a + b for a, b in zip(terms[::2], terms[1::2])] + terms[len(terms) & ~1 :]
    return terms[0]


def gate_kernel(q_hbm, k_hbm, v_hbm, u_hbm, x_ref, g_ref, stage_ref, sems, *, groups, pieces):
    tokens = q_hbm.shape[0]
    members = groups // SETS
    rows = tokens // pieces
    copies = []
    for piece in range(pieces):
        at = pl.ds(piece * rows, rows)
        for i, ref in enumerate((q_hbm, k_hbm, v_hbm, u_hbm)):
            copies.append(pltpu.make_async_copy(ref.at[at], stage_ref.at[i, at], sems.at[piece, i]))
            copies[-1].start()

    def body(tile, _):
        at = pl.ds(pl.multiple_of(tile * 16, 16), 16)
        for group in range(groups):
            member, which = group // SETS, group % SETS
            cols = slice(group * LANES, (group + 1) * LANES)
            q, k, v, u = (stage_ref[i, at, cols].astype(F32) for i in range(4))
            x = (k * v).astype(BF16).astype(F32)
            g = (u * q).astype(BF16).astype(F32)
            for half in range(2):
                where = pl.ds((tile * 16 + half * 8) * members + member, 8, stride=members)
                x_ref[which, where, :] = x[half * 8 : half * 8 + 8]
                g_ref[which, where, :] = g[half * 8 : half * 8 + 8]
        return 0

    for piece in range(pieces):
        for copy in copies[piece * 4 : piece * 4 + 4]:
            copy.wait()
        lax.fori_loop(piece * rows // 16, (piece + 1) * rows // 16, body, 0)


def param_rows(par_ref, which, param, mode, modes, members):
    return par_ref[pl.ds((which * 2 + param) * modes + mode, members, stride=SETS * 2 * modes), :]


def rate_block(par_ref, which, member, modes):
    start = ((member * SETS + which) * 2) * modes
    return par_ref[pl.ds(pl.multiple_of(start, modes), modes), :]


def lag_kernel(x_ref, g_ref, lag_ref, *, tokens, members):
    for which in range(SETS):

        def step(i, lags):
            base = i * STRETCH
            x = [x_ref[which, pl.ds((base + t) * members, members), :] for t in range(STRETCH)]
            g = [g_ref[which, pl.ds((base + t) * members, members), :] for t in range(STRETCH)]
            return tuple(lags[j] + total([g[t] * x[t - j] for t in range(j, STRETCH)]) for j in range(STRETCH))

        zero = tuple(jnp.zeros((members, LANES), F32) for _ in range(STRETCH))
        lags = lax.fori_loop(0, tokens // STRETCH, step, zero)
        for j in range(STRETCH):
            lag_ref[which, j] = lags[j]


def state_kernel(me_ref, x_ref, g_ref, par_ref, sk_ref, hs_ref, ks_ref, *scratch, tokens, modes, members, flip):
    core = me_ref[0] % SETS
    which = 1 - core if flip else core
    w = [jnp.exp(-param_rows(par_ref, which, 0, m, modes, members)) for m in range(modes)]
    stretches = tokens // STRETCH

    def step(i, carry):
        s, k = carry
        back = stretches - 1 - i
        for m in range(modes):
            hs_ref[i, m] = s[m]
        for t in range(STRETCH):
            x = x_ref[which, pl.ds((i * STRETCH + t) * members, members), :]
            g = g_ref[which, pl.ds((back * STRETCH + STRETCH - 1 - t) * members, members), :]
            s = tuple(w[m] * s[m] + x for m in range(modes))
            k = tuple(w[m] * k[m] + g for m in range(modes))
        for m in range(modes):
            ks_ref[back, m] = k[m]
        return s, k

    zero = tuple(jnp.zeros((members, LANES), F32) for _ in range(modes))
    s, k = lax.fori_loop(0, stretches, step, (zero, zero), unroll=2)
    full = scratch[0] if flip else sk_ref
    for m in range(modes):
        at = pl.ds(m, members, stride=modes)
        full[0, at, :] = s[m]
        full[1, at, :] = k[m]
    if flip:
        sk_ref[...] = full[...].astype(BF16)


def local_kernel(
    me_ref, x_ref, g_ref, lag_ref, hs_ref, ks_ref, par_ref, y_ref, z_ref, sums_ref, *, tokens, modes, members, part, flip
):
    core = me_ref[0] % SETS
    which = 1 - core if flip else core
    stretches = tokens // STRETCH
    length = float(STRETCH)
    taps = [jnp.zeros((members, LANES), F32)] * STRETCH
    zero = jnp.zeros((members, LANES), F32)
    for first in range(0, modes, part):
        rate = [param_rows(par_ref, which, 0, first + m, modes, members) for m in range(part)]
        w = [jnp.exp(-rate[m]) for m in range(part)]
        fade = [jnp.exp(rate[m] * -length) for m in range(part)]
        amp = [param_rows(par_ref, which, 1, first + m, modes, members) * jnp.sqrt(rate[m]) for m in range(part)]
        power = amp
        for j in range(STRETCH):
            taps[j] = taps[j] + total(power)
            power = [power[m] * w[m] for m in range(part)]

        def step(i, carry):
            back = stretches - 1 - i
            x = [x_ref[which, pl.ds((i * STRETCH + t) * members, members), :] for t in range(STRETCH)]
            g = [g_ref[which, pl.ds((back * STRETCH + t) * members, members), :] for t in range(STRETCH)]
            x = [x[t] * float(STRETCH - 1 - t) for t in range(STRETCH - 1)]
            g = [g[t] * float(t) for t in range(STRETCH)]
            out = []
            for m in range(part):
                same, next_, b_k, b_s, sd, kd = carry[m]
                h, k = hs_ref[i, first + m], ks_ref[i, first + m]
                h_back = hs_ref[back, first + m]
                after = lax.rem(i + 1, stretches)
                k_after = jnp.where(i + 1 == stretches, 0.0, ks_ref[after, first + m])
                after = lax.rem(back + 1, stretches)
                k_back = jnp.where(i == 0, 0.0, ks_ref[after, first + m])
                s_own = x[0]
                for t in range(1, STRETCH - 1):
                    s_own = s_own * w[m] + x[t]
                s_own = s_own * w[m]
                k_own = g[STRETCH - 1]
                for t in range(STRETCH - 2, 0, -1):
                    k_own = k_own * w[m] + g[t]
                k_own = k_own * w[m]
                out.append(
                    (
                        same + h * k,
                        next_ + h * k_after,
                        b_k + h_back * k_own,
                        b_s + k_after * s_own,
                        fade[m] * (sd + length * h) + s_own,
                        fade[m] * (kd + length * k_back) + k_own,
                    )
                )
            return tuple(out)

        sums = lax.fori_loop(0, stretches, step, ((zero,) * 6,) * part, unroll=2)
        for m in range(part):
            same, next_, b_k, b_s, sd, kd = sums[m]
            r, d = lag_ref[which, STRETCH - 1], (length - 1.0) * lag_ref[which, STRETCH - 1]
            for j in range(STRETCH - 2, -1, -1):
                r = r * w[m] + lag_ref[which, j]
                d = d * w[m] + float(j) * lag_ref[which, j]
            at = pl.ds(first + m, members, stride=modes)
            sums_ref[0, at, :] = r + w[m] * (same - fade[m] * next_)
            sums_ref[1, at, :] = d + w[m] * (b_k + b_s + same + (length - 1.0) * (fade[m] * next_))
            sums_ref[2, at, :] = sd
            sums_ref[3, at, :] = kd

    def within(i, _):
        at = [pl.ds((i * STRETCH + t) * members, members) for t in range(STRETCH)]
        x = [x_ref[which, at[t], :] for t in range(STRETCH)]
        g = [g_ref[which, at[t], :] for t in range(STRETCH)]
        for t in range(STRETCH):
            y_ref[at[t], :] = total([taps[j] * x[t - j] for j in range(t + 1)])
            z_ref[at[t], :] = total([taps[j] * g[t + j] for j in range(STRETCH - t)])
        return 0

    lax.fori_loop(0, stretches, within, 0, unroll=2)


def flags(bit):
    bit = bit.astype(F32)
    return bit, 1.0 - bit


def put_message(ref, me, span, at, s, k, last):
    if last:
        earlier, later = flags((me // span) % 2 == 1)
        ref[at, :] = (earlier * k + later * s).astype(BF16)
    else:
        ref[0, at, :] = s.astype(BF16)
        ref[1, at, :] = k.astype(BF16)


def pair_kernel(me_ref, mine_ref, got_ref, par_ref, tot_ref, message_ref, *, tokens, modes, members, last):
    me = me_ref[0]
    core = me % SETS
    second, first = flags(core == 1)
    for member in range(members):
        at = pl.ds(member * modes, modes)
        fade = jnp.exp(rate_block(par_ref, core, member, modes) * -float(tokens))
        s, k = mine_ref[0, at, :], mine_ref[1, at, :]
        gs, gk = got_ref[0, at, :].astype(F32), got_ref[1, at, :].astype(F32)
        s_sum = second * (fade * gs + s) + first * (fade * s + gs)
        k_sum = second * (gk + fade * k) + first * (k + fade * gk)
        tot_ref[0, at, :] = s_sum
        tot_ref[1, at, :] = k_sum
        put_message(message_ref, me, SETS, at, s_sum, k_sum, last)


def level_kernel(
    me_ref, tot_ref, got_ref, enter_ref, par_ref, out_ref, new_ref, message_ref, *, tokens, modes, members, span, last
):
    me = me_ref[0]
    core = me % SETS
    earlier, later = flags((me // span) % 2 == 1)
    inside = (me // 2) % (span // 2) * 2
    gap = earlier * inside.astype(F32) + later * (span - 2 - inside).astype(F32)
    for member in range(members):
        at = pl.ds(member * modes, modes)
        rate = rate_block(par_ref, core, member, modes)
        far = jnp.exp(rate * -float(tokens * span))
        weight = jnp.exp(rate * (gap * -float(tokens)))
        s, k = tot_ref[0, at, :], tot_ref[1, at, :]
        gs, gk = got_ref[0, at, :].astype(F32), got_ref[1, at, :].astype(F32)
        s_sum = earlier * (far * gs + s) + later * (far * s + gs)
        k_sum = earlier * (gk + far * k) + later * (k + far * gk)
        out_ref[0, at, :] = s_sum
        out_ref[1, at, :] = k_sum
        before = earlier * (weight * gs)
        after = later * (weight * gk)
        if span > 2:
            before += enter_ref[0, at, :]
            after += enter_ref[1, at, :]
        new_ref[0, at, :] = before
        new_ref[1, at, :] = after
        put_message(message_ref, me, span * 2, at, s_sum, k_sum, last)


def enter_kernel(
    me_ref, enter_ref, far_ref, mine_ref, got_ref, par_ref, keep_ref, send_ref, *, tokens, modes, members, span
):
    me = me_ref[0]
    core = me % SETS
    second, first = flags(core == 1)
    earlier, later = flags((me // span) % 2 == 1)
    inside = (me // 2) % (span // 2) * 2
    gap = earlier * inside.astype(F32) + later * (span - 2 - inside).astype(F32)
    for member in range(members):
        at = pl.ds(member * modes, modes)
        rate = rate_block(par_ref, core, member, modes)
        value = jnp.exp(rate * (gap * -float(tokens))) * far_ref[at, :].astype(F32)
        before, after = earlier * value, later * value
        if span > 2:
            before += enter_ref[0, at, :]
            after += enter_ref[1, at, :]
        fade = jnp.exp(rate * -float(tokens))
        s, k = mine_ref[0, at, :], mine_ref[1, at, :]
        gs, gk = got_ref[0, at, :].astype(F32), got_ref[1, at, :].astype(F32)
        near_s = (second * gs + first * s) + fade * before
        near_k = (first * gk + second * k) + fade * after
        keep_ref[0, at, :] = first * before + second * near_s
        keep_ref[1, at, :] = first * near_k + second * after
        send_ref[0, at, :] = (second * before + first * near_s).astype(BF16)
        send_ref[1, at, :] = (second * near_k + first * after).astype(BF16)


def finish_kernel(me_ref, y_ref, z_ref, hs_ref, ks_ref, par_ref, in_ref, k_ref, v_ref, u_ref, *refs, tokens, modes, members, flip):
    if flip:
        dq_ref, dk_ref, dv_ref, dq_hbm, dk_hbm, dv_hbm, token_ref, yo_ref, zo_ref, enter_ref, sems = refs[3:]
    else:
        dq_ref, dk_ref, dv_ref, token_ref, yo_ref, zo_ref, enter_ref = refs
    core = me_ref[0] % SETS
    which = 1 - core if flip else core
    stretches = tokens // STRETCH
    enter_ref[...] = in_ref[...].astype(F32)
    rate = [param_rows(par_ref, which, 0, m, modes, members) for m in range(modes)]
    w = [jnp.exp(-rate[m]) for m in range(modes)]
    fade = [jnp.exp(rate[m] * -float(STRETCH)) for m in range(modes)]
    amp = [param_rows(par_ref, which, 1, m, modes, members) * jnp.sqrt(rate[m]) * w[m] for m in range(modes)]
    h = tuple(enter_ref[0, pl.ds(m, members, stride=modes), :] for m in range(modes))
    k = tuple(enter_ref[1, pl.ds(m, members, stride=modes), :] for m in range(modes))

    def step(i, carry):
        h, k = carry
        back = stretches - 1 - i
        p = [amp[m] * (h[m] + hs_ref[i, m]) for m in range(modes)]
        for t in range(STRETCH):
            at = pl.ds((i * STRETCH + t) * members, members)
            yo_ref[at, :] = y_ref[at, :] + total(p)
            if t < STRETCH - 1:
                p = [w[m] * p[m] for m in range(modes)]
        after = lax.rem(back + 1, stretches)
        q = [amp[m] * (k[m] + jnp.where(i == 0, 0.0, ks_ref[after, m])) for m in range(modes)]
        for t in range(STRETCH):
            at = pl.ds((back * STRETCH + STRETCH - 1 - t) * members, members)
            zo_ref[at, :] = z_ref[at, :] + total(q)
            if t < STRETCH - 1:
                q = [w[m] * q[m] for m in range(modes)]
        return tuple(fade[m] * h[m] for m in range(modes)), tuple(fade[m] * k[m] for m in range(modes))

    lax.fori_loop(0, stretches, step, (h, k), unroll=1)

    copies = []
    token_ref[...] = yo_ref[0:8, :]
    for tile in range(tokens // 16):
        rows = pl.ds(tile * 16, 16)
        for member in range(members):
            cols = pl.ds(pl.multiple_of((member * SETS + which) * LANES, LANES), LANES)
            halves = [pl.ds((tile * 16 + half * 8) * members + member, 8, stride=members) for half in range(2)]
            y = jnp.concatenate([yo_ref[at, :] for at in halves], axis=0).astype(BF16).astype(F32)
            z = jnp.concatenate([zo_ref[at, :] for at in halves], axis=0).astype(BF16).astype(F32)
            dq_ref[rows, cols] = (u_ref[rows, cols].astype(F32) * y).astype(BF16)
            dk_ref[rows, cols] = (z * v_ref[rows, cols].astype(F32)).astype(BF16)
            dv_ref[rows, cols] = (z * k_ref[rows, cols].astype(F32)).astype(BF16)
        if flip:
            for index, (ref, out) in enumerate(((dq_ref, dq_hbm), (dk_ref, dk_hbm), (dv_ref, dv_hbm))):
                copies.append(pltpu.make_async_copy(ref.at[rows], out.at[rows], sems.at[index, tile]))
                copies[-1].start()
    for copy in copies:
        copy.wait()


def join(rate, left, right, length):
    r_a, d_a, sd_a, kd_a, s_a, k_a = left
    r_b, d_b, sd_b, kd_b, s_b, k_b = right
    w = jnp.exp(-rate)
    fade = jnp.exp(rate * -length)
    r = r_a + r_b + w * (s_a * k_b)
    d = d_a + d_b + w * (s_a * kd_b + (sd_a + s_a) * k_b)
    sd = fade * (sd_a + length * s_a) + sd_b
    kd = kd_a + fade * (kd_b + length * k_b)
    return r, d, sd, kd


def sums_kernel(me_ref, mine_ref, theirs_ref, sk_ref, got_ref, par_ref, *refs, tokens, modes, members, span):
    keep_ref, send_ref = refs[-2:]
    me = me_ref[0]
    core = me % SETS
    second, first = flags((me // span) % 2 == 1)
    side = (me // (span * 2)) % 2
    own = (me // 2) % span
    for ref, parity in ((keep_ref, side), (send_ref, 1 - side)):
        for to in range(members // span // 2):
            index = to * 2 + parity
            member = index * span + own
            src = pl.ds(pl.multiple_of(index * modes, modes), modes)
            at = pl.ds(pl.multiple_of(member * modes, modes), modes)
            mine = tuple(mine_ref[i, src, :] for i in range(4)) + (sk_ref[0, at, :], sk_ref[1, at, :])
            theirs = tuple(theirs_ref[i, src, :].astype(F32) for i in range(4)) + tuple(
                got_ref[i, at, :].astype(F32) for i in range(2)
            )
            left = tuple(second * b + first * a for a, b in zip(mine, theirs))
            right = tuple(second * a + first * b for a, b in zip(mine, theirs))
            for i, value in enumerate(join(rate_block(par_ref, core, member, modes), left, right, float(tokens * span))):
                ref[i, pl.ds(to * modes, modes), :] = value.astype(ref.dtype)


def sums_last_kernel(
    me_ref, mine_ref, theirs_ref, sk_ref, far_ref, own_ref, after_ref, r_out, log_out, *, modes, span, scale
):
    me = me_ref[0]
    second, first = flags((me // span) % 2 == 1)
    at = pl.ds(pl.multiple_of(me // 2 * modes, modes), modes)
    r_m, d_m, sd_m, kd_m = (mine_ref[i] for i in range(4))
    r_t, d_t, sd_t, kd_t = (theirs_ref[i].astype(F32) for i in range(4))
    far = far_ref[at, :].astype(F32)
    s_a = second * far + first * sk_ref[0, at, :]
    k_b = second * sk_ref[1, at, :] + first * far
    sd_a = second * sd_t + first * sd_m
    kd_b = second * kd_m + first * kd_t
    rate, residue = own_ref[0], own_ref[1]
    w = jnp.exp(-rate)
    r = r_m + r_t + w * (s_a * k_b)
    d = d_m + d_t + w * (s_a * kd_b + (sd_a + s_a) * k_b)
    root = jnp.sqrt(rate) * scale
    r_out[...] = root * r
    log_out[...] = root * residue * (0.5 * r - rate * d)


def call(body, out_shape, in_specs, flops, out_specs=None, scratch=(), aliases=None):
    return pl.pallas_call(
        body,
        out_shape=out_shape,
        in_specs=in_specs,
        out_specs=jax.tree.map(lambda _: VMEM, out_shape) if out_specs is None else out_specs,
        scratch_shapes=scratch,
        input_output_aliases=aliases or {},
        compiler_params=pltpu.CompilerParams(vmem_limit_bytes=16 * 1024 * 1024),
        cost_estimate=pl.CostEstimate(flops=flops, bytes_accessed=1024 * 1024, transcendentals=0),
    )


def exchange(value, distance, count):
    return lax.ppermute(value, "ctx", [(i, i ^ distance) for i in range(count)])


def tie(*values):
    return lax.optimization_barrier(values)


def local(query_proj, key_proj, value_proj, output_grad, residue, decay_rate):
    tokens, channels = query_proj.shape
    own_channels, modes = residue.shape
    count = lax.axis_size("ctx")
    groups = channels // LANES
    members = groups // SETS
    sizes = dict(tokens=tokens, modes=modes, members=members)
    work = tokens * channels * modes // SETS
    index = lax.axis_index("ctx")
    me = index.astype(jnp.int32).reshape(1)

    def shape(*dims, dtype=F32):
        return jax.ShapeDtypeStruct(dims, dtype)

    rows = members * modes
    gates = shape(SETS, tokens * members, LANES)
    series = shape(tokens * members, LANES)
    pair, pair16 = shape(2, rows, LANES), shape(2, rows, LANES, dtype=BF16)
    one16 = shape(rows, LANES, dtype=BF16)

    (own,) = tie(jnp.stack([decay_rate.T, residue.T]))
    params, distance, axis = own, count // 2, 0
    pieces = 4
    gated, gate_grad = call(
        functools.partial(gate_kernel, groups=groups, pieces=pieces),
        (gates, gates),
        [HBM] * 4,
        work,
        scratch=(pltpu.VMEM((4, tokens, channels), BF16), pltpu.SemaphoreType.DMA((pieces, 4))),
    )(*(pltpu.with_memory_space_constraint(a, pltpu.HBM) for a in (query_proj, key_proj, value_proj, output_grad)))
    while distance:
        other = exchange(params, distance, count)
        if axis == 0:
            other, gated, gate_grad = tie(other, gated, gate_grad)
            (lags,) = call(
                functools.partial(lag_kernel, tokens=tokens, members=members),
                (shape(SETS, STRETCH, members, LANES),),
                [VMEM] * 2,
                work,
            )(gated, gate_grad)
        if axis == 1:
            other, lags = tie(other, lags)
        upper = (index // distance) % 2 == 1
        params = jnp.stack([jnp.where(upper, other, params), jnp.where(upper, params, other)], axis=axis)
        distance //= 2
        axis += 1
    params = params.reshape((count,) + own.shape)
    if own_channels != LANES:
        params = params.transpose(1, 2, 0, 3).reshape(2, modes, groups, LANES).transpose(2, 0, 1, 3)
    par = params.reshape(groups * 2 * modes, LANES)

    entering = shape(tokens // STRETCH, modes, members, LANES)
    states_in = [SMEM, VMEM, VMEM, VMEM]
    sk_other, hs_other, ks_other = call(
        functools.partial(state_kernel, flip=True, **sizes),
        (pair16, entering, entering),
        states_in,
        work * 4,
        scratch=(pltpu.VMEM(pair.shape, F32),),
    )(me, gated, gate_grad, par)
    sk_got = exchange(sk_other, 1, count)
    sk_mine, hs_mine, ks_mine = call(
        functools.partial(state_kernel, flip=False, **sizes), (pair, entering, entering), states_in, work * 4
    )(me, gated, gate_grad, par)

    def within(flip, hs, ks):
        body = functools.partial(local_kernel, part=min(4, modes), flip=flip, **sizes)
        return call(body, (series, series, shape(4, rows, LANES)), [SMEM] + [VMEM] * 6, work * 6)(
            me, gated, gate_grad, lags, hs, ks, par
        )

    top = count // 2
    tot, message = call(
        functools.partial(pair_kernel, last=top == SETS, **sizes), (pair, one16 if top == SETS else pair16), [SMEM] + [VMEM] * 3, rows
    )(me, sk_mine, sk_got, par)
    y_other, z_other, sums_other = within(True, hs_other, ks_other)
    enter, levels, span = sk_mine, {}, SETS
    while span < top:
        got = exchange(message, span, count)
        if span == SETS:
            got, sums_other = tie(got, sums_other)
        levels[span] = tot, got
        last = span * 2 == top
        tot, enter, message = call(
            functools.partial(level_kernel, span=span, last=last, **sizes),
            (pair, pair, one16 if last else pair16),
            [SMEM] + [VMEM] * 4,
            rows,
        )(me, tot, got, enter, par)
        if span == SETS:
            tot, hs_mine, ks_mine = tie(tot, hs_mine, ks_mine)
        span *= 2
    far = exchange(message, top, count)
    y_mine, z_mine, sums_mine = within(False, hs_mine, ks_mine)

    def join_sums(span, kept, theirs, *after):
        half = rows // span // 2
        return call(
            functools.partial(sums_kernel, span=span, **sizes),
            (shape(4, half, LANES), shape(4, half, LANES, dtype=BF16)),
            [SMEM] + [VMEM] * (5 + len(after)),
            rows,
        )(me, kept, theirs, *levels[span], par, *after)

    tree = groups == count and top > 2 * SETS
    if tree:
        levels[1] = (sk_mine, sk_got)
        kept, message = join_sums(1, sums_mine, exchange(sums_other.astype(BF16), 1, count))
        kept, message = join_sums(2, kept, exchange(message, 2, count))
    keep, send = call(functools.partial(enter_kernel, span=top, **sizes), (pair, pair16), [SMEM] + [VMEM] * 5, rows)(
        me, enter, far, sk_mine, sk_got, par
    )
    enter_got = exchange(send, 1, count)
    if tree:
        message, keep = tie(message, keep)

    grads = (shape(tokens, channels, dtype=BF16),) * 3
    token = shape(8, LANES)
    scratch = (pltpu.VMEM(series.shape, F32), pltpu.VMEM(series.shape, F32), pltpu.VMEM(pair.shape, F32))
    finish = functools.partial(finish_kernel, **sizes)
    *done, token_first = call(functools.partial(finish, flip=False), grads + (token,), [SMEM] + [VMEM] * 9, work * 4, None, scratch)(
        me, y_mine, z_mine, hs_mine, ks_mine, par, keep, key_proj, value_proj, output_grad
    )
    *done, token_last = call(
        functools.partial(finish, flip=True),
        grads + grads + (token,),
        [SMEM] + [VMEM] * 12,
        work * 4,
        (VMEM,) * 3 + (ANY,) * 3 + (VMEM,),
        scratch + (pltpu.SemaphoreType.DMA((3, tokens // 16)),),
        {10: 0, 11: 1, 12: 2},
    )(me, y_other, z_other, hs_other, ks_other, par, enter_got, key_proj, value_proj, output_grad, *done)
    done = done[3:]

    scale = float(tokens * count) ** (-0.5)
    if tree:
        span = 4
        while span < top:
            kept, message = join_sums(span, kept, exchange(message, span, count), token_first)
            span *= 2
        out = call(
            functools.partial(sums_last_kernel, modes=modes, span=top, scale=scale),
            (shape(modes, LANES),) * 2,
            [SMEM] + [VMEM] * 6,
            rows,
        )(me, kept, exchange(message, top, count), tot, far, own, token_last)
        residue_grad, log_grad = out[0].T, out[1].T
    else:
        core = index % SETS
        dims = (members, modes, LANES)

        def sets(mine, other):
            mine, other = mine.astype(F32).reshape(dims), other.astype(F32).reshape(dims)
            return jnp.where(core == 0, jnp.stack([mine, other]), jnp.stack([other, mine]))

        h_in, k_in = (sets(keep[i], enter_got[i]) for i in range(2))
        s, k = (sets(sk_mine[i], sk_other[i]) for i in range(2))
        r, d, s_d, k_d = (sets(sums_mine[i], sums_other[i]) for i in range(4))
        rate = params[:, 0].reshape(members, SETS, modes, LANES).transpose(1, 0, 2, 3)
        w = jnp.exp(-rate)
        r_part = r + w * h_in * k
        d_part = d + w * (h_in * k_d + k_in * (s_d + s)) + float(tokens) * jnp.exp(-rate * float(tokens + 1)) * h_in * k_in
        parts = jnp.stack([r_part, d_part], axis=2).transpose(1, 0, 2, 3, 4).reshape(groups, 2, modes, LANES)
        parts = parts.transpose(1, 2, 0, 3).reshape(2, modes, count, own_channels).transpose(2, 0, 1, 3)
        sums = lax.all_to_all(parts, "ctx", split_axis=0, concat_axis=0, tiled=True).sum(axis=0)
        root = scale * jnp.sqrt(decay_rate)
        residue_grad = root * sums[0].T
        log_grad = root * residue * (0.5 * sums[0].T - decay_rate * sums[1].T)
    return (*done, residue_grad, log_grad)


def solution(mesh):
    in_specs = (P("ctx", "ch"),) * 4 + (P(("ch", "ctx"), None),) * 2
    out_specs = (P("ctx", "ch"),) * 3 + (P(("ch", "ctx"), None),) * 2
    return jax.shard_map(local, mesh=mesh, in_specs=in_specs, out_specs=out_specs, check_vma=False)
```

```python
import functools

import jax
import jax.numpy as jnp
from jax import lax
from jax.experimental import pallas as pl
from jax.experimental.pallas import tpu as pltpu
from jax.sharding import PartitionSpec as P

LANES = 128
SETS = 2
STRETCH = 8
F32 = jnp.float32
BF16 = jnp.bfloat16
VMEM = pl.BlockSpec(memory_space=pltpu.VMEM)
SMEM = pl.BlockSpec(memory_space=pltpu.SMEM)
ANY = pl.BlockSpec(memory_space=pl.ANY)
HBM = pl.BlockSpec(memory_space=pltpu.HBM)


def total(terms):
    terms = list(terms)
    while len(terms) > 1:
        terms = [a + b for a, b in zip(terms[::2], terms[1::2])] + terms[len(terms) & ~1 :]
    return terms[0]


def set_columns(member, which):
    return pl.ds(pl.multiple_of((member * SETS + which) * LANES, LANES), LANES)


def gate_kernel(me_ref, q_hbm, k_hbm, v_hbm, u_hbm, own_ref, send_ref, stage_ref, sems, *, members, pieces):
    tokens = q_hbm.shape[0]
    core = me_ref[0] % SETS
    rows = tokens // pieces
    copies = []
    for piece in range(pieces):
        at = pl.ds(piece * rows, rows)
        for i, ref in enumerate((q_hbm, k_hbm, v_hbm, u_hbm)):
            copies.append(pltpu.make_async_copy(ref.at[at], stage_ref.at[i, at], sems.at[piece, i]))
            copies[-1].start()

    def body(tile, _):
        at = pl.ds(pl.multiple_of(tile * 16, 16), 16)
        for out_ref, which in ((own_ref, core), (send_ref, 1 - core)):
            for member in range(members):
                cols = set_columns(member, which)
                q, k, v, u = (stage_ref[i, at, cols].astype(F32) for i in range(4))
                out_ref[0, member, at, :] = (k * v).astype(BF16)
                out_ref[1, member, at, :] = (u * q).astype(BF16)
        return 0

    for piece in range(pieces):
        for copy in copies[piece * 4 : piece * 4 + 4]:
            copy.wait()
        lax.fori_loop(piece * rows // 16, (piece + 1) * rows // 16, body, 0)


def series_kernel(me_ref, own_ref, got_ref, x_ref, g_ref, lag_ref, *, tokens, members):
    core = me_ref[0] % SETS
    for ref, chunk in ((own_ref, core), (got_ref, 1 - core)):

        def body(tile, _):
            rows = pl.ds(pl.multiple_of(tile * 16, 16), 16)
            for member in range(members):
                for i, out_ref in enumerate((x_ref, g_ref)):
                    value = ref[i, member, rows, :].astype(F32)
                    for half in range(2):
                        start = (chunk * tokens + tile * 16 + half * 8) * members + member
                        out_ref[pl.ds(start, 8, stride=members), :] = value[half * 8 : half * 8 + 8]
            return 0

        lax.fori_loop(0, tokens // 16, body, 0)

    def step(i, lags):
        x = [x_ref[pl.ds((i * STRETCH + t) * members, members), :] for t in range(STRETCH)]
        g = [g_ref[pl.ds((i * STRETCH + t) * members, members), :] for t in range(STRETCH)]
        return tuple(lags[j] + total([g[t] * x[t - j] for t in range(j, STRETCH)]) for j in range(STRETCH))

    zero = tuple(jnp.zeros((members, LANES), F32) for _ in range(STRETCH))
    lags = lax.fori_loop(0, SETS * tokens // STRETCH, step, zero)
    for j in range(STRETCH):
        lag_ref[j] = lags[j]


def param_rows(par_ref, param, mode, modes, members):
    return par_ref[pl.ds(param * modes + mode, members, stride=2 * modes), :]


def rate_block(par_ref, member, modes):
    return par_ref[pl.ds(pl.multiple_of(member * 2 * modes, modes), modes), :]


def state_kernel(x_ref, g_ref, par_ref, sk_ref, hs_ref, ks_ref, xw_ref, gw_ref, *, length, modes, members):
    w = [jnp.exp(-param_rows(par_ref, 0, m, modes, members)) for m in range(modes)]
    stretches = length // STRETCH

    def step(i, carry):
        s, k = carry
        back = stretches - 1 - i
        for m in range(modes):
            hs_ref[i, m] = s[m]
        for t in range(STRETCH):
            at = pl.ds((i * STRETCH + t) * members, members)
            at_back = pl.ds((back * STRETCH + STRETCH - 1 - t) * members, members)
            x, g = x_ref[at, :], g_ref[at_back, :]
            xw_ref[at, :] = x * float(STRETCH - 1 - t)
            gw_ref[at_back, :] = g * float(STRETCH - 1 - t)
            s = tuple(w[m] * s[m] + x for m in range(modes))
            k = tuple(w[m] * k[m] + g for m in range(modes))
        for m in range(modes):
            ks_ref[back, m] = k[m]
        return s, k

    zero = tuple(jnp.zeros((members, LANES), F32) for _ in range(modes))
    for m in range(modes):
        ks_ref[stretches, m] = zero[m]
    s, k = lax.fori_loop(0, stretches, step, (zero, zero), unroll=2)
    for m in range(modes):
        at = pl.ds(m, members, stride=modes)
        sk_ref[0, at, :] = s[m]
        sk_ref[1, at, :] = k[m]


def taps_kernel(x_ref, g_ref, par_ref, y_ref, z_ref, *, length, modes, members):
    rate = [param_rows(par_ref, 0, m, modes, members) for m in range(modes)]
    w = [jnp.exp(-rate[m]) for m in range(modes)]
    power = [param_rows(par_ref, 1, m, modes, members) * jnp.sqrt(rate[m]) for m in range(modes)]
    taps = []
    for j in range(STRETCH):
        taps.append(total(power))
        power = [power[m] * w[m] for m in range(modes)]

    def within(i, _):
        at = [pl.ds((i * STRETCH + t) * members, members) for t in range(STRETCH)]
        x = [x_ref[at[t], :] for t in range(STRETCH)]
        g = [g_ref[at[t], :] for t in range(STRETCH)]
        for t in range(STRETCH):
            y_ref[at[t], :] = total([taps[j] * x[t - j] for j in range(t + 1)])
            z_ref[at[t], :] = total([taps[j] * g[t + j] for j in range(STRETCH - t)])
        return 0

    lax.fori_loop(0, length // STRETCH, within, 0, unroll=2)


def flags(bit):
    bit = bit.astype(F32)
    return bit, 1.0 - bit


def put_states(ref, me, span, member, s, k, modes, members, last):
    at = pl.ds(member * modes, modes)
    if last:
        earlier, later = flags((me // span) % 2 == 1)
        ref[at, :] = (earlier * k + later * s).astype(BF16)
    else:
        ref[at, :] = s.astype(BF16)
        ref[pl.ds((members + member) * modes, modes), :] = k.astype(BF16)


def sums_kernel(
    me_ref, x_ref, g_ref, lag_ref, hs_ref, ks_ref, sk_ref, par_ref, sums_ref, message_ref, *kept,
    length, modes, members, part, unroll, last, tree,
):
    stretches = length // STRETCH
    width = float(STRETCH)
    zero = jnp.zeros((members, LANES), F32)
    for first in range(0, modes, part):
        rate = [param_rows(par_ref, 0, first + m, modes, members) for m in range(part)]
        w = [jnp.exp(-rate[m]) for m in range(part)]
        fade = [jnp.exp(rate[m] * -width) for m in range(part)]

        def step(i, carry):
            back = stretches - 1 - i
            x = [x_ref[pl.ds((i * STRETCH + t) * members, members), :] for t in range(STRETCH - 1)]
            g = [g_ref[pl.ds((back * STRETCH + t) * members, members), :] for t in range(STRETCH)]
            out = []
            for m in range(part):
                same, next_, b_k, b_s, sd, kd = carry[m]
                h, k = hs_ref[i, first + m], ks_ref[i, first + m]
                h_back = hs_ref[back, first + m]
                k_after, k_back = ks_ref[i + 1, first + m], ks_ref[back + 1, first + m]
                s_own = x[0]
                for t in range(1, STRETCH - 1):
                    s_own = s_own * w[m] + x[t]
                s_own = s_own * w[m]
                k_own = g[STRETCH - 1]
                for t in range(STRETCH - 2, 0, -1):
                    k_own = k_own * w[m] + g[t]
                k_own = k_own * w[m]
                out.append(
                    (
                        same + h * k,
                        next_ + h * k_after,
                        b_k + h_back * k_own,
                        b_s + k_after * s_own,
                        fade[m] * (sd + width * h) + s_own,
                        fade[m] * (kd + width * k_back) + k_own,
                    )
                )
            return tuple(out)

        sums = lax.fori_loop(0, stretches, step, ((zero,) * 6,) * part, unroll=unroll)
        for m in range(part):
            same, next_, b_k, b_s, sd, kd = sums[m]
            r, d = lag_ref[STRETCH - 1], (width - 1.0) * lag_ref[STRETCH - 1]
            for j in range(STRETCH - 2, -1, -1):
                r = r * w[m] + lag_ref[j]
                d = d * w[m] + float(j) * lag_ref[j]
            at = pl.ds(first + m, members, stride=modes)
            sums_ref[0, at, :] = r + w[m] * (same - fade[m] * next_)
            sums_ref[1, at, :] = d + w[m] * (b_k + b_s + same + (width - 1.0) * (fade[m] * next_))
            sums_ref[2, at, :] = sd
            sums_ref[3, at, :] = kd

    me = me_ref[0]
    for member in range(members):
        at = pl.ds(member * modes, modes)
        put_states(message_ref, me, SETS, member, sk_ref[0, at, :], sk_ref[1, at, :], modes, members, last)
    if tree:
        side = (me // SETS) % 2
        offset = members * modes * (1 if last else 2)
        for to in range(members // 2):
            for i in range(4):
                index = pl.ds(pl.multiple_of((to * 2 + side) * modes, modes), modes)
                kept[0][i, pl.ds(to * modes, modes), :] = sums_ref[i, index, :]
                index = pl.ds(pl.multiple_of((to * 2 + 1 - side) * modes, modes), modes)
                message_ref[pl.ds(offset + (i * (members // 2) + to) * modes, modes), :] = sums_ref[i, index, :].astype(BF16)


def join(rate, left, right, length):
    r_a, d_a, sd_a, kd_a, s_a, k_a = left
    r_b, d_b, sd_b, kd_b, s_b, k_b = right
    w = jnp.exp(-rate)
    fade = jnp.exp(rate * -length)
    r = r_a + r_b + w * (s_a * k_b)
    d = d_a + d_b + w * (s_a * kd_b + (sd_a + s_a) * k_b)
    sd = fade * (sd_a + length * s_a) + sd_b
    kd = kd_a + fade * (kd_b + length * k_b)
    return r, d, sd, kd


def level_kernel(
    me_ref, tot_ref, got_ref, enter_ref, par_ref, *refs, tokens, modes, members, span, last, tree
):
    if tree:
        kept_ref, out_ref, new_ref, message_ref, keep_ref = refs
    else:
        out_ref, new_ref, message_ref = refs
    me = me_ref[0]
    second = (me // span) % 2
    earlier, later = flags(second == 1)
    inside = (me // 2) % (span // 2) * 2
    gap = earlier * inside.astype(F32) + later * (span - 2 - inside).astype(F32)
    rows = members * modes
    for member in range(members):
        at = pl.ds(member * modes, modes)
        rate = rate_block(par_ref, member, modes)
        far = jnp.exp(rate * -float(tokens * span))
        weight = jnp.exp(rate * (gap * -float(tokens)))
        s, k = tot_ref[0, at, :], tot_ref[1, at, :]
        gs, gk = got_ref[at, :].astype(F32), got_ref[pl.ds(rows + member * modes, modes), :].astype(F32)
        s_sum = earlier * (far * gs + s) + later * (far * s + gs)
        k_sum = earlier * (gk + far * k) + later * (k + far * gk)
        out_ref[0, at, :] = s_sum
        out_ref[1, at, :] = k_sum
        before = earlier * (weight * gs)
        after = later * (weight * gk)
        if span > 2:
            before += enter_ref[0, at, :]
            after += enter_ref[1, at, :]
        new_ref[0, at, :] = before
        new_ref[1, at, :] = after
        put_states(message_ref, me, span * 2, member, s_sum, k_sum, modes, members, last)
    if not tree:
        return
    side = (me // (span * 2)) % 2
    own = (me // 2) % span
    count = members // span
    offset = rows * (1 if last else 2)
    for parity in (0, 1):
        for to in range(count // 2):
            index = to * 2 + (side if parity == 0 else 1 - side)
            member = index * span + own
            src = pl.ds(pl.multiple_of(index * modes, modes), modes)
            at = pl.ds(pl.multiple_of(member * modes, modes), modes)
            at_k = pl.ds(pl.multiple_of((members + member) * modes, modes), modes)
            mine = tuple(kept_ref[i, src, :] for i in range(4)) + (tot_ref[0, at, :], tot_ref[1, at, :])
            theirs = tuple(
                got_ref[pl.ds(pl.multiple_of(rows * 2 + (i * count + index) * modes, modes), modes), :].astype(F32) for i in range(4)
            ) + (got_ref[at, :].astype(F32), got_ref[at_k, :].astype(F32))
            left = tuple(earlier * b + later * a for a, b in zip(mine, theirs))
            right = tuple(earlier * a + later * b for a, b in zip(mine, theirs))
            for i, value in enumerate(join(rate_block(par_ref, member, modes), left, right, float(tokens * span))):
                if parity == 0:
                    keep_ref[i, pl.ds(to * modes, modes), :] = value
                else:
                    message_ref[pl.ds(offset + (i * (count // 2) + to) * modes, modes), :] = value.astype(BF16)


def enter_kernel(me_ref, enter_ref, far_ref, par_ref, in_ref, *, tokens, modes, members, span):
    me = me_ref[0]
    earlier, later = flags((me // span) % 2 == 1)
    inside = (me // 2) % (span // 2) * 2
    gap = earlier * inside.astype(F32) + later * (span - 2 - inside).astype(F32)
    for member in range(members):
        at = pl.ds(member * modes, modes)
        value = jnp.exp(rate_block(par_ref, member, modes) * (gap * -float(tokens))) * far_ref[at, :].astype(F32)
        before, after = earlier * value, later * value
        if span > 2:
            before += enter_ref[0, at, :]
            after += enter_ref[1, at, :]
        in_ref[0, at, :] = before
        in_ref[1, at, :] = after


def finish_kernel(me_ref, y_ref, z_ref, hs_ref, ks_ref, par_ref, in_ref, *refs, tokens, modes, members, own):
    if own:
        k_ref, v_ref, u_ref, dq_ref, dk_ref, dv_ref, yo_ref, zo_ref = refs
    else:
        send_ref, yo_ref, zo_ref = refs
    core = me_ref[0] % SETS
    chunk = core if own else 1 - core
    second, first = flags(chunk == 1)
    stretches = tokens // STRETCH
    base = chunk * stretches
    rate = [param_rows(par_ref, 0, m, modes, members) for m in range(modes)]
    w = [jnp.exp(-rate[m]) for m in range(modes)]
    fade = [jnp.exp(rate[m] * -float(STRETCH)) for m in range(modes)]
    amp = [param_rows(par_ref, 1, m, modes, members) * jnp.sqrt(rate[m]) * w[m] for m in range(modes)]
    h = tuple(
        in_ref[0, pl.ds(m, members, stride=modes), :] * jnp.exp(rate[m] * (second * -float(tokens))) for m in range(modes)
    )
    k = tuple(
        in_ref[1, pl.ds(m, members, stride=modes), :] * jnp.exp(rate[m] * (first * -float(tokens))) for m in range(modes)
    )

    def forward(i, h):
        p = [amp[m] * (h[m] + hs_ref[base + i, m]) for m in range(modes)]
        for t in range(STRETCH):
            at = pl.ds((i * STRETCH + t) * members, members)
            yo_ref[at, :] = y_ref[pl.ds(((base + i) * STRETCH + t) * members, members), :] + total(p)
            if t < STRETCH - 1:
                p = [w[m] * p[m] for m in range(modes)]
        return tuple(fade[m] * h[m] for m in range(modes))

    def backward(i, k):
        back = stretches - 1 - i
        q = [amp[m] * (k[m] + ks_ref[base + back + 1, m]) for m in range(modes)]
        for t in range(STRETCH):
            row = back * STRETCH + STRETCH - 1 - t
            zo_ref[pl.ds(row * members, members), :] = z_ref[pl.ds((base * STRETCH + row) * members, members), :] + total(q)
            if t < STRETCH - 1:
                q = [w[m] * q[m] for m in range(modes)]
        return tuple(fade[m] * k[m] for m in range(modes))

    def put(source, store):
        for tile in range(tokens // 16):
            rows = pl.ds(tile * 16, 16)
            for member in range(members):
                halves = [pl.ds((tile * 16 + half * 8) * members + member, 8, stride=members) for half in range(2)]
                store(rows, member, jnp.concatenate([source[at, :] for at in halves], axis=0).astype(BF16))

    def store_y(rows, member, value):
        if own:
            cols = set_columns(member, core)
            dq_ref[rows, cols] = (u_ref[rows, cols].astype(F32) * value.astype(F32)).astype(BF16)
        else:
            send_ref[0, member, rows, :] = value

    def store_z(rows, member, value):
        if own:
            cols = set_columns(member, core)
            value = value.astype(F32)
            dk_ref[rows, cols] = (value * v_ref[rows, cols].astype(F32)).astype(BF16)
            dv_ref[rows, cols] = (value * k_ref[rows, cols].astype(F32)).astype(BF16)
        else:
            send_ref[1, member, rows, :] = value

    lax.fori_loop(0, stretches, forward, h)
    put(yo_ref, store_y)
    lax.fori_loop(0, stretches, backward, k)
    put(zo_ref, store_z)


def last_kernel(me_ref, got_ref, k_ref, v_ref, u_ref, *refs, tokens, modes, members, span, scale, tree):
    refs = list(refs)
    if tree:
        kept_ref, far_ref, tot_ref, own_ref = refs[:4]
        refs = refs[4:]
    dq_ref, dk_ref, dv_ref, dq_hbm, dk_hbm, dv_hbm = refs[3:9]
    me = me_ref[0]
    core = me % SETS
    copies = []
    if tree:
        r_hbm, log_hbm, sems, par_sems, out_ref = refs[9:]
        earlier, later = flags((me // span) % 2 == 1)
        at = pl.ds(pl.multiple_of(me // 2 * modes, modes), modes)
        rows = members * modes
        r_m, d_m, sd_m, kd_m = (kept_ref[i] for i in range(4))
        r_t, d_t, sd_t, kd_t = (far_ref[pl.ds(rows + i * modes, modes), :].astype(F32) for i in range(4))
        far = far_ref[at, :].astype(F32)
        s_a = earlier * far + later * tot_ref[0, at, :]
        k_b = earlier * tot_ref[1, at, :] + later * far
        sd_a = earlier * sd_t + later * sd_m
        kd_b = earlier * kd_m + later * kd_t
        rate, residue = own_ref[0], own_ref[1]
        w = jnp.exp(-rate)
        r = r_m + r_t + w * (s_a * k_b)
        d = d_m + d_t + w * (s_a * kd_b + (sd_a + s_a) * k_b)
        root = jnp.sqrt(rate) * scale
        out_ref[0] = root * r
        out_ref[1] = root * residue * (0.5 * r - rate * d)
        for i, ref in enumerate((r_hbm, log_hbm)):
            copies.append(pltpu.make_async_copy(out_ref.at[i], ref, par_sems.at[i]))
            copies[-1].start()
    else:
        (sems,) = refs[9:]
    for tile in range(tokens // 16):
        rows = pl.ds(tile * 16, 16)
        for member in range(members):
            cols = set_columns(member, 1 - core)
            y = got_ref[0, member, rows, :].astype(F32)
            z = got_ref[1, member, rows, :].astype(F32)
            dq_ref[rows, cols] = (u_ref[rows, cols].astype(F32) * y).astype(BF16)
            dk_ref[rows, cols] = (z * v_ref[rows, cols].astype(F32)).astype(BF16)
            dv_ref[rows, cols] = (z * k_ref[rows, cols].astype(F32)).astype(BF16)
        for i, (ref, out) in enumerate(((dq_ref, dq_hbm), (dk_ref, dk_hbm), (dv_ref, dv_hbm))):
            copies.append(pltpu.make_async_copy(ref.at[rows], out.at[rows], sems.at[i, tile]))
            copies[-1].start()
    for copy in copies:
        copy.wait()


def call(body, out_shape, in_specs, flops, out_specs=None, scratch=(), aliases=None):
    return pl.pallas_call(
        body,
        out_shape=out_shape,
        in_specs=in_specs,
        out_specs=jax.tree.map(lambda _: VMEM, out_shape) if out_specs is None else out_specs,
        scratch_shapes=scratch,
        input_output_aliases=aliases or {},
        compiler_params=pltpu.CompilerParams(vmem_limit_bytes=16 * 1024 * 1024),
        cost_estimate=pl.CostEstimate(flops=flops, bytes_accessed=1024 * 1024, transcendentals=0),
    )


def exchange(value, distance, count):
    return lax.ppermute(value, "ctx", [(i, i ^ distance) for i in range(count)])


def tie(*values):
    return lax.optimization_barrier(values)


def local(query_proj, key_proj, value_proj, output_grad, residue, decay_rate):
    tokens, channels = query_proj.shape
    own_channels, modes = residue.shape
    count = lax.axis_size("ctx")
    groups = channels // LANES
    members = groups // SETS
    rows = members * modes
    length = tokens * SETS
    top = count // 2
    tree = groups == count and own_channels == LANES and top > SETS
    work = tokens * channels * modes
    index = lax.axis_index("ctx")
    core = index % SETS
    me = index.astype(jnp.int32).reshape(1)

    def shape(*dims, dtype=F32):
        return jax.ShapeDtypeStruct(dims, dtype)

    half = shape(2, members, tokens, LANES, dtype=BF16)
    series = shape(length * members, LANES)
    pieces = 4
    own_gates, send_gates = call(
        functools.partial(gate_kernel, members=members, pieces=pieces),
        (half, half),
        [SMEM] + [HBM] * 4,
        work,
        scratch=(pltpu.VMEM((4, tokens, channels), BF16), pltpu.SemaphoreType.DMA((pieces, 4))),
    )(me, *(pltpu.with_memory_space_constraint(a, pltpu.HBM) for a in (query_proj, key_proj, value_proj, output_grad)))

    (own,) = tie(jnp.stack([decay_rate.T, residue.T]))
    params, axis = own, 0
    distance = count // 2
    while distance > (1 if tree else 0):
        other = exchange(params, distance, count)
        if axis == 0:
            other, own_gates, send_gates = tie(other, own_gates, send_gates)
            got_gates = exchange(send_gates, 1, count)
            gated, gate_grad, lags = call(
                functools.partial(series_kernel, tokens=tokens, members=members),
                (series, series, shape(STRETCH, members, LANES)),
                [SMEM] + [VMEM] * 2,
                work,
            )(me, own_gates, got_gates)
        if axis == 2:
            other, gated, gate_grad, lags = tie(other, gated, gate_grad, lags)
        upper = (index // distance) % 2 == 1
        params = jnp.stack([jnp.where(upper, other, params), jnp.where(upper, params, other)], axis=axis)
        distance //= 2
        axis += 1
    if tree:
        params = params.reshape((members,) + own.shape)
    else:
        params = params.reshape((count,) + own.shape).transpose(1, 2, 0, 3).reshape(2, modes, members, SETS, LANES)
        params = lax.dynamic_index_in_dim(params, core, 3, keepdims=False).transpose(2, 0, 1, 3)
    par = params.reshape(members * 2 * modes, LANES)

    stretches = length // STRETCH
    pair = shape(2, rows, LANES)
    sk, hs, ks, x_weighted, g_weighted = call(
        functools.partial(state_kernel, length=length, modes=modes, members=members),
        (pair, shape(stretches, modes, members, LANES), shape(stretches + 1, modes, members, LANES), series, series),
        [VMEM] * 3,
        work * 4,
    )(gated, gate_grad, par)

    def message_shape(span):
        return shape(rows * (1 if span == top else 2) + (4 * rows // span if tree else 0), LANES, dtype=BF16)

    sums, message, *kept = call(
        functools.partial(
            sums_kernel, length=length, modes=modes, members=members, part=min(4, modes), unroll=4, last=top == SETS, tree=tree
        ),
        (shape(4, rows, LANES), message_shape(SETS)) + ((shape(4, rows // 2, LANES),) if tree else ()),
        [SMEM] + [VMEM] * 7,
        work * 6,
    )(me, x_weighted, g_weighted, lags, hs, ks, sk, par)

    tot, enter, span = sk, sk, SETS
    while span < top:
        got = exchange(message, span, count)
        last = span * 2 == top
        tot, enter, message, *kept = call(
            functools.partial(level_kernel, tokens=tokens, modes=modes, members=members, span=span, last=last, tree=tree),
            (pair, pair, message_shape(span * 2)) + ((shape(4, rows // span // 2, LANES),) if tree else ()),
            [SMEM] + [VMEM] * (5 if tree else 4),
            rows,
        )(me, tot, got, enter, par, *kept)
        if span == SETS:
            tot, gated, gate_grad = tie(tot, gated, gate_grad)
        span *= 2
    far = exchange(message, top, count)
    y, z = call(
        functools.partial(taps_kernel, length=length, modes=modes, members=members), (series, series), [VMEM] * 3, work
    )(gated, gate_grad, par)
    (states_in,) = call(
        functools.partial(enter_kernel, tokens=tokens, modes=modes, members=members, span=top), (pair,), [SMEM] + [VMEM] * 3, rows
    )(me, enter, far, par)

    scratch = (pltpu.VMEM((tokens * members, LANES), F32),) * 2
    finish = functools.partial(finish_kernel, tokens=tokens, modes=modes, members=members)
    (send_conv,) = call(functools.partial(finish, own=False), (half,), [SMEM] + [VMEM] * 6, work * 2, scratch=scratch)(
        me, y, z, hs, ks, par, states_in
    )
    got_conv = exchange(send_conv, 1, count)
    grads = (shape(tokens, channels, dtype=BF16),) * 3
    done = call(functools.partial(finish, own=True), grads, [SMEM] + [VMEM] * 9, work * 2, scratch=scratch)(
        me, y, z, hs, ks, par, states_in, key_proj, value_proj, output_grad
    )
    scale = float(tokens * count) ** (-0.5)
    extra = (*kept, far, tot, own) if tree else ()
    first = 5 + len(extra)
    out = call(
        functools.partial(last_kernel, tokens=tokens, modes=modes, members=members, span=top, scale=scale, tree=tree),
        grads + grads + ((shape(modes, LANES),) * 2 if tree else ()),
        [SMEM] + [VMEM] * (first + 2),
        work,
        (VMEM,) * 3 + (ANY,) * (5 if tree else 3),
        (pltpu.SemaphoreType.DMA((3, tokens // 16)),)
        + ((pltpu.SemaphoreType.DMA((2,)), pltpu.VMEM((2, modes, LANES), F32)) if tree else ()),
        {first: 0, first + 1: 1, first + 2: 2},
    )(me, got_conv, key_proj, value_proj, output_grad, *extra, *done)

    if tree:
        residue_grad, log_grad = out[6].T, out[7].T
    else:
        dims = (members, modes, LANES)
        h_in, k_in = (a.reshape(dims) for a in states_in)
        s, k = (a.reshape(dims) for a in sk)
        r, d, s_d, k_d = (a.reshape(dims) for a in sums)
        rate = params[:, 0]
        w = jnp.exp(-rate)
        r = r + w * h_in * k
        d = d + w * (h_in * k_d + k_in * (s_d + s)) + float(length) * jnp.exp(-rate * float(length + 1)) * h_in * k_in
        parts = jnp.stack([r, d], axis=1)
        parts = jnp.stack([jnp.where(core == 0, parts, 0.0), jnp.where(core == 1, parts, 0.0)], axis=1)
        parts = parts.reshape(groups, 2, modes, LANES).transpose(1, 2, 0, 3)
        parts = parts.reshape(2, modes, count, own_channels).transpose(2, 0, 1, 3)
        sums = lax.all_to_all(parts, "ctx", split_axis=0, concat_axis=0, tiled=True).sum(axis=0)
        root = scale * jnp.sqrt(decay_rate)
        residue_grad = root * sums[0].T
        log_grad = root * residue * (0.5 * sums[0].T - decay_rate * sums[1].T)
    return out[3], out[4], out[5], residue_grad, log_grad


def solution(mesh):
    in_specs = (P("ctx", "ch"),) * 4 + (P(("ch", "ctx"), None),) * 2
    out_specs = (P("ctx", "ch"),) * 3 + (P(("ch", "ctx"), None),) * 2
    return jax.shard_map(local, mesh=mesh, in_specs=in_specs, out_specs=out_specs, check_vma=False)
```

```python
import functools

import jax
import jax.numpy as jnp
from jax import lax
from jax.experimental import pallas as pl
from jax.experimental.pallas import tpu as pltpu
from jax.sharding import PartitionSpec as P

LANES = 128
SETS = 2
STRETCH = 8
F32 = jnp.float32
BF16 = jnp.bfloat16
VMEM = pl.BlockSpec(memory_space=pltpu.VMEM)
SMEM = pl.BlockSpec(memory_space=pltpu.SMEM)
ANY = pl.BlockSpec(memory_space=pl.ANY)
HBM = pl.BlockSpec(memory_space=pltpu.HBM)


def total(terms):
    terms = list(terms)
    while len(terms) > 1:
        terms = [a + b for a, b in zip(terms[::2], terms[1::2])] + terms[len(terms) & ~1 :]
    return terms[0]


def set_columns(member, which):
    return pl.ds(pl.multiple_of((member * SETS + which) * LANES, LANES), LANES)


def gate_kernel(me_ref, q_hbm, k_hbm, v_hbm, u_hbm, own_ref, send_ref, stage_ref, sems, *, members, pieces):
    tokens = q_hbm.shape[0]
    core = me_ref[0] % SETS
    rows = tokens // pieces
    copies = []
    for piece in range(pieces):
        at = pl.ds(piece * rows, rows)
        for i, ref in enumerate((q_hbm, k_hbm, v_hbm, u_hbm)):
            copies.append(pltpu.make_async_copy(ref.at[at], stage_ref.at[i, at], sems.at[piece, i]))
            copies[-1].start()

    def body(tile, _):
        at = pl.ds(pl.multiple_of(tile * 16, 16), 16)
        for out_ref, which in ((own_ref, core), (send_ref, 1 - core)):
            for member in range(members):
                cols = set_columns(member, which)
                q, k, v, u = (stage_ref[i, at, cols].astype(F32) for i in range(4))
                out_ref[0, member, at, :] = (k * v).astype(BF16)
                out_ref[1, member, at, :] = (u * q).astype(BF16)
        return 0

    for piece in range(pieces):
        for copy in copies[piece * 4 : piece * 4 + 4]:
            copy.wait()
        lax.fori_loop(piece * rows // 16, (piece + 1) * rows // 16, body, 0)


def series_kernel(me_ref, own_ref, got_ref, x_ref, g_ref, lag_ref, *, tokens, members):
    core = me_ref[0] % SETS
    half = members // 2
    for ref, chunk in ((own_ref, core), (got_ref, 1 - core)):

        def body(tile, _):
            rows = pl.ds(pl.multiple_of(tile * 16, 16), 16)
            for member in range(members):
                for i, out_ref in enumerate((x_ref, g_ref)):
                    value = ref[i, member, rows, :].astype(F32)
                    for part in range(2):
                        start = (tile * 16 + part * 8) * members + chunk * half + member // 2
                        out_ref[member % 2, pl.ds(start, 8, stride=members), :] = value[part * 8 : part * 8 + 8]
            return 0

        lax.fori_loop(0, tokens // 16, body, 0)

    for side in range(2):

        def step(i, lags):
            x = [x_ref[side, pl.ds((i * STRETCH + t) * members, members), :] for t in range(STRETCH)]
            g = [g_ref[side, pl.ds((i * STRETCH + t) * members, members), :] for t in range(STRETCH)]
            return tuple(lags[j] + total([g[t] * x[t - j] for t in range(j, STRETCH)]) for j in range(STRETCH))

        zero = tuple(jnp.zeros((members, LANES), F32) for _ in range(STRETCH))
        lags = lax.fori_loop(0, tokens // STRETCH, step, zero)
        for j in range(STRETCH):
            lag_ref[side, j] = lags[j]


def param_rows(par_ref, param, mode, modes, members):
    return par_ref[pl.ds(param * modes + mode, members, stride=2 * modes), :]


def rate_block(par_ref, member, modes):
    return par_ref[pl.ds(pl.multiple_of(member * 2 * modes, modes), modes), :]


def half_rows(par_ref, start, stride, members):
    rows = par_ref[pl.ds(start, members // 2, stride=stride), :]
    return jnp.concatenate([rows, rows], axis=0)


def chosen_half(me_ref, flip):
    side = (me_ref[0] // SETS) % 2
    return 1 - side if flip else side


def state_kernel(me_ref, x_ref, g_ref, par_ref, sk_ref, hs_ref, ks_ref, xw_ref, gw_ref, *, tokens, modes, members, flip):
    side = chosen_half(me_ref, flip)
    half = members // 2
    w = [jnp.exp(-half_rows(par_ref, m, 2 * modes, members)) for m in range(modes)]
    stretches = tokens // STRETCH

    def step(i, carry):
        s, k = carry
        back = stretches - 1 - i
        for m in range(modes):
            hs_ref[i, m] = s[m]
        for t in range(STRETCH):
            at = pl.ds((i * STRETCH + t) * members, members)
            at_back = pl.ds((back * STRETCH + STRETCH - 1 - t) * members, members)
            x, g = x_ref[side, at, :], g_ref[side, at_back, :]
            xw_ref[at, :] = x * float(STRETCH - 1 - t)
            gw_ref[at_back, :] = g * float(STRETCH - 1 - t)
            s = tuple(w[m] * s[m] + x for m in range(modes))
            k = tuple(w[m] * k[m] + g for m in range(modes))
        for m in range(modes):
            ks_ref[back, m] = k[m]
        return s, k

    zero = tuple(jnp.zeros((members, LANES), F32) for _ in range(modes))
    for m in range(modes):
        ks_ref[stretches, m] = zero[m]
    s, k = lax.fori_loop(0, stretches, step, (zero, zero), unroll=2)
    for m in range(modes):
        at = pl.ds(m, half, stride=modes)
        for i, value in enumerate((s[m], k[m])):
            sk_ref[i, 0, at, :] = value[:half]
            sk_ref[i, 1, at, :] = value[half:]


def taps_kernel(x_ref, g_ref, par_ref, y_ref, z_ref, *, tokens, modes, members):
    half = members // 2
    for side in range(2):
        rate = [half_rows(par_ref, side * 2 * modes + m, 4 * modes, members) for m in range(modes)]
        w = [jnp.exp(-rate[m]) for m in range(modes)]
        power = [half_rows(par_ref, (side * 2 + 1) * modes + m, 4 * modes, members) * jnp.sqrt(rate[m]) for m in range(modes)]
        taps = []
        for j in range(STRETCH):
            taps.append(total(power))
            power = [power[m] * w[m] for m in range(modes)]

        def within(i, _):
            at = [pl.ds((i * STRETCH + t) * members, members) for t in range(STRETCH)]
            x = [x_ref[side, at[t], :] for t in range(STRETCH)]
            g = [g_ref[side, at[t], :] for t in range(STRETCH)]
            for t in range(STRETCH):
                y = total([taps[j] * x[t - j] for j in range(t + 1)])
                z = total([taps[j] * g[t + j] for j in range(STRETCH - t)])
                for chunk in range(2):
                    to = pl.ds((chunk * tokens + i * STRETCH + t) * members + side, half, stride=2)
                    y_ref[to, :] = y[chunk * half : (chunk + 1) * half]
                    z_ref[to, :] = z[chunk * half : (chunk + 1) * half]
            return 0

        lax.fori_loop(0, tokens // STRETCH, within, 0, unroll=2)


def order_kernel(me_ref, hs_own, ks_own, hs_far, ks_far, hs_ref, ks_ref, *, tokens, modes, members):
    half = members // 2
    for src, out, count in ((0, hs_ref, tokens // STRETCH), (1, ks_ref, tokens // STRETCH + 1)):

        def body(i, _):
            for flip, ref in ((False, (hs_own, ks_own)[src]), (True, (hs_far, ks_far)[src])):
                side = chosen_half(me_ref, flip)
                for m in range(modes):
                    for chunk in range(2):
                        out[chunk, i, pl.ds(m * members + side, half, stride=2), :] = ref[i, m, chunk * half : (chunk + 1) * half, :]
            return 0

        lax.fori_loop(0, count, body, 0)


def flags(bit):
    bit = bit.astype(F32)
    return bit, 1.0 - bit


def put_states(ref, me, span, at, at_k, s, k, last):
    if last:
        earlier, later = flags((me // span) % 2 == 1)
        ref[at, :] = (earlier * k + later * s).astype(BF16)
    else:
        ref[at, :] = s.astype(BF16)
        ref[at_k, :] = k.astype(BF16)


def blocks(member, modes, members):
    if isinstance(member, int):
        return pl.ds(member * modes, modes), pl.ds((members + member) * modes, modes)
    return tuple(pl.ds(pl.multiple_of(m * modes, modes), modes) for m in (member, members + member))


def sums_kernel(me_ref, x_ref, g_ref, lag_ref, hs_ref, ks_ref, sk_ref, par_ref, *refs, tokens, modes, members, part, unroll, flip, last, tree):
    if flip:
        sk_own, par_own, sums_ref, tot_ref, message_ref, work_ref = refs
    else:
        sums_ref, work_ref = refs
    side = chosen_half(me_ref, flip)
    half = members // 2
    stretches = tokens // STRETCH
    width = float(STRETCH)
    zero = jnp.zeros((members, LANES), F32)
    for first in range(0, modes, part):
        rate = [half_rows(par_ref, first + m, 2 * modes, members) for m in range(part)]
        w = [jnp.exp(-rate[m]) for m in range(part)]
        fade = [jnp.exp(rate[m] * -width) for m in range(part)]

        def step(i, carry):
            back = stretches - 1 - i
            x = [x_ref[pl.ds((i * STRETCH + t) * members, members), :] for t in range(STRETCH - 1)]
            g = [g_ref[pl.ds((back * STRETCH + t) * members, members), :] for t in range(STRETCH)]
            out = []
            for m in range(part):
                same, next_, b_k, b_s, sd, kd = carry[m]
                h, k = hs_ref[i, first + m], ks_ref[i, first + m]
                h_back = hs_ref[back, first + m]
                k_after, k_back = ks_ref[i + 1, first + m], ks_ref[back + 1, first + m]
                s_own = x[0]
                for t in range(1, STRETCH - 1):
                    s_own = s_own * w[m] + x[t]
                s_own = s_own * w[m]
                k_own = g[STRETCH - 1]
                for t in range(STRETCH - 2, 0, -1):
                    k_own = k_own * w[m] + g[t]
                k_own = k_own * w[m]
                out.append(
                    (
                        same + h * k,
                        next_ + h * k_after,
                        b_k + h_back * k_own,
                        b_s + k_after * s_own,
                        fade[m] * (sd + width * h) + s_own,
                        fade[m] * (kd + width * k_back) + k_own,
                    )
                )
            return tuple(out)

        sums = lax.fori_loop(0, stretches, step, ((zero,) * 6,) * part, unroll=unroll)
        lags = [lag_ref[side, j] for j in range(STRETCH)]
        for m in range(part):
            same, next_, b_k, b_s, sd, kd = sums[m]
            r, d = lags[STRETCH - 1], (width - 1.0) * lags[STRETCH - 1]
            for j in range(STRETCH - 2, -1, -1):
                r = r * w[m] + lags[j]
                d = d * w[m] + float(j) * lags[j]
            r = r + w[m] * (same - fade[m] * next_)
            d = d + w[m] * (b_k + b_s + same + (width - 1.0) * (fade[m] * next_))
            at = pl.ds(first + m, half, stride=modes)
            for i, value in enumerate((r, d, sd, kd)):
                work_ref[i, 0, at, :] = value[:half]
                work_ref[i, 1, at, :] = value[half:]

    me = me_ref[0]
    rows = members * modes
    for z in range(half):
        at = pl.ds(z * modes, modes)
        left, right = (tuple(work_ref[i, c, at, :] for i in range(4)) + (sk_ref[0, c, at, :], sk_ref[1, c, at, :]) for c in range(2))
        rate = par_ref[pl.ds(z * 2 * modes, modes), :]
        for i, value in enumerate(join(rate, left, right, float(tokens))):
            sums_ref[i, at, :] = value
            if flip and tree:
                offset = rows * (1 if last else 2)
                message_ref[pl.ds(offset + (i * half + z) * modes, modes), :] = value.astype(BF16)
        if flip:
            for ref, member, par in ((sk_ref, z * 2 + side, par_ref), (sk_own, z * 2 + 1 - side, par_own)):
                fade = jnp.exp(par[pl.ds(z * 2 * modes, modes), :] * -float(tokens))
                s = fade * ref[0, 0, at, :] + ref[0, 1, at, :]
                k = ref[1, 0, at, :] + fade * ref[1, 1, at, :]
                to, to_k = blocks(member, modes, members)
                tot_ref[0, to, :] = s
                tot_ref[1, to, :] = k
                put_states(message_ref, me, SETS, to, to_k, s, k, last)


def join(rate, left, right, length):
    r_a, d_a, sd_a, kd_a, s_a, k_a = left
    r_b, d_b, sd_b, kd_b, s_b, k_b = right
    w = jnp.exp(-rate)
    fade = jnp.exp(rate * -length)
    r = r_a + r_b + w * (s_a * k_b)
    d = d_a + d_b + w * (s_a * kd_b + (sd_a + s_a) * k_b)
    sd = fade * (sd_a + length * s_a) + sd_b
    kd = kd_a + fade * (kd_b + length * k_b)
    return r, d, sd, kd


def level_kernel(
    me_ref, tot_ref, got_ref, enter_ref, par_ref, *refs, tokens, modes, members, span, last, tree
):
    if tree:
        kept_ref, out_ref, new_ref, message_ref, keep_ref = refs
    else:
        out_ref, new_ref, message_ref = refs
    me = me_ref[0]
    second = (me // span) % 2
    earlier, later = flags(second == 1)
    inside = (me // 2) % (span // 2) * 2
    gap = earlier * inside.astype(F32) + later * (span - 2 - inside).astype(F32)
    rows = members * modes
    for member in range(members):
        at = pl.ds(member * modes, modes)
        rate = rate_block(par_ref, member, modes)
        far = jnp.exp(rate * -float(tokens * span))
        weight = jnp.exp(rate * (gap * -float(tokens)))
        s, k = tot_ref[0, at, :], tot_ref[1, at, :]
        gs, gk = got_ref[at, :].astype(F32), got_ref[pl.ds(rows + member * modes, modes), :].astype(F32)
        s_sum = earlier * (far * gs + s) + later * (far * s + gs)
        k_sum = earlier * (gk + far * k) + later * (k + far * gk)
        out_ref[0, at, :] = s_sum
        out_ref[1, at, :] = k_sum
        before = earlier * (weight * gs)
        after = later * (weight * gk)
        if span > 2:
            before += enter_ref[0, at, :]
            after += enter_ref[1, at, :]
        new_ref[0, at, :] = before
        new_ref[1, at, :] = after
        put_states(message_ref, me, span * 2, *blocks(member, modes, members), s_sum, k_sum, last)
    if not tree:
        return
    side = (me // (span * 2)) % 2
    own = (me // 2) % span
    count = members // span
    offset = rows * (1 if last else 2)
    for parity in (0, 1):
        for to in range(count // 2):
            index = to * 2 + (side if parity == 0 else 1 - side)
            member = index * span + own
            src = pl.ds(pl.multiple_of(index * modes, modes), modes)
            at = pl.ds(pl.multiple_of(member * modes, modes), modes)
            at_k = pl.ds(pl.multiple_of((members + member) * modes, modes), modes)
            mine = tuple(kept_ref[i, src, :] for i in range(4)) + (tot_ref[0, at, :], tot_ref[1, at, :])
            theirs = tuple(
                got_ref[pl.ds(pl.multiple_of(rows * 2 + (i * count + index) * modes, modes), modes), :].astype(F32) for i in range(4)
            ) + (got_ref[at, :].astype(F32), got_ref[at_k, :].astype(F32))
            left = tuple(earlier * b + later * a for a, b in zip(mine, theirs))
            right = tuple(earlier * a + later * b for a, b in zip(mine, theirs))
            for i, value in enumerate(join(rate_block(par_ref, member, modes), left, right, float(tokens * span))):
                if parity == 0:
                    keep_ref[i, pl.ds(to * modes, modes), :] = value
                else:
                    message_ref[pl.ds(offset + (i * (count // 2) + to) * modes, modes), :] = value.astype(BF16)


def enter_kernel(me_ref, enter_ref, far_ref, par_ref, sk_own, sk_far, in_ref, *, tokens, modes, members, span):
    me = me_ref[0]
    earlier, later = flags((me // span) % 2 == 1)
    inside = (me // 2) % (span // 2) * 2
    gap = earlier * inside.astype(F32) + later * (span - 2 - inside).astype(F32)
    for ref, flip in ((sk_own, False), (sk_far, True)):
        side = chosen_half(me_ref, flip)
        for z in range(members // 2):
            src = pl.ds(z * modes, modes)
            at, _ = blocks(z * 2 + side, modes, members)
            rate = rate_block(par_ref, z * 2 + side, modes)
            value = jnp.exp(rate * (gap * -float(tokens))) * far_ref[at, :].astype(F32)
            fade = jnp.exp(rate * -float(tokens))
            before, after = earlier * value, later * value
            if span > 2:
                before += enter_ref[0, at, :]
                after += enter_ref[1, at, :]
            in_ref[0, 0, at, :] = before
            in_ref[0, 1, at, :] = ref[1, 1, src, :] + fade * after
            in_ref[1, 0, at, :] = ref[0, 0, src, :] + fade * before
            in_ref[1, 1, at, :] = after


def finish_kernel(me_ref, y_ref, z_ref, hs_ref, ks_ref, par_ref, in_ref, *refs, tokens, modes, members, own):
    if own:
        k_ref, v_ref, u_ref, dq_ref, dk_ref, dv_ref, yo_ref, zo_ref = refs
    else:
        send_ref, yo_ref, zo_ref = refs
    core = me_ref[0] % SETS
    chunk = core if own else 1 - core
    stretches = tokens // STRETCH
    base = chunk * stretches
    rate = [param_rows(par_ref, 0, m, modes, members) for m in range(modes)]
    w = [jnp.exp(-rate[m]) for m in range(modes)]
    fade = [jnp.exp(rate[m] * -float(STRETCH)) for m in range(modes)]
    amp = [param_rows(par_ref, 1, m, modes, members) * jnp.sqrt(rate[m]) * w[m] for m in range(modes)]
    h = tuple(in_ref[chunk, 0, pl.ds(m, members, stride=modes), :] for m in range(modes))
    k = tuple(in_ref[chunk, 1, pl.ds(m, members, stride=modes), :] for m in range(modes))

    def forward(i, h):
        p = [amp[m] * (h[m] + hs_ref[chunk, i, pl.ds(m * members, members), :]) for m in range(modes)]
        for t in range(STRETCH):
            at = pl.ds((i * STRETCH + t) * members, members)
            yo_ref[at, :] = y_ref[pl.ds(((base + i) * STRETCH + t) * members, members), :] + total(p)
            if t < STRETCH - 1:
                p = [w[m] * p[m] for m in range(modes)]
        return tuple(fade[m] * h[m] for m in range(modes))

    def backward(i, k):
        back = stretches - 1 - i
        q = [amp[m] * (k[m] + ks_ref[chunk, back + 1, pl.ds(m * members, members), :]) for m in range(modes)]
        for t in range(STRETCH):
            row = back * STRETCH + STRETCH - 1 - t
            zo_ref[pl.ds(row * members, members), :] = z_ref[pl.ds((base * STRETCH + row) * members, members), :] + total(q)
            if t < STRETCH - 1:
                q = [w[m] * q[m] for m in range(modes)]
        return tuple(fade[m] * k[m] for m in range(modes))

    def put(source, store):
        for tile in range(tokens // 16):
            rows = pl.ds(tile * 16, 16)
            for member in range(members):
                halves = [pl.ds((tile * 16 + half * 8) * members + member, 8, stride=members) for half in range(2)]
                store(rows, member, jnp.concatenate([source[at, :] for at in halves], axis=0).astype(BF16))

    def store_y(rows, member, value):
        if own:
            cols = set_columns(member, core)
            dq_ref[rows, cols] = (u_ref[rows, cols].astype(F32) * value.astype(F32)).astype(BF16)
        else:
            send_ref[0, member, rows, :] = value

    def store_z(rows, member, value):
        if own:
            cols = set_columns(member, core)
            value = value.astype(F32)
            dk_ref[rows, cols] = (value * v_ref[rows, cols].astype(F32)).astype(BF16)
            dv_ref[rows, cols] = (value * k_ref[rows, cols].astype(F32)).astype(BF16)
        else:
            send_ref[1, member, rows, :] = value

    lax.fori_loop(0, stretches, forward, h)
    put(yo_ref, store_y)
    lax.fori_loop(0, stretches, backward, k)
    put(zo_ref, store_z)


def last_kernel(me_ref, got_ref, k_ref, v_ref, u_ref, *refs, tokens, modes, members, span, scale, tree):
    refs = list(refs)
    if tree:
        kept_ref, far_ref, tot_ref, own_ref = refs[:4]
        refs = refs[4:]
    dq_ref, dk_ref, dv_ref, dq_hbm, dk_hbm, dv_hbm = refs[3:9]
    me = me_ref[0]
    core = me % SETS
    copies = []
    if tree:
        r_hbm, log_hbm, sems, par_sems, out_ref = refs[9:]
        earlier, later = flags((me // span) % 2 == 1)
        at = pl.ds(pl.multiple_of(me // 2 * modes, modes), modes)
        rows = members * modes
        r_m, d_m, sd_m, kd_m = (kept_ref[i] for i in range(4))
        r_t, d_t, sd_t, kd_t = (far_ref[pl.ds(rows + i * modes, modes), :].astype(F32) for i in range(4))
        far = far_ref[at, :].astype(F32)
        s_a = earlier * far + later * tot_ref[0, at, :]
        k_b = earlier * tot_ref[1, at, :] + later * far
        sd_a = earlier * sd_t + later * sd_m
        kd_b = earlier * kd_m + later * kd_t
        rate, residue = own_ref[0], own_ref[1]
        w = jnp.exp(-rate)
        r = r_m + r_t + w * (s_a * k_b)
        d = d_m + d_t + w * (s_a * kd_b + (sd_a + s_a) * k_b)
        root = jnp.sqrt(rate) * scale
        out_ref[0] = root * r
        out_ref[1] = root * residue * (0.5 * r - rate * d)
        for i, ref in enumerate((r_hbm, log_hbm)):
            copies.append(pltpu.make_async_copy(out_ref.at[i], ref, par_sems.at[i]))
            copies[-1].start()
    else:
        (sems,) = refs[9:]
    for tile in range(tokens // 16):
        rows = pl.ds(tile * 16, 16)
        for member in range(members):
            cols = set_columns(member, 1 - core)
            y = got_ref[0, member, rows, :].astype(F32)
            z = got_ref[1, member, rows, :].astype(F32)
            dq_ref[rows, cols] = (u_ref[rows, cols].astype(F32) * y).astype(BF16)
            dk_ref[rows, cols] = (z * v_ref[rows, cols].astype(F32)).astype(BF16)
            dv_ref[rows, cols] = (z * k_ref[rows, cols].astype(F32)).astype(BF16)
        for i, (ref, out) in enumerate(((dq_ref, dq_hbm), (dk_ref, dk_hbm), (dv_ref, dv_hbm))):
            copies.append(pltpu.make_async_copy(ref.at[rows], out.at[rows], sems.at[i, tile]))
            copies[-1].start()
    for copy in copies:
        copy.wait()


def call(body, out_shape, in_specs, flops, out_specs=None, scratch=(), aliases=None):
    return pl.pallas_call(
        body,
        out_shape=out_shape,
        in_specs=in_specs,
        out_specs=jax.tree.map(lambda _: VMEM, out_shape) if out_specs is None else out_specs,
        scratch_shapes=scratch,
        input_output_aliases=aliases or {},
        compiler_params=pltpu.CompilerParams(vmem_limit_bytes=16 * 1024 * 1024),
        cost_estimate=pl.CostEstimate(flops=flops, bytes_accessed=1024 * 1024, transcendentals=0),
    )


def exchange(value, distance, count):
    return lax.ppermute(value, "ctx", [(i, i ^ distance) for i in range(count)])


def tie(*values):
    return lax.optimization_barrier(values)


def local(query_proj, key_proj, value_proj, output_grad, residue, decay_rate):
    tokens, channels = query_proj.shape
    own_channels, modes = residue.shape
    count = lax.axis_size("ctx")
    groups = channels // LANES
    members = groups // SETS
    rows = members * modes
    length = tokens * SETS
    top = count // 2
    tree = groups == count and own_channels == LANES and top > SETS
    work = tokens * channels * modes
    index = lax.axis_index("ctx")
    core = index % SETS
    side = (index // SETS) % 2
    me = index.astype(jnp.int32).reshape(1)

    def shape(*dims, dtype=F32):
        return jax.ShapeDtypeStruct(dims, dtype)

    half = shape(2, members, tokens, LANES, dtype=BF16)
    series = shape(length * members, LANES)
    half_series = shape(tokens * members, LANES)
    pieces = 4
    pair = shape(2, rows, LANES)
    stretches = tokens // STRETCH
    sizes = dict(tokens=tokens, modes=modes, members=members)

    def chip_states(flip, gated, gate_grad, par):
        states = shape(2, 2, rows // 2, LANES), shape(stretches, modes, members, LANES), shape(stretches + 1, modes, members, LANES)
        out = call(
            functools.partial(state_kernel, flip=flip, **sizes), states + (half_series,) * 2, [SMEM] + [VMEM] * 3, work * 2
        )(me, gated, gate_grad, par)
        return list(out)

    own_gates, send_gates = call(
        functools.partial(gate_kernel, members=members, pieces=pieces),
        (half, half),
        [SMEM] + [HBM] * 4,
        work,
        scratch=(pltpu.VMEM((4, tokens, channels), BF16), pltpu.SemaphoreType.DMA((pieces, 4))),
    )(me, *(pltpu.with_memory_space_constraint(a, pltpu.HBM) for a in (query_proj, key_proj, value_proj, output_grad)))

    (own,) = tie(jnp.stack([decay_rate.T, residue.T]))
    params, axis = own, 0
    distance = count // 2
    while distance > (1 if tree else 0):
        other = exchange(params, distance, count)
        if axis == 0:
            other, own_gates, send_gates = tie(other, own_gates, send_gates)
            got_gates = exchange(send_gates, 1, count)
            gated, gate_grad, lags = call(
                functools.partial(series_kernel, tokens=tokens, members=members),
                (shape(2, tokens * members, LANES),) * 2 + (shape(2, STRETCH, members, LANES),),
                [SMEM] + [VMEM] * 2,
                work,
            )(me, own_gates, got_gates)
        if axis == 1:
            other, gated, gate_grad, lags = tie(other, gated, gate_grad, lags)
        if tree and distance == SETS:
            par_own, par_far = (a.reshape(rows, LANES) for a in (params, other))
            states_own = chip_states(False, gated, gate_grad, par_own)
            par_far, states_own[0] = tie(par_far, states_own[0])
        upper = (index // distance) % 2 == 1
        params = jnp.stack([jnp.where(upper, other, params), jnp.where(upper, params, other)], axis=axis)
        distance //= 2
        axis += 1
    if tree:
        params = params.reshape((members,) + own.shape)
    else:
        params = params.reshape((count,) + own.shape).transpose(1, 2, 0, 3).reshape(2, modes, members, SETS, LANES)
        params = lax.dynamic_index_in_dim(params, core, 3, keepdims=False).transpose(2, 0, 1, 3)
        halves = params.reshape(members // 2, 2, 2, modes, LANES)
        par_own, par_far = (
            lax.dynamic_index_in_dim(halves, s, 1, keepdims=False).reshape(rows, LANES) for s in (side, 1 - side)
        )
        states_own = chip_states(False, gated, gate_grad, par_own)
    par = params.reshape(members * 2 * modes, LANES)

    sk_far, hs_far, ks_far, *weighted_far = chip_states(True, gated, gate_grad, par_far)
    sk_own, hs_own, ks_own, *weighted_own = states_own

    def message_shape(span):
        return shape(rows * (1 if span == top else 2) + (4 * rows // span if tree else 0), LANES, dtype=BF16)

    def chip_sums(flip, outs, weighted, hs, ks, sk, *par):
        return call(
            functools.partial(sums_kernel, part=min(4, modes), unroll=4, flip=flip, last=top == SETS, tree=tree, **sizes),
            (shape(4, rows // 2, LANES),) + outs,
            [SMEM] + [VMEM] * (6 + len(par)),
            work * 3,
            scratch=(pltpu.VMEM((4, 2, rows // 2, LANES), F32),),
        )(me, *weighted, lags, hs, ks, sk, *par)

    sums_far, tot, message = chip_sums(
        True, (pair, message_shape(SETS)), weighted_far, hs_far, ks_far, sk_far, par_far, sk_own, par_own
    )
    tot, weighted_own[0] = tie(tot, weighted_own[0])
    (sums_own,) = chip_sums(False, (), weighted_own, hs_own, ks_own, sk_own, par_own)

    enter, span, pair_tot, kept = tot, SETS, tot, [sums_own] if tree else []
    while span < top:
        got = exchange(message, span, count)
        last = span * 2 == top
        tot, enter, message, *kept = call(
            functools.partial(level_kernel, tokens=tokens, modes=modes, members=members, span=span, last=last, tree=tree),
            (pair, pair, message_shape(span * 2)) + ((shape(4, rows // span // 2, LANES),) if tree else ()),
            [SMEM] + [VMEM] * (5 if tree else 4),
            rows,
        )(me, tot, got, enter, par, *kept)
        if span == SETS:
            tot, hs_own, gated, gate_grad = tie(tot, hs_own, gated, gate_grad)
        span *= 2
    far = exchange(message, top, count)
    hs, ks = call(
        functools.partial(order_kernel, **sizes),
        (shape(2, stretches, modes * members, LANES), shape(2, stretches + 1, modes * members, LANES)),
        [SMEM] + [VMEM] * 4,
        work,
    )(me, hs_own, ks_own, hs_far, ks_far)
    y, z = call(functools.partial(taps_kernel, **sizes), (series, series), [VMEM] * 3, work)(gated, gate_grad, par)
    far, y, hs = tie(far, y, hs)
    (states_in,) = call(
        functools.partial(enter_kernel, span=top, **sizes), (shape(2, 2, rows, LANES),), [SMEM] + [VMEM] * 5, rows
    )(me, enter, far, par, sk_own, sk_far)

    scratch = (pltpu.VMEM((tokens * members, LANES), F32),) * 2
    finish = functools.partial(finish_kernel, tokens=tokens, modes=modes, members=members)
    (send_conv,) = call(functools.partial(finish, own=False), (half,), [SMEM] + [VMEM] * 6, work * 2, scratch=scratch)(
        me, y, z, hs, ks, par, states_in
    )
    got_conv = exchange(send_conv, 1, count)
    grads = (shape(tokens, channels, dtype=BF16),) * 3
    done = call(functools.partial(finish, own=True), grads, [SMEM] + [VMEM] * 9, work * 2, scratch=scratch)(
        me, y, z, hs, ks, par, states_in, key_proj, value_proj, output_grad
    )
    scale = float(tokens * count) ** (-0.5)
    extra = (*kept, far, tot, own) if tree else ()
    first = 5 + len(extra)
    out = call(
        functools.partial(last_kernel, tokens=tokens, modes=modes, members=members, span=top, scale=scale, tree=tree),
        grads + grads + ((shape(modes, LANES),) * 2 if tree else ()),
        [SMEM] + [VMEM] * (first + 2),
        work,
        (VMEM,) * 3 + (ANY,) * (5 if tree else 3),
        (pltpu.SemaphoreType.DMA((3, tokens // 16)),)
        + ((pltpu.SemaphoreType.DMA((2,)), pltpu.VMEM((2, modes, LANES), F32)) if tree else ()),
        {first: 0, first + 1: 1, first + 2: 2},
    )(me, got_conv, key_proj, value_proj, output_grad, *extra, *done)

    if tree:
        residue_grad, log_grad = out[6].T, out[7].T
    else:
        dims = (members, modes, LANES)
        h_in, k_in = states_in[0, 0].reshape(dims), states_in[1, 1].reshape(dims)
        s, k = (a.reshape(dims) for a in pair_tot)
        own_half, far_half = (a.reshape(4, members // 2, modes, LANES) for a in (sums_own, sums_far))
        ordered = jnp.where(side == 0, jnp.stack([own_half, far_half], 2), jnp.stack([far_half, own_half], 2))
        r, d, s_d, k_d = ordered.reshape((4,) + dims)
        rate = params[:, 0]
        w = jnp.exp(-rate)
        r = r + w * h_in * k
        d = d + w * (h_in * k_d + k_in * (s_d + s)) + float(length) * jnp.exp(-rate * float(length + 1)) * h_in * k_in
        parts = jnp.stack([r, d], axis=1)
        parts = jnp.stack([jnp.where(core == 0, parts, 0.0), jnp.where(core == 1, parts, 0.0)], axis=1)
        parts = parts.reshape(groups, 2, modes, LANES).transpose(1, 2, 0, 3)
        parts = parts.reshape(2, modes, count, own_channels).transpose(2, 0, 1, 3)
        sums = lax.all_to_all(parts, "ctx", split_axis=0, concat_axis=0, tiled=True).sum(axis=0)
        root = scale * jnp.sqrt(decay_rate)
        residue_grad = root * sums[0].T
        log_grad = root * residue * (0.5 * sums[0].T - decay_rate * sums[1].T)
    return out[3], out[4], out[5], residue_grad, log_grad


def solution(mesh):
    in_specs = (P("ctx", "ch"),) * 4 + (P(("ch", "ctx"), None),) * 2
    out_specs = (P("ctx", "ch"),) * 3 + (P(("ch", "ctx"), None),) * 2
    return jax.shard_map(local, mesh=mesh, in_specs=in_specs, out_specs=out_specs, check_vma=False)
```

```python
import functools

import jax
import jax.numpy as jnp
from jax import lax
from jax.experimental import pallas as pl
from jax.experimental.pallas import tpu as pltpu
from jax.sharding import PartitionSpec as P

LANES = 128
SETS = 2
STRETCH = 8
WAYS = 4
HOPS = (3, 1, 2)
F32 = jnp.float32
BF16 = jnp.bfloat16
VMEM = pl.BlockSpec(memory_space=pltpu.VMEM)
SMEM = pl.BlockSpec(memory_space=pltpu.SMEM)
ANY = pl.BlockSpec(memory_space=pl.ANY)
HBM = pl.BlockSpec(memory_space=pltpu.HBM)


def total(terms):
    terms = list(terms)
    while len(terms) > 1:
        terms = [a + b for a, b in zip(terms[::2], terms[1::2])] + terms[len(terms) & ~1 :]
    return terms[0]


def set_columns(member, which):
    return pl.ds(pl.multiple_of((member * SETS + which) * LANES, LANES), LANES)


def gate_kernel(me_ref, q_hbm, k_hbm, v_hbm, u_hbm, own_ref, send_ref, stage_ref, sems, *, members, pieces):
    tokens = q_hbm.shape[0]
    core = me_ref[0] % SETS
    rows = tokens // pieces
    copies = []
    for piece in range(pieces):
        at = pl.ds(piece * rows, rows)
        for i, ref in enumerate((q_hbm, k_hbm, v_hbm, u_hbm)):
            copies.append(pltpu.make_async_copy(ref.at[at], stage_ref.at[i, at], sems.at[piece, i]))
            copies[-1].start()

    def body(tile, _):
        at = pl.ds(pl.multiple_of(tile * 16, 16), 16)
        for out_ref, which in ((own_ref, core), (send_ref, 1 - core)):
            for member in range(members):
                cols = set_columns(member, which)
                q, k, v, u = (stage_ref[i, at, cols].astype(F32) for i in range(4))
                out_ref[0, member, at, :] = (k * v).astype(BF16)
                out_ref[1, member, at, :] = (u * q).astype(BF16)
        return 0

    for piece in range(pieces):
        for copy in copies[piece * 4 : piece * 4 + 4]:
            copy.wait()
        lax.fori_loop(piece * rows // 16, (piece + 1) * rows // 16, body, 0)


def series_kernel(me_ref, own_ref, got_ref, x_ref, g_ref, lag_ref, *, tokens, members):
    core = me_ref[0] % SETS
    half = members // 2
    for ref, chunk in ((own_ref, core), (got_ref, 1 - core)):

        def body(tile, _):
            rows = pl.ds(pl.multiple_of(tile * 16, 16), 16)
            for member in range(members):
                for i, out_ref in enumerate((x_ref, g_ref)):
                    value = ref[i, member, rows, :].astype(F32)
                    for part in range(2):
                        start = (tile * 16 + part * 8) * members + chunk * half + member // 2
                        out_ref[member % 2, pl.ds(start, 8, stride=members), :] = value[part * 8 : part * 8 + 8]
            return 0

        lax.fori_loop(0, tokens // 16, body, 0)

    for side in range(2):

        def step(i, lags):
            x = [x_ref[side, pl.ds((i * STRETCH + t) * members, members), :] for t in range(STRETCH)]
            g = [g_ref[side, pl.ds((i * STRETCH + t) * members, members), :] for t in range(STRETCH)]
            return tuple(lags[j] + total([g[t] * x[t - j] for t in range(j, STRETCH)]) for j in range(STRETCH))

        zero = tuple(jnp.zeros((members, LANES), F32) for _ in range(STRETCH))
        lags = lax.fori_loop(0, tokens // STRETCH, step, zero)
        for j in range(STRETCH):
            lag_ref[side, j] = lags[j]


def param_rows(par_ref, param, mode, modes, members):
    return par_ref[pl.ds(param * modes + mode, members, stride=2 * modes), :]


def half_rows(par_ref, start, stride, members):
    rows = par_ref[pl.ds(start, members // 2, stride=stride), :]
    return jnp.concatenate([rows, rows], axis=0)


def chosen_half(me_ref, flip):
    side = (me_ref[0] // SETS) % 2
    return 1 - side if flip else side


def ranked(me_ref, rank, members):
    half = members // 2
    return rank % half * 2 + chosen_half(me_ref, rank >= half)


def state_kernel(me_ref, x_ref, g_ref, par_ref, sk_ref, hs_ref, ks_ref, xw_ref, gw_ref, *, tokens, modes, members, flip):
    side = chosen_half(me_ref, flip)
    half = members // 2
    w = [jnp.exp(-half_rows(par_ref, m, 2 * modes, members)) for m in range(modes)]
    stretches = tokens // STRETCH

    def step(i, carry):
        s, k = carry
        back = stretches - 1 - i
        for m in range(modes):
            hs_ref[i, m] = s[m]
        for t in range(STRETCH):
            at = pl.ds((i * STRETCH + t) * members, members)
            at_back = pl.ds((back * STRETCH + STRETCH - 1 - t) * members, members)
            x, g = x_ref[side, at, :], g_ref[side, at_back, :]
            xw_ref[at, :] = x * float(STRETCH - 1 - t)
            gw_ref[at_back, :] = g * float(STRETCH - 1 - t)
            s = tuple(w[m] * s[m] + x for m in range(modes))
            k = tuple(w[m] * k[m] + g for m in range(modes))
        for m in range(modes):
            ks_ref[back, m] = k[m]
        return s, k

    zero = tuple(jnp.zeros((members, LANES), F32) for _ in range(modes))
    for m in range(modes):
        ks_ref[stretches, m] = zero[m]
    s, k = lax.fori_loop(0, stretches, step, (zero, zero), unroll=2)
    for m in range(modes):
        at = pl.ds(m, half, stride=modes)
        for i, value in enumerate((s[m], k[m])):
            sk_ref[i, 0, at, :] = value[:half]
            sk_ref[i, 1, at, :] = value[half:]


def taps_kernel(me_ref, x_ref, g_ref, par_ref, y_ref, z_ref, *, tokens, modes, members):
    half = members // 2
    for flip in (0, 1):
        side = chosen_half(me_ref, flip)
        start = flip * half * 2 * modes
        rate = [half_rows(par_ref, start + m, 2 * modes, members) for m in range(modes)]
        w = [jnp.exp(-rate[m]) for m in range(modes)]
        power = [half_rows(par_ref, start + modes + m, 2 * modes, members) * jnp.sqrt(rate[m]) for m in range(modes)]
        taps = []
        for j in range(STRETCH):
            taps.append(total(power))
            power = [power[m] * w[m] for m in range(modes)]

        def within(i, _):
            at = [pl.ds((i * STRETCH + t) * members, members) for t in range(STRETCH)]
            x = [x_ref[side, at[t], :] for t in range(STRETCH)]
            g = [g_ref[side, at[t], :] for t in range(STRETCH)]
            for t in range(STRETCH):
                y = total([taps[j] * x[t - j] for j in range(t + 1)])
                z = total([taps[j] * g[t + j] for j in range(STRETCH - t)])
                for chunk in range(2):
                    to = pl.ds((chunk * tokens + i * STRETCH + t) * members + flip * half, half)
                    y_ref[to, :] = y[chunk * half : (chunk + 1) * half]
                    z_ref[to, :] = z[chunk * half : (chunk + 1) * half]
            return 0

        lax.fori_loop(0, tokens // STRETCH, within, 0, unroll=2)


def order_kernel(hs_own, ks_own, hs_far, ks_far, hs_ref, ks_ref, *, tokens, modes, members):
    half = members // 2
    for src, out, count in ((0, hs_ref, tokens // STRETCH), (1, ks_ref, tokens // STRETCH + 1)):

        def body(i, _):
            for flip, ref in ((0, (hs_own, ks_own)[src]), (1, (hs_far, ks_far)[src])):
                for m in range(modes):
                    for chunk in range(2):
                        out[chunk, i, pl.ds(m * members + flip * half, half), :] = ref[i, m, chunk * half : (chunk + 1) * half, :]
            return 0

        lax.fori_loop(0, count, body, 0)


def flags(bit):
    bit = bit.astype(F32)
    return bit, 1.0 - bit


def put_states(refs, me, span, at, at_k, s, k, last):
    if last:
        place = me // span
        for hop, ref in zip(HOPS, refs):
            earlier, later = flags((place ^ hop) < place)
            ref[at, :] = (earlier * k + later * s).astype(BF16)
    else:
        refs[0][at, :] = s.astype(BF16)
        refs[0][at_k, :] = k.astype(BF16)


def blocks(rank, modes, members):
    return pl.ds(rank * modes, modes), pl.ds((members + rank) * modes, modes)


def sums_kernel(me_ref, x_ref, g_ref, lag_ref, hs_ref, ks_ref, sk_ref, par_ref, *refs, tokens, modes, members, part, unroll, flip, tree):
    if flip:
        sk_own, par_own, *sums_ref, tot_ref, message_ref, work_ref = refs
    else:
        *sums_ref, work_ref = refs
    side = chosen_half(me_ref, flip)
    half = members // 2
    stretches = tokens // STRETCH
    width = float(STRETCH)
    zero = jnp.zeros((members, LANES), F32)
    for first in range(0, modes, part):
        rate = [half_rows(par_ref, first + m, 2 * modes, members) for m in range(part)]
        w = [jnp.exp(-rate[m]) for m in range(part)]
        fade = [jnp.exp(rate[m] * -width) for m in range(part)]

        def step(i, carry):
            back = stretches - 1 - i
            x = [x_ref[pl.ds((i * STRETCH + t) * members, members), :] for t in range(STRETCH - 1)]
            g = [g_ref[pl.ds((back * STRETCH + t) * members, members), :] for t in range(STRETCH)]
            out = []
            for m in range(part):
                same, next_, b_k, b_s, sd, kd = carry[m]
                h, k = hs_ref[i, first + m], ks_ref[i, first + m]
                h_back = hs_ref[back, first + m]
                k_after, k_back = ks_ref[i + 1, first + m], ks_ref[back + 1, first + m]
                s_own = x[0]
                for t in range(1, STRETCH - 1):
                    s_own = s_own * w[m] + x[t]
                s_own = s_own * w[m]
                k_own = g[STRETCH - 1]
                for t in range(STRETCH - 2, 0, -1):
                    k_own = k_own * w[m] + g[t]
                k_own = k_own * w[m]
                out.append(
                    (
                        same + h * k,
                        next_ + h * k_after,
                        b_k + h_back * k_own,
                        b_s + k_after * s_own,
                        fade[m] * (sd + width * h) + s_own,
                        fade[m] * (kd + width * k_back) + k_own,
                    )
                )
            return tuple(out)

        sums = lax.fori_loop(0, stretches, step, ((zero,) * 6,) * part, unroll=unroll)
        lags = [lag_ref[side, j] for j in range(STRETCH)]
        for m in range(part):
            same, next_, b_k, b_s, sd, kd = sums[m]
            r, d = lags[STRETCH - 1], (width - 1.0) * lags[STRETCH - 1]
            for j in range(STRETCH - 2, -1, -1):
                r = r * w[m] + lags[j]
                d = d * w[m] + float(j) * lags[j]
            r = r + w[m] * (same - fade[m] * next_)
            d = d + w[m] * (b_k + b_s + same + (width - 1.0) * (fade[m] * next_))
            at = pl.ds(first + m, half, stride=modes)
            for i, value in enumerate((r, d, sd, kd)):
                work_ref[i, 0, at, :] = value[:half]
                work_ref[i, 1, at, :] = value[half:]

    me = me_ref[0]
    rows = members * modes
    for z in range(half):
        at = pl.ds(z * modes, modes)
        left, right = (tuple(work_ref[i, c, at, :] for i in range(4)) + (sk_ref[0, c, at, :], sk_ref[1, c, at, :]) for c in range(2))
        rate = par_ref[pl.ds(z * 2 * modes, modes), :]
        for i, value in enumerate(join(rate, left, right, float(tokens))):
            for ref in sums_ref:
                ref[i, at, :] = value
            if flip and tree:
                message_ref[pl.ds(rows * 2 + (i * half + z) * modes, modes), :] = value.astype(BF16)
        if flip:
            for ref, rank, par in ((sk_ref, half + z, par_ref), (sk_own, z, par_own)):
                fade = jnp.exp(par[pl.ds(z * 2 * modes, modes), :] * -float(tokens))
                s = fade * ref[0, 0, at, :] + ref[0, 1, at, :]
                k = ref[1, 0, at, :] + fade * ref[1, 1, at, :]
                to, to_k = blocks(rank, modes, members)
                tot_ref[0, to, :] = s
                tot_ref[1, to, :] = k
                put_states([message_ref], me, SETS, to, to_k, s, k, False)


def join(rate, left, right, length):
    r_a, d_a, sd_a, kd_a, s_a, k_a = left
    r_b, d_b, sd_b, kd_b, s_b, k_b = right
    w = jnp.exp(-rate)
    fade = jnp.exp(rate * -length)
    r = r_a + r_b + w * (s_a * k_b)
    d = d_a + d_b + w * (s_a * kd_b + (sd_a + s_a) * k_b)
    sd = fade * (sd_a + length * s_a) + sd_b
    kd = kd_a + fade * (kd_b + length * k_b)
    return r, d, sd, kd


def level_kernel(
    me_ref, tot_ref, got_ref, enter_ref, par_ref, *refs, tokens, modes, members, span, last, tree
):
    refs = list(refs)
    if tree:
        kept_ref, work_ref, keep_ref = refs.pop(0), refs.pop(), refs.pop()
    out_ref = None if last else refs.pop(0)
    new_ref, *messages = refs
    me = me_ref[0]
    second = (me // span) % 2
    earlier, later = flags(second == 1)
    inside = (me // 2) % (span // 2) * 2
    gap = earlier * inside.astype(F32) + later * (span - 2 - inside).astype(F32)
    rows = members * modes
    half = members // 2

    def received(rank):
        at, at_k = blocks((rank + half) % members if span == 2 else rank, modes, members)
        return got_ref[at, :].astype(F32), got_ref[at_k, :].astype(F32)

    sums = []
    for rank in range(members):
        at, at_k = blocks(rank, modes, members)
        rate = par_ref[pl.ds(rank * 2 * modes, modes), :]
        far = jnp.exp(rate * -float(tokens * span))
        weight = jnp.exp(rate * (gap * -float(tokens)))
        s, k = tot_ref[0, at, :], tot_ref[1, at, :]
        gs, gk = received(rank)
        s_sum = earlier * (far * gs + s) + later * (far * s + gs)
        k_sum = earlier * (gk + far * k) + later * (k + far * gk)
        if not last:
            out_ref[0, at, :] = s_sum
            out_ref[1, at, :] = k_sum
        before = earlier * (weight * gs)
        after = later * (weight * gk)
        if span > 2:
            before += enter_ref[0, at, :]
            after += enter_ref[1, at, :]
        new_ref[0, at, :] = before
        new_ref[1, at, :] = after
        put_states(messages, me, span * 2, at, at_k, s_sum, k_sum, last)
        if tree and span == 2 and rank < half:
            block = pl.ds(rank * modes, modes)
            mine = tuple(kept_ref[i, block, :] for i in range(4)) + (s, k)
            theirs = tuple(got_ref[pl.ds(rows * 2 + (i * half + rank) * modes, modes), :].astype(F32) for i in range(4)) + (gs, gk)
            left = tuple(earlier * b + later * a for a, b in zip(mine, theirs))
            right = tuple(earlier * a + later * b for a, b in zip(mine, theirs))
            for i, value in enumerate(join(rate, left, right, float(tokens * span)) + (s_sum, k_sum)):
                work_ref[rank, i] = value
    if tree:
        place = me // (span * 2)
        keep_ref[...] = work_ref[place]
        for hop, ref in zip(HOPS, messages):
            for i in range(6):
                ref[pl.ds(rows + i * modes, modes), :] = work_ref[place ^ hop, i].astype(BF16)


def enter_kernel(me_ref, enter_ref, a_ref, b_ref, c_ref, par_ref, sk_own, sk_far, in_ref, *, tokens, modes, members, span):
    me = me_ref[0]
    place = me // span
    inside = (me // 2) % (span // 2) * 2
    partners = []
    for hop, ref in zip(HOPS, (a_ref, b_ref, c_ref)):
        partner = place ^ hop
        earlier, later = flags(partner < place)
        gap = earlier * (span * (place - partner - 1) + inside).astype(F32)
        gap += later * (span * (partner - place - 1) + (span - 2 - inside)).astype(F32)
        partners.append((ref, earlier, later, gap * -float(tokens)))
    for ref, flip in ((sk_own, 0), (sk_far, 1)):
        for z in range(members // 2):
            src = pl.ds(z * modes, modes)
            rank = flip * (members // 2) + z
            at, _ = blocks(rank, modes, members)
            rate = par_ref[pl.ds(rank * 2 * modes, modes), :]
            before, after = enter_ref[0, at, :], enter_ref[1, at, :]
            for got_ref, earlier, later, gap in partners:
                value = jnp.exp(rate * gap) * got_ref[at, :].astype(F32)
                before += earlier * value
                after += later * value
            fade = jnp.exp(rate * -float(tokens))
            in_ref[0, 0, at, :] = before
            in_ref[0, 1, at, :] = ref[1, 1, src, :] + fade * after
            in_ref[1, 0, at, :] = ref[0, 0, src, :] + fade * before
            in_ref[1, 1, at, :] = after


def finish_kernel(me_ref, y_ref, z_ref, hs_ref, ks_ref, par_ref, in_ref, *refs, tokens, modes, members, own):
    if own:
        k_ref, v_ref, u_ref, dq_ref, dk_ref, dv_ref, yo_ref, zo_ref = refs
    else:
        send_ref, yo_ref, zo_ref = refs
    core = me_ref[0] % SETS
    chunk = core if own else 1 - core
    stretches = tokens // STRETCH
    base = chunk * stretches
    rate = [param_rows(par_ref, 0, m, modes, members) for m in range(modes)]
    w = [jnp.exp(-rate[m]) for m in range(modes)]
    fade = [jnp.exp(rate[m] * -float(STRETCH)) for m in range(modes)]
    amp = [param_rows(par_ref, 1, m, modes, members) * jnp.sqrt(rate[m]) * w[m] for m in range(modes)]
    h = tuple(in_ref[chunk, 0, pl.ds(m, members, stride=modes), :] for m in range(modes))
    k = tuple(in_ref[chunk, 1, pl.ds(m, members, stride=modes), :] for m in range(modes))

    def forward(i, h):
        p = [amp[m] * (h[m] + hs_ref[chunk, i, pl.ds(m * members, members), :]) for m in range(modes)]
        for t in range(STRETCH):
            at = pl.ds((i * STRETCH + t) * members, members)
            yo_ref[at, :] = y_ref[pl.ds(((base + i) * STRETCH + t) * members, members), :] + total(p)
            if t < STRETCH - 1:
                p = [w[m] * p[m] for m in range(modes)]
        return tuple(fade[m] * h[m] for m in range(modes))

    def backward(i, k):
        back = stretches - 1 - i
        q = [amp[m] * (k[m] + ks_ref[chunk, back + 1, pl.ds(m * members, members), :]) for m in range(modes)]
        for t in range(STRETCH):
            row = back * STRETCH + STRETCH - 1 - t
            zo_ref[pl.ds(row * members, members), :] = z_ref[pl.ds((base * STRETCH + row) * members, members), :] + total(q)
            if t < STRETCH - 1:
                q = [w[m] * q[m] for m in range(modes)]
        return tuple(fade[m] * k[m] for m in range(modes))

    def put(source, store):
        for tile in range(tokens // 16):
            rows = pl.ds(tile * 16, 16)
            for member in range(members):
                halves = [pl.ds((tile * 16 + half * 8) * members + member, 8, stride=members) for half in range(2)]
                store(rows, member, jnp.concatenate([source[at, :] for at in halves], axis=0).astype(BF16))

    def store_y(rows, member, value):
        if own:
            cols = set_columns(ranked(me_ref, member, members), core)
            dq_ref[rows, cols] = (u_ref[rows, cols].astype(F32) * value.astype(F32)).astype(BF16)
        else:
            send_ref[0, member, rows, :] = value

    def store_z(rows, member, value):
        if own:
            cols = set_columns(ranked(me_ref, member, members), core)
            value = value.astype(F32)
            dk_ref[rows, cols] = (value * v_ref[rows, cols].astype(F32)).astype(BF16)
            dv_ref[rows, cols] = (value * k_ref[rows, cols].astype(F32)).astype(BF16)
        else:
            send_ref[1, member, rows, :] = value

    lax.fori_loop(0, stretches, forward, h)
    put(yo_ref, store_y)
    lax.fori_loop(0, stretches, backward, k)
    put(zo_ref, store_z)


def last_kernel(me_ref, got_ref, k_ref, v_ref, u_ref, *refs, tokens, modes, members, span, scale, tree):
    refs = list(refs)
    if tree:
        kept_ref, a_ref, b_ref, c_ref, own_ref = refs[:5]
        refs = refs[5:]
    dq_ref, dk_ref, dv_ref, dq_hbm, dk_hbm, dv_hbm = refs[3:9]
    me = me_ref[0]
    core = me % SETS
    copies = []
    if tree:
        r_hbm, log_hbm, sems, par_sems, out_ref, group_ref = refs[9:]
        place = me // span
        group_ref[place] = kept_ref[...]
        for hop, ref in zip(HOPS, (a_ref, b_ref, c_ref)):
            for i in range(6):
                group_ref[place ^ hop, i] = ref[pl.ds((members + i) * modes, modes), :].astype(F32)
        rate, residue = own_ref[0], own_ref[1]
        w = jnp.exp(-rate)
        width = float(tokens * span)
        fade = jnp.exp(rate * -width)
        r, d, sd, _, s, _ = (group_ref[0, i] for i in range(6))
        for z in range(1, WAYS):
            r_b, d_b, sd_b, kd_b, s_b, k_b = (group_ref[z, i] for i in range(6))
            r = r + r_b + w * (s * k_b)
            d = d + d_b + w * (s * kd_b + (sd + s) * k_b)
            sd = fade * (sd + width * s) + sd_b
            s = fade * s + s_b
        root = jnp.sqrt(rate) * scale
        out_ref[0] = root * r
        out_ref[1] = root * residue * (0.5 * r - rate * d)
        for i, ref in enumerate((r_hbm, log_hbm)):
            copies.append(pltpu.make_async_copy(out_ref.at[i], ref, par_sems.at[i]))
            copies[-1].start()
    else:
        (sems,) = refs[9:]
    for tile in range(tokens // 16):
        rows = pl.ds(tile * 16, 16)
        for member in range(members):
            cols = set_columns(ranked(me_ref, member, members), 1 - core)
            y = got_ref[0, member, rows, :].astype(F32)
            z = got_ref[1, member, rows, :].astype(F32)
            dq_ref[rows, cols] = (u_ref[rows, cols].astype(F32) * y).astype(BF16)
            dk_ref[rows, cols] = (z * v_ref[rows, cols].astype(F32)).astype(BF16)
            dv_ref[rows, cols] = (z * k_ref[rows, cols].astype(F32)).astype(BF16)
        for i, (ref, out) in enumerate(((dq_ref, dq_hbm), (dk_ref, dk_hbm), (dv_ref, dv_hbm))):
            copies.append(pltpu.make_async_copy(ref.at[rows], out.at[rows], sems.at[i, tile]))
            copies[-1].start()
    for copy in copies:
        copy.wait()


def call(body, out_shape, in_specs, flops, out_specs=None, scratch=(), aliases=None):
    return pl.pallas_call(
        body,
        out_shape=out_shape,
        in_specs=in_specs,
        out_specs=jax.tree.map(lambda _: VMEM, out_shape) if out_specs is None else out_specs,
        scratch_shapes=scratch,
        input_output_aliases=aliases or {},
        compiler_params=pltpu.CompilerParams(vmem_limit_bytes=16 * 1024 * 1024),
        cost_estimate=pl.CostEstimate(flops=flops, bytes_accessed=1024 * 1024, transcendentals=0),
    )


def exchange(value, distance, count):
    return lax.ppermute(value, "ctx", [(i, i ^ distance) for i in range(count)])


def tie(*values):
    return lax.optimization_barrier(values)


def local(query_proj, key_proj, value_proj, output_grad, residue, decay_rate):
    tokens, channels = query_proj.shape
    own_channels, modes = residue.shape
    count = lax.axis_size("ctx")
    groups = channels // LANES
    members = groups // SETS
    rows = members * modes
    length = tokens * SETS
    top = count // WAYS
    tree = groups == count == SETS * 2 * WAYS and own_channels == LANES
    work = tokens * channels * modes
    index = lax.axis_index("ctx")
    core = index % SETS
    side = (index // SETS) % 2
    me = index.astype(jnp.int32).reshape(1)

    def shape(*dims, dtype=F32):
        return jax.ShapeDtypeStruct(dims, dtype)

    half = shape(2, members, tokens, LANES, dtype=BF16)
    series = shape(length * members, LANES)
    half_series = shape(tokens * members, LANES)
    pieces = 4
    pair = shape(2, rows, LANES)
    stretches = tokens // STRETCH
    sizes = dict(tokens=tokens, modes=modes, members=members)

    def chip_states(flip, gated, gate_grad, par):
        states = shape(2, 2, rows // 2, LANES), shape(stretches, modes, members, LANES), shape(stretches + 1, modes, members, LANES)
        out = call(
            functools.partial(state_kernel, flip=flip, **sizes), states + (half_series,) * 2, [SMEM] + [VMEM] * 3, work * 2
        )(me, gated, gate_grad, par)
        return list(out)

    own_gates, send_gates = call(
        functools.partial(gate_kernel, members=members, pieces=pieces),
        (half, half),
        [SMEM] + [HBM] * 4,
        work,
        scratch=(pltpu.VMEM((4, tokens, channels), BF16), pltpu.SemaphoreType.DMA((pieces, 4))),
    )(me, *(pltpu.with_memory_space_constraint(a, pltpu.HBM) for a in (query_proj, key_proj, value_proj, output_grad)))

    (own,) = tie(jnp.stack([decay_rate.T, residue.T]))
    params, axis = own, 0
    distance = count // 2
    while distance > (1 if tree else 0):
        other = exchange(params, distance, count)
        if axis == 0:
            other, own_gates, send_gates = tie(other, own_gates, send_gates)
            got_gates = exchange(send_gates, 1, count)
            gated, gate_grad, lags = call(
                functools.partial(series_kernel, tokens=tokens, members=members),
                (shape(2, tokens * members, LANES),) * 2 + (shape(2, STRETCH, members, LANES),),
                [SMEM] + [VMEM] * 2,
                work,
            )(me, own_gates, got_gates)
        if axis == 1:
            other, gated, gate_grad, lags = tie(other, gated, gate_grad, lags)
        if tree and distance == SETS:
            par_own, par_far = (a.reshape(rows, LANES) for a in (params, other))
            states_own = chip_states(False, gated, gate_grad, par_own)
            par_far, states_own[0] = tie(par_far, states_own[0])
            break
        upper = (index // distance) % 2 == 1
        params = jnp.stack([jnp.where(upper, other, params), jnp.where(upper, params, other)], axis=axis)
        distance //= 2
        axis += 1
    if not tree:
        params = params.reshape((count,) + own.shape).transpose(1, 2, 0, 3).reshape(2, modes, members, SETS, LANES)
        params = lax.dynamic_index_in_dim(params, core, 3, keepdims=False).transpose(2, 0, 1, 3)
        halves = params.reshape(members // 2, 2, 2, modes, LANES)
        par_own, par_far = (
            lax.dynamic_index_in_dim(halves, s, 1, keepdims=False).reshape(rows, LANES) for s in (side, 1 - side)
        )
        states_own = chip_states(False, gated, gate_grad, par_own)
    par = jnp.concatenate([par_own, par_far])

    sk_far, hs_far, ks_far, *weighted_far = chip_states(True, gated, gate_grad, par_far)
    sk_own, hs_own, ks_own, *weighted_own = states_own

    def message_shapes(span):
        if span == top:
            return (shape(rows + (6 * modes if tree else 0), LANES, dtype=BF16),) * (WAYS - 1)
        return (shape(rows * 2 + (4 * rows // span if tree else 0), LANES, dtype=BF16),)

    def chip_sums(flip, outs, weighted, hs, ks, sk, *par):
        return call(
            functools.partial(sums_kernel, part=min(4, modes), unroll=4, flip=flip, tree=tree, **sizes),
            (() if flip and tree else (shape(4, rows // 2, LANES),)) + outs,
            [SMEM] + [VMEM] * (6 + len(par)),
            work * 3,
            scratch=(pltpu.VMEM((4, 2, rows // 2, LANES), F32),),
        )(me, *weighted, lags, hs, ks, sk, *par)

    *sums_far, tot, message = chip_sums(
        True, (pair, *message_shapes(SETS)), weighted_far, hs_far, ks_far, sk_far, par_far, sk_own, par_own
    )
    messages = [message]
    tot, weighted_own[0] = tie(tot, weighted_own[0])
    (sums_own,) = chip_sums(False, (), weighted_own, hs_own, ks_own, sk_own, par_own)

    enter, span, pair_tot, kept = tot, SETS, tot, [sums_own] if tree else []
    while span < top:
        got = exchange(messages[0], span, count)
        last = span * 2 == top
        extra = (shape(6, modes, LANES) if last else shape(4, rows // span // 2, LANES),) if tree else ()
        out = call(
            functools.partial(level_kernel, span=span, last=last, tree=tree, **sizes),
            (pair,) * (1 if last else 2) + message_shapes(span * 2) + extra,
            [SMEM] + [VMEM] * (5 if tree else 4),
            rows,
            scratch=(pltpu.VMEM((members // 2, 6, modes, LANES), F32),) if tree else (),
        )(me, tot, got, enter, par, *kept)
        if not last:
            tot, *out = out
        enter, *messages = out
        if tree:
            kept = [messages.pop()]
        if span == SETS:
            enter, hs_own, gated, gate_grad = tie(enter, hs_own, gated, gate_grad)
        span *= 2
    far = [exchange(message, hop * top, count) for hop, message in zip(HOPS, messages)]
    hs, ks = call(
        functools.partial(order_kernel, **sizes),
        (shape(2, stretches, modes * members, LANES), shape(2, stretches + 1, modes * members, LANES)),
        [VMEM] * 4,
        work,
    )(hs_own, ks_own, hs_far, ks_far)
    y, z = call(functools.partial(taps_kernel, **sizes), (series, series), [SMEM] + [VMEM] * 3, work)(
        me, gated, gate_grad, par
    )
    far[0], y, hs = tie(far[0], y, hs)
    (states_in,) = call(
        functools.partial(enter_kernel, span=top, **sizes), (shape(2, 2, rows, LANES),), [SMEM] + [VMEM] * 7, rows
    )(me, enter, *far, par, sk_own, sk_far)

    scratch = (pltpu.VMEM((tokens * members, LANES), F32),) * 2
    finish = functools.partial(finish_kernel, tokens=tokens, modes=modes, members=members)
    (send_conv,) = call(functools.partial(finish, own=False), (half,), [SMEM] + [VMEM] * 6, work * 2, scratch=scratch)(
        me, y, z, hs, ks, par, states_in
    )
    got_conv = exchange(send_conv, 1, count)
    grads = (shape(tokens, channels, dtype=BF16),) * 3
    done = call(functools.partial(finish, own=True), grads, [SMEM] + [VMEM] * 9, work * 2, scratch=scratch)(
        me, y, z, hs, ks, par, states_in, key_proj, value_proj, output_grad
    )
    scale = float(tokens * count) ** (-0.5)
    extra = (*kept, *far, own) if tree else ()
    first = 5 + len(extra)
    out = call(
        functools.partial(last_kernel, tokens=tokens, modes=modes, members=members, span=top, scale=scale, tree=tree),
        grads + grads + ((shape(modes, LANES),) * 2 if tree else ()),
        [SMEM] + [VMEM] * (first + 2),
        work,
        (VMEM,) * 3 + (ANY,) * (5 if tree else 3),
        (pltpu.SemaphoreType.DMA((3, tokens // 16)),)
        + ((pltpu.SemaphoreType.DMA((2,)), pltpu.VMEM((2, modes, LANES), F32), pltpu.VMEM((WAYS, 6, modes, LANES), F32)) if tree else ()),
        {first: 0, first + 1: 1, first + 2: 2},
    )(me, got_conv, key_proj, value_proj, output_grad, *extra, *done)

    if tree:
        residue_grad, log_grad = out[6].T, out[7].T
    else:
        dims = (members, modes, LANES)

        def by_member(a):
            a = a.reshape(2, members // 2, modes, LANES)
            return jnp.where(side == 0, a, a[::-1]).transpose(1, 0, 2, 3).reshape(dims)

        h_in, k_in = by_member(states_in[0, 0]), by_member(states_in[1, 1])
        s, k = (by_member(a) for a in pair_tot)
        r, d, s_d, k_d = (by_member(jnp.stack([a, b])) for a, b in zip(sums_own, sums_far[0]))
        rate = params[:, 0]
        w = jnp.exp(-rate)
        r = r + w * h_in * k
        d = d + w * (h_in * k_d + k_in * (s_d + s)) + float(length) * jnp.exp(-rate * float(length + 1)) * h_in * k_in
        parts = jnp.stack([r, d], axis=1)
        parts = jnp.stack([jnp.where(core == 0, parts, 0.0), jnp.where(core == 1, parts, 0.0)], axis=1)
        parts = parts.reshape(groups, 2, modes, LANES).transpose(1, 2, 0, 3)
        parts = parts.reshape(2, modes, count, own_channels).transpose(2, 0, 1, 3)
        sums = lax.all_to_all(parts, "ctx", split_axis=0, concat_axis=0, tiled=True).sum(axis=0)
        root = scale * jnp.sqrt(decay_rate)
        residue_grad = root * sums[0].T
        log_grad = root * residue * (0.5 * sums[0].T - decay_rate * sums[1].T)
    return out[3], out[4], out[5], residue_grad, log_grad


def solution(mesh):
    in_specs = (P("ctx", "ch"),) * 4 + (P(("ch", "ctx"), None),) * 2
    out_specs = (P("ctx", "ch"),) * 3 + (P(("ch", "ctx"), None),) * 2
    return jax.shard_map(local, mesh=mesh, in_specs=in_specs, out_specs=out_specs, check_vma=False)
```

```python
import functools

import jax
import jax.numpy as jnp
from jax import lax
from jax.experimental import pallas as pl
from jax.experimental.pallas import tpu as pltpu
from jax.sharding import PartitionSpec as P

LANES = 128
SETS = 2
STRETCH = 8
WAYS = 4
HOPS = (3, 1, 2)
F32 = jnp.float32
BF16 = jnp.bfloat16
VMEM = pl.BlockSpec(memory_space=pltpu.VMEM)
SMEM = pl.BlockSpec(memory_space=pltpu.SMEM)
ANY = pl.BlockSpec(memory_space=pl.ANY)
HBM = pl.BlockSpec(memory_space=pltpu.HBM)


def total(terms):
    terms = list(terms)
    while len(terms) > 1:
        terms = [a + b for a, b in zip(terms[::2], terms[1::2])] + terms[len(terms) & ~1 :]
    return terms[0]


def set_columns(member, which):
    return pl.ds(pl.multiple_of((member * SETS + which) * LANES, LANES), LANES)


def gate_kernel(me_ref, q_hbm, k_hbm, v_hbm, u_hbm, own_ref, send_ref, stage_ref, sems, *, members, pieces):
    tokens = q_hbm.shape[0]
    core = me_ref[0] % SETS
    rows = tokens // pieces
    copies = []
    for piece in range(pieces):
        at = pl.ds(piece * rows, rows)
        for i, ref in enumerate((q_hbm, k_hbm, v_hbm, u_hbm)):
            copies.append(pltpu.make_async_copy(ref.at[at], stage_ref.at[i, at], sems.at[piece, i]))
            copies[-1].start()

    def body(tile, _):
        at = pl.ds(pl.multiple_of(tile * 16, 16), 16)
        for out_ref, which in ((own_ref, core), (send_ref, 1 - core)):
            for member in range(members):
                cols = set_columns(member, which)
                q, k, v, u = (stage_ref[i, at, cols].astype(F32) for i in range(4))
                out_ref[0, member, at, :] = (k * v).astype(BF16)
                out_ref[1, member, at, :] = (u * q).astype(BF16)
        return 0

    for piece in range(pieces):
        for copy in copies[piece * 4 : piece * 4 + 4]:
            copy.wait()
        lax.fori_loop(piece * rows // 16, (piece + 1) * rows // 16, body, 0)


def series_kernel(me_ref, own_ref, got_ref, x_ref, g_ref, lag_ref, *, tokens, members):
    core = me_ref[0] % SETS
    half = members // 2
    for ref, chunk in ((own_ref, core), (got_ref, 1 - core)):

        def body(tile, _):
            rows = pl.ds(pl.multiple_of(tile * 16, 16), 16)
            for member in range(members):
                for i, out_ref in enumerate((x_ref, g_ref)):
                    value = ref[i, member, rows, :].astype(F32)
                    for part in range(2):
                        start = (tile * 16 + part * 8) * members + chunk * half + member // 2
                        out_ref[member % 2, pl.ds(start, 8, stride=members), :] = value[part * 8 : part * 8 + 8]
            return 0

        lax.fori_loop(0, tokens // 16, body, 0)

    for side in range(2):

        def step(i, lags):
            x = [x_ref[side, pl.ds((i * STRETCH + t) * members, members), :] for t in range(STRETCH)]
            g = [g_ref[side, pl.ds((i * STRETCH + t) * members, members), :] for t in range(STRETCH)]
            return tuple(lags[j] + total([g[t] * x[t - j] for t in range(j, STRETCH)]) for j in range(STRETCH))

        zero = tuple(jnp.zeros((members, LANES), F32) for _ in range(STRETCH))
        lags = lax.fori_loop(0, tokens // STRETCH, step, zero)
        for j in range(STRETCH):
            lag_ref[side, j] = lags[j]


def param_rows(par_ref, param, mode, modes, members):
    return par_ref[pl.ds(param * modes + mode, members, stride=2 * modes), :]


def half_rows(par_ref, start, stride, members):
    rows = par_ref[pl.ds(start, members // 2, stride=stride), :]
    return jnp.concatenate([rows, rows], axis=0)


def chosen_half(me_ref, flip):
    side = (me_ref[0] // SETS) % 2
    return 1 - side if flip else side


def ranked(me_ref, rank, members):
    half = members // 2
    return rank % half * 2 + chosen_half(me_ref, rank >= half)


def state_kernel(me_ref, x_ref, g_ref, par_ref, sk_ref, hs_ref, ks_ref, xw_ref, gw_ref, *, tokens, modes, members, flip):
    side = chosen_half(me_ref, flip)
    half = members // 2
    w = [jnp.exp(-half_rows(par_ref, m, 2 * modes, members)) for m in range(modes)]
    stretches = tokens // STRETCH

    def step(i, carry):
        s, k = carry
        back = stretches - 1 - i
        for m in range(modes):
            hs_ref[i, m] = s[m]
        for t in range(STRETCH):
            at = pl.ds((i * STRETCH + t) * members, members)
            at_back = pl.ds((back * STRETCH + STRETCH - 1 - t) * members, members)
            x, g = x_ref[side, at, :], g_ref[side, at_back, :]
            xw_ref[at, :] = x * float(STRETCH - 1 - t)
            gw_ref[at_back, :] = g * float(STRETCH - 1 - t)
            s = tuple(w[m] * s[m] + x for m in range(modes))
            k = tuple(w[m] * k[m] + g for m in range(modes))
        for m in range(modes):
            ks_ref[back, m] = k[m]
        return s, k

    zero = tuple(jnp.zeros((members, LANES), F32) for _ in range(modes))
    for m in range(modes):
        ks_ref[stretches, m] = zero[m]
    s, k = lax.fori_loop(0, stretches, step, (zero, zero), unroll=2)
    for m in range(modes):
        at = pl.ds(m, half, stride=modes)
        for i, value in enumerate((s[m], k[m])):
            sk_ref[i, 0, at, :] = value[:half]
            sk_ref[i, 1, at, :] = value[half:]


def taps_kernel(me_ref, x_ref, g_ref, par_ref, y_ref, z_ref, *, tokens, modes, members):
    half = members // 2
    for flip in (0, 1):
        side = chosen_half(me_ref, flip)
        start = flip * half * 2 * modes
        rate = [half_rows(par_ref, start + m, 2 * modes, members) for m in range(modes)]
        w = [jnp.exp(-rate[m]) for m in range(modes)]
        power = [half_rows(par_ref, start + modes + m, 2 * modes, members) * jnp.sqrt(rate[m]) for m in range(modes)]
        taps = []
        for j in range(STRETCH):
            taps.append(total(power))
            power = [power[m] * w[m] for m in range(modes)]

        def within(i, _):
            at = [pl.ds((i * STRETCH + t) * members, members) for t in range(STRETCH)]
            x = [x_ref[side, at[t], :] for t in range(STRETCH)]
            g = [g_ref[side, at[t], :] for t in range(STRETCH)]
            for t in range(STRETCH):
                y = total([taps[j] * x[t - j] for j in range(t + 1)])
                z = total([taps[j] * g[t + j] for j in range(STRETCH - t)])
                for chunk in range(2):
                    to = pl.ds((chunk * tokens + i * STRETCH + t) * members + flip * half, half)
                    y_ref[to, :] = y[chunk * half : (chunk + 1) * half]
                    z_ref[to, :] = z[chunk * half : (chunk + 1) * half]
            return 0

        lax.fori_loop(0, tokens // STRETCH, within, 0, unroll=2)


def order_kernel(hs_own, ks_own, hs_far, ks_far, par_ref, hs_ref, ks_ref, const_ref, *, tokens, modes, members):
    half = members // 2
    for m in range(modes):
        rate = param_rows(par_ref, 0, m, modes, members)
        w = jnp.exp(-rate)
        const_ref[0, m] = w
        const_ref[1, m] = jnp.exp(rate * -float(STRETCH))
        const_ref[2, m] = param_rows(par_ref, 1, m, modes, members) * jnp.sqrt(rate) * w
    amp = []
    for flip in range(2):
        start = flip * half * 2 * modes
        rates = [half_rows(par_ref, start + m, 2 * modes, members) for m in range(modes)]
        residues = [half_rows(par_ref, start + modes + m, 2 * modes, members) for m in range(modes)]
        amp.append([residues[m] * jnp.sqrt(rates[m]) * jnp.exp(-rates[m]) for m in range(modes)])
    for src, out, count in ((0, hs_ref, tokens // STRETCH), (1, ks_ref, tokens // STRETCH + 1)):

        def body(i, _):
            for flip, ref in ((0, (hs_own, ks_own)[src]), (1, (hs_far, ks_far)[src])):
                for m in range(modes):
                    value = ref[i, m] * amp[flip][m]
                    for chunk in range(2):
                        out[chunk, i, pl.ds(m * members + flip * half, half), :] = value[chunk * half : (chunk + 1) * half]
            return 0

        lax.fori_loop(0, count, body, 0)


def flags(bit):
    bit = bit.astype(F32)
    return bit, 1.0 - bit


def put_states(refs, me, span, at, at_k, s, k, last):
    if last:
        place = me // span
        for hop, ref in zip(HOPS, refs):
            earlier, later = flags((place ^ hop) < place)
            ref[at, :] = (earlier * k + later * s).astype(BF16)
    else:
        refs[0][at, :] = s.astype(BF16)
        refs[0][at_k, :] = k.astype(BF16)


def blocks(rank, modes, members):
    return pl.ds(rank * modes, modes), pl.ds((members + rank) * modes, modes)


def sums_kernel(me_ref, x_ref, g_ref, lag_ref, hs_ref, ks_ref, sk_ref, par_ref, *refs, tokens, modes, members, part, unroll, flip, tree):
    if flip:
        sk_own, par_own, *sums_ref, tot_ref, message_ref, work_ref = refs
    else:
        *sums_ref, work_ref = refs
    side = chosen_half(me_ref, flip)
    half = members // 2
    stretches = tokens // STRETCH
    width = float(STRETCH)
    zero = jnp.zeros((members, LANES), F32)
    for first in range(0, modes, part):
        rate = [half_rows(par_ref, first + m, 2 * modes, members) for m in range(part)]
        w = [jnp.exp(-rate[m]) for m in range(part)]
        fade = [jnp.exp(rate[m] * -width) for m in range(part)]

        def step(i, carry):
            back = stretches - 1 - i
            x = [x_ref[pl.ds((i * STRETCH + t) * members, members), :] for t in range(STRETCH - 1)]
            g = [g_ref[pl.ds((back * STRETCH + t) * members, members), :] for t in range(STRETCH)]
            out = []
            for m in range(part):
                same, next_, b_k, b_s, sd, kd = carry[m]
                h, k = hs_ref[i, first + m], ks_ref[i, first + m]
                h_back = hs_ref[back, first + m]
                k_after, k_back = ks_ref[i + 1, first + m], ks_ref[back + 1, first + m]
                s_own = x[0]
                for t in range(1, STRETCH - 1):
                    s_own = s_own * w[m] + x[t]
                s_own = s_own * w[m]
                k_own = g[STRETCH - 1]
                for t in range(STRETCH - 2, 0, -1):
                    k_own = k_own * w[m] + g[t]
                k_own = k_own * w[m]
                out.append(
                    (
                        same + h * k,
                        next_ + h * k_after,
                        b_k + h_back * k_own,
                        b_s + k_after * s_own,
                        fade[m] * (sd + width * h) + s_own,
                        fade[m] * (kd + width * k_back) + k_own,
                    )
                )
            return tuple(out)

        sums = lax.fori_loop(0, stretches, step, ((zero,) * 6,) * part, unroll=unroll)
        lags = [lag_ref[side, j] for j in range(STRETCH)]
        for m in range(part):
            same, next_, b_k, b_s, sd, kd = sums[m]
            r, d = lags[STRETCH - 1], (width - 1.0) * lags[STRETCH - 1]
            for j in range(STRETCH - 2, -1, -1):
                r = r * w[m] + lags[j]
                d = d * w[m] + float(j) * lags[j]
            r = r + w[m] * (same - fade[m] * next_)
            d = d + w[m] * (b_k + b_s + same + (width - 1.0) * (fade[m] * next_))
            at = pl.ds(first + m, half, stride=modes)
            for i, value in enumerate((r, d, sd, kd)):
                work_ref[i, 0, at, :] = value[:half]
                work_ref[i, 1, at, :] = value[half:]

    me = me_ref[0]
    rows = members * modes
    for z in range(half):
        at = pl.ds(z * modes, modes)
        left, right = (tuple(work_ref[i, c, at, :] for i in range(4)) + (sk_ref[0, c, at, :], sk_ref[1, c, at, :]) for c in range(2))
        rate = par_ref[pl.ds(z * 2 * modes, modes), :]
        for i, value in enumerate(join(rate, left, right, float(tokens))):
            for ref in sums_ref:
                ref[i, at, :] = value
            if flip and tree:
                message_ref[pl.ds(rows * 2 + (i * half + z) * modes, modes), :] = value.astype(BF16)
        if flip:
            for ref, rank, par in ((sk_ref, half + z, par_ref), (sk_own, z, par_own)):
                fade = jnp.exp(par[pl.ds(z * 2 * modes, modes), :] * -float(tokens))
                s = fade * ref[0, 0, at, :] + ref[0, 1, at, :]
                k = ref[1, 0, at, :] + fade * ref[1, 1, at, :]
                to, to_k = blocks(rank, modes, members)
                tot_ref[0, to, :] = s
                tot_ref[1, to, :] = k
                put_states([message_ref], me, SETS, to, to_k, s, k, False)


def join(rate, left, right, length):
    r_a, d_a, sd_a, kd_a, s_a, k_a = left
    r_b, d_b, sd_b, kd_b, s_b, k_b = right
    w = jnp.exp(-rate)
    fade = jnp.exp(rate * -length)
    r = r_a + r_b + w * (s_a * k_b)
    d = d_a + d_b + w * (s_a * kd_b + (sd_a + s_a) * k_b)
    sd = fade * (sd_a + length * s_a) + sd_b
    kd = kd_a + fade * (kd_b + length * k_b)
    return r, d, sd, kd


def level_kernel(
    me_ref, tot_ref, got_ref, enter_ref, par_ref, *refs, tokens, modes, members, span, last, tree
):
    refs = list(refs)
    if tree:
        kept_ref, work_ref, keep_ref = refs.pop(0), refs.pop(), refs.pop()
    out_ref = None if last else refs.pop(0)
    new_ref, *messages = refs
    me = me_ref[0]
    second = (me // span) % 2
    earlier, later = flags(second == 1)
    inside = (me // 2) % (span // 2) * 2
    gap = earlier * inside.astype(F32) + later * (span - 2 - inside).astype(F32)
    rows = members * modes
    half = members // 2

    def received(rank):
        at, at_k = blocks((rank + half) % members if span == 2 else rank, modes, members)
        return got_ref[at, :].astype(F32), got_ref[at_k, :].astype(F32)

    sums = []
    for rank in range(members):
        at, at_k = blocks(rank, modes, members)
        rate = par_ref[pl.ds(rank * 2 * modes, modes), :]
        far = jnp.exp(rate * -float(tokens * span))
        weight = jnp.exp(rate * (gap * -float(tokens)))
        s, k = tot_ref[0, at, :], tot_ref[1, at, :]
        gs, gk = received(rank)
        s_sum = earlier * (far * gs + s) + later * (far * s + gs)
        k_sum = earlier * (gk + far * k) + later * (k + far * gk)
        if not last:
            out_ref[0, at, :] = s_sum
            out_ref[1, at, :] = k_sum
        before = earlier * (weight * gs)
        after = later * (weight * gk)
        if span > 2:
            before += enter_ref[0, at, :]
            after += enter_ref[1, at, :]
        new_ref[0, at, :] = before
        new_ref[1, at, :] = after
        put_states(messages, me, span * 2, at, at_k, s_sum, k_sum, last)
        if tree and span == 2 and rank < half:
            block = pl.ds(rank * modes, modes)
            mine = tuple(kept_ref[i, block, :] for i in range(4)) + (s, k)
            theirs = tuple(got_ref[pl.ds(rows * 2 + (i * half + rank) * modes, modes), :].astype(F32) for i in range(4)) + (gs, gk)
            left = tuple(earlier * b + later * a for a, b in zip(mine, theirs))
            right = tuple(earlier * a + later * b for a, b in zip(mine, theirs))
            for i, value in enumerate(join(rate, left, right, float(tokens * span)) + (s_sum, k_sum)):
                work_ref[rank, i] = value
    if tree:
        place = me // (span * 2)
        keep_ref[...] = work_ref[place]
        for hop, ref in zip(HOPS, messages):
            for i in range(6):
                ref[pl.ds(rows + i * modes, modes), :] = work_ref[place ^ hop, i].astype(BF16)


def enter_kernel(me_ref, enter_ref, a_ref, b_ref, c_ref, par_ref, sk_own, sk_far, in_ref, *, tokens, modes, members, span):
    me = me_ref[0]
    place = me // span
    inside = (me // 2) % (span // 2) * 2
    partners = []
    for hop, ref in zip(HOPS, (a_ref, b_ref, c_ref)):
        partner = place ^ hop
        earlier, later = flags(partner < place)
        gap = earlier * (span * (place - partner - 1) + inside).astype(F32)
        gap += later * (span * (partner - place - 1) + (span - 2 - inside)).astype(F32)
        partners.append((ref, earlier, later, gap * -float(tokens)))
    for ref, flip in ((sk_own, 0), (sk_far, 1)):
        for z in range(members // 2):
            src = pl.ds(z * modes, modes)
            rank = flip * (members // 2) + z
            at, _ = blocks(rank, modes, members)
            rate = par_ref[pl.ds(rank * 2 * modes, modes), :]
            before, after = enter_ref[0, at, :], enter_ref[1, at, :]
            for got_ref, earlier, later, gap in partners:
                value = jnp.exp(rate * gap) * got_ref[at, :].astype(F32)
                before += earlier * value
                after += later * value
            fade = jnp.exp(rate * -float(tokens))
            in_ref[0, 0, at, :] = before
            in_ref[0, 1, at, :] = ref[1, 1, src, :] + fade * after
            in_ref[1, 0, at, :] = ref[0, 0, src, :] + fade * before
            in_ref[1, 1, at, :] = after


def finish_kernel(me_ref, y_ref, z_ref, hs_ref, ks_ref, const_ref, in_ref, *refs, tokens, modes, members, own):
    if own:
        k_ref, v_ref, u_ref, dq_ref, dk_ref, dv_ref, yo_ref, zo_ref = refs
    else:
        send_ref, yo_ref, zo_ref = refs
    core = me_ref[0] % SETS
    chunk = core if own else 1 - core
    stretches = tokens // STRETCH
    base = chunk * stretches
    w, fade, amp = ([const_ref[i, m] for m in range(modes)] for i in range(3))
    h = tuple(amp[m] * in_ref[chunk, 0, pl.ds(m, members, stride=modes), :] for m in range(modes))
    k = tuple(amp[m] * in_ref[chunk, 1, pl.ds(m, members, stride=modes), :] for m in range(modes))

    def forward(i, h):
        p = [h[m] + hs_ref[chunk, i, pl.ds(m * members, members), :] for m in range(modes)]
        for t in range(STRETCH):
            at = pl.ds((i * STRETCH + t) * members, members)
            yo_ref[at, :] = y_ref[pl.ds(((base + i) * STRETCH + t) * members, members), :] + total(p)
            if t < STRETCH - 1:
                p = [w[m] * p[m] for m in range(modes)]
        return tuple(fade[m] * h[m] for m in range(modes))

    def backward(i, k):
        back = stretches - 1 - i
        q = [k[m] + ks_ref[chunk, back + 1, pl.ds(m * members, members), :] for m in range(modes)]
        for t in range(STRETCH):
            row = back * STRETCH + STRETCH - 1 - t
            zo_ref[pl.ds(row * members, members), :] = z_ref[pl.ds((base * STRETCH + row) * members, members), :] + total(q)
            if t < STRETCH - 1:
                q = [w[m] * q[m] for m in range(modes)]
        return tuple(fade[m] * k[m] for m in range(modes))

    def put(source, store):
        for tile in range(tokens // 16):
            rows = pl.ds(tile * 16, 16)
            for member in range(members):
                halves = [pl.ds((tile * 16 + half * 8) * members + member, 8, stride=members) for half in range(2)]
                store(rows, member, jnp.concatenate([source[at, :] for at in halves], axis=0).astype(BF16))

    def store_y(rows, member, value):
        if own:
            cols = set_columns(ranked(me_ref, member, members), core)
            dq_ref[rows, cols] = (u_ref[rows, cols].astype(F32) * value.astype(F32)).astype(BF16)
        else:
            send_ref[0, member, rows, :] = value

    def store_z(rows, member, value):
        if own:
            cols = set_columns(ranked(me_ref, member, members), core)
            value = value.astype(F32)
            dk_ref[rows, cols] = (value * v_ref[rows, cols].astype(F32)).astype(BF16)
            dv_ref[rows, cols] = (value * k_ref[rows, cols].astype(F32)).astype(BF16)
        else:
            send_ref[1, member, rows, :] = value

    lax.fori_loop(0, stretches, forward, h, unroll=4)
    put(yo_ref, store_y)
    lax.fori_loop(0, stretches, backward, k, unroll=4)
    put(zo_ref, store_z)


def last_kernel(me_ref, got_ref, k_ref, v_ref, u_ref, *refs, tokens, modes, members, span, scale, tree):
    refs = list(refs)
    if tree:
        kept_ref, a_ref, b_ref, c_ref, own_ref = refs[:5]
        refs = refs[5:]
    dq_ref, dk_ref, dv_ref, dq_hbm, dk_hbm, dv_hbm = refs[3:9]
    me = me_ref[0]
    core = me % SETS
    copies = []
    if tree:
        r_hbm, log_hbm, sems, par_sems, out_ref, group_ref = refs[9:]
        place = me // span
        group_ref[place] = kept_ref[...]
        for hop, ref in zip(HOPS, (a_ref, b_ref, c_ref)):
            for i in range(6):
                group_ref[place ^ hop, i] = ref[pl.ds((members + i) * modes, modes), :].astype(F32)
        rate, residue = own_ref[0], own_ref[1]
        w = jnp.exp(-rate)
        width = float(tokens * span)
        fade = jnp.exp(rate * -width)
        r, d, sd, _, s, _ = (group_ref[0, i] for i in range(6))
        for z in range(1, WAYS):
            r_b, d_b, sd_b, kd_b, s_b, k_b = (group_ref[z, i] for i in range(6))
            r = r + r_b + w * (s * k_b)
            d = d + d_b + w * (s * kd_b + (sd + s) * k_b)
            sd = fade * (sd + width * s) + sd_b
            s = fade * s + s_b
        root = jnp.sqrt(rate) * scale
        out_ref[0] = root * r
        out_ref[1] = root * residue * (0.5 * r - rate * d)
        for i, ref in enumerate((r_hbm, log_hbm)):
            copies.append(pltpu.make_async_copy(out_ref.at[i], ref, par_sems.at[i]))
            copies[-1].start()
    else:
        (sems,) = refs[9:]
    for tile in range(tokens // 16):
        rows = pl.ds(tile * 16, 16)
        for member in range(members):
            cols = set_columns(ranked(me_ref, member, members), 1 - core)
            y = got_ref[0, member, rows, :].astype(F32)
            z = got_ref[1, member, rows, :].astype(F32)
            dq_ref[rows, cols] = (u_ref[rows, cols].astype(F32) * y).astype(BF16)
            dk_ref[rows, cols] = (z * v_ref[rows, cols].astype(F32)).astype(BF16)
            dv_ref[rows, cols] = (z * k_ref[rows, cols].astype(F32)).astype(BF16)
        for i, (ref, out) in enumerate(((dq_ref, dq_hbm), (dk_ref, dk_hbm), (dv_ref, dv_hbm))):
            copies.append(pltpu.make_async_copy(ref.at[rows], out.at[rows], sems.at[i, tile]))
            copies[-1].start()
    for copy in copies:
        copy.wait()


def call(body, out_shape, in_specs, flops, out_specs=None, scratch=(), aliases=None):
    return pl.pallas_call(
        body,
        out_shape=out_shape,
        in_specs=in_specs,
        out_specs=jax.tree.map(lambda _: VMEM, out_shape) if out_specs is None else out_specs,
        scratch_shapes=scratch,
        input_output_aliases=aliases or {},
        compiler_params=pltpu.CompilerParams(vmem_limit_bytes=16 * 1024 * 1024),
        cost_estimate=pl.CostEstimate(flops=flops, bytes_accessed=1024 * 1024, transcendentals=0),
    )


def exchange(value, distance, count):
    return lax.ppermute(value, "ctx", [(i, i ^ distance) for i in range(count)])


def tie(*values):
    return lax.optimization_barrier(values)


def local(query_proj, key_proj, value_proj, output_grad, residue, decay_rate):
    tokens, channels = query_proj.shape
    own_channels, modes = residue.shape
    count = lax.axis_size("ctx")
    groups = channels // LANES
    members = groups // SETS
    rows = members * modes
    length = tokens * SETS
    top = count // WAYS
    tree = groups == count == SETS * 2 * WAYS and own_channels == LANES
    work = tokens * channels * modes
    index = lax.axis_index("ctx")
    core = index % SETS
    side = (index // SETS) % 2
    me = index.astype(jnp.int32).reshape(1)

    def shape(*dims, dtype=F32):
        return jax.ShapeDtypeStruct(dims, dtype)

    half = shape(2, members, tokens, LANES, dtype=BF16)
    series = shape(length * members, LANES)
    half_series = shape(tokens * members, LANES)
    pieces = 4
    pair = shape(2, rows, LANES)
    stretches = tokens // STRETCH
    sizes = dict(tokens=tokens, modes=modes, members=members)

    def chip_states(flip, gated, gate_grad, par):
        states = shape(2, 2, rows // 2, LANES), shape(stretches, modes, members, LANES), shape(stretches + 1, modes, members, LANES)
        out = call(
            functools.partial(state_kernel, flip=flip, **sizes), states + (half_series,) * 2, [SMEM] + [VMEM] * 3, work * 2
        )(me, gated, gate_grad, par)
        return list(out)

    own_gates, send_gates = call(
        functools.partial(gate_kernel, members=members, pieces=pieces),
        (half, half),
        [SMEM] + [HBM] * 4,
        work,
        scratch=(pltpu.VMEM((4, tokens, channels), BF16), pltpu.SemaphoreType.DMA((pieces, 4))),
    )(me, *(pltpu.with_memory_space_constraint(a, pltpu.HBM) for a in (query_proj, key_proj, value_proj, output_grad)))

    (own,) = tie(jnp.stack([decay_rate.T, residue.T]))
    params, axis = own, 0
    distance = count // 2
    while distance > (1 if tree else 0):
        other = exchange(params, distance, count)
        if axis == 0:
            other, own_gates, send_gates = tie(other, own_gates, send_gates)
            got_gates = exchange(send_gates, 1, count)
            gated, gate_grad, lags = call(
                functools.partial(series_kernel, tokens=tokens, members=members),
                (shape(2, tokens * members, LANES),) * 2 + (shape(2, STRETCH, members, LANES),),
                [SMEM] + [VMEM] * 2,
                work,
            )(me, own_gates, got_gates)
        if axis == 1:
            other, gated, gate_grad, lags = tie(other, gated, gate_grad, lags)
        if tree and distance == SETS:
            par_own, par_far = (a.reshape(rows, LANES) for a in (params, other))
            states_own = chip_states(False, gated, gate_grad, par_own)
            par_far, states_own[0] = tie(par_far, states_own[0])
            break
        upper = (index // distance) % 2 == 1
        params = jnp.stack([jnp.where(upper, other, params), jnp.where(upper, params, other)], axis=axis)
        distance //= 2
        axis += 1
    if not tree:
        params = params.reshape((count,) + own.shape).transpose(1, 2, 0, 3).reshape(2, modes, members, SETS, LANES)
        params = lax.dynamic_index_in_dim(params, core, 3, keepdims=False).transpose(2, 0, 1, 3)
        halves = params.reshape(members // 2, 2, 2, modes, LANES)
        par_own, par_far = (
            lax.dynamic_index_in_dim(halves, s, 1, keepdims=False).reshape(rows, LANES) for s in (side, 1 - side)
        )
        states_own = chip_states(False, gated, gate_grad, par_own)
    par = jnp.concatenate([par_own, par_far])

    sk_far, hs_far, ks_far, *weighted_far = chip_states(True, gated, gate_grad, par_far)
    sk_own, hs_own, ks_own, *weighted_own = states_own

    def message_shapes(span):
        if span == top:
            return (shape(rows + (6 * modes if tree else 0), LANES, dtype=BF16),) * (WAYS - 1)
        return (shape(rows * 2 + (4 * rows // span if tree else 0), LANES, dtype=BF16),)

    def chip_sums(flip, outs, weighted, hs, ks, sk, *par):
        return call(
            functools.partial(sums_kernel, part=min(2, modes), unroll=16, flip=flip, tree=tree, **sizes),
            (() if flip and tree else (shape(4, rows // 2, LANES),)) + outs,
            [SMEM] + [VMEM] * (6 + len(par)),
            work * 3,
            scratch=(pltpu.VMEM((4, 2, rows // 2, LANES), F32),),
        )(me, *weighted, lags, hs, ks, sk, *par)

    *sums_far, tot, message = chip_sums(
        True, (pair, *message_shapes(SETS)), weighted_far, hs_far, ks_far, sk_far, par_far, sk_own, par_own
    )
    messages = [message]
    tot, weighted_own[0] = tie(tot, weighted_own[0])
    (sums_own,) = chip_sums(False, (), weighted_own, hs_own, ks_own, sk_own, par_own)

    enter, span, pair_tot, kept = tot, SETS, tot, [sums_own] if tree else []
    while span < top:
        got = exchange(messages[0], span, count)
        last = span * 2 == top
        extra = (shape(6, modes, LANES) if last else shape(4, rows // span // 2, LANES),) if tree else ()
        out = call(
            functools.partial(level_kernel, span=span, last=last, tree=tree, **sizes),
            (pair,) * (1 if last else 2) + message_shapes(span * 2) + extra,
            [SMEM] + [VMEM] * (5 if tree else 4),
            rows,
            scratch=(pltpu.VMEM((members // 2, 6, modes, LANES), F32),) if tree else (),
        )(me, tot, got, enter, par, *kept)
        if not last:
            tot, *out = out
        enter, *messages = out
        if tree:
            kept = [messages.pop()]
        if span == SETS:
            enter, hs_own, gated, gate_grad = tie(enter, hs_own, gated, gate_grad)
        span *= 2
    far = [exchange(message, hop * top, count) for hop, message in zip(HOPS, messages)]
    hs, ks, const = call(
        functools.partial(order_kernel, **sizes),
        (
            shape(2, stretches, modes * members, LANES),
            shape(2, stretches + 1, modes * members, LANES),
            shape(3, modes, members, LANES),
        ),
        [VMEM] * 5,
        work,
    )(hs_own, ks_own, hs_far, ks_far, par)
    y, z = call(functools.partial(taps_kernel, **sizes), (series, series), [SMEM] + [VMEM] * 3, work)(
        me, gated, gate_grad, par
    )
    far[0], y, hs = tie(far[0], y, hs)
    (states_in,) = call(
        functools.partial(enter_kernel, span=top, **sizes), (shape(2, 2, rows, LANES),), [SMEM] + [VMEM] * 7, rows
    )(me, enter, *far, par, sk_own, sk_far)

    scratch = (pltpu.VMEM((tokens * members, LANES), F32),) * 2
    finish = functools.partial(finish_kernel, tokens=tokens, modes=modes, members=members)
    (send_conv,) = call(functools.partial(finish, own=False), (half,), [SMEM] + [VMEM] * 6, work * 2, scratch=scratch)(
        me, y, z, hs, ks, const, states_in
    )
    got_conv = exchange(send_conv, 1, count)
    grads = (shape(tokens, channels, dtype=BF16),) * 3
    done = call(functools.partial(finish, own=True), grads, [SMEM] + [VMEM] * 9, work * 2, scratch=scratch)(
        me, y, z, hs, ks, const, states_in, key_proj, value_proj, output_grad
    )
    scale = float(tokens * count) ** (-0.5)
    extra = (*kept, *far, own) if tree else ()
    first = 5 + len(extra)
    out = call(
        functools.partial(last_kernel, tokens=tokens, modes=modes, members=members, span=top, scale=scale, tree=tree),
        grads + grads + ((shape(modes, LANES),) * 2 if tree else ()),
        [SMEM] + [VMEM] * (first + 2),
        work,
        (VMEM,) * 3 + (ANY,) * (5 if tree else 3),
        (pltpu.SemaphoreType.DMA((3, tokens // 16)),)
        + ((pltpu.SemaphoreType.DMA((2,)), pltpu.VMEM((2, modes, LANES), F32), pltpu.VMEM((WAYS, 6, modes, LANES), F32)) if tree else ()),
        {first: 0, first + 1: 1, first + 2: 2},
    )(me, got_conv, key_proj, value_proj, output_grad, *extra, *done)

    if tree:
        residue_grad, log_grad = out[6].T, out[7].T
    else:
        dims = (members, modes, LANES)

        def by_member(a):
            a = a.reshape(2, members // 2, modes, LANES)
            return jnp.where(side == 0, a, a[::-1]).transpose(1, 0, 2, 3).reshape(dims)

        h_in, k_in = by_member(states_in[0, 0]), by_member(states_in[1, 1])
        s, k = (by_member(a) for a in pair_tot)
        r, d, s_d, k_d = (by_member(jnp.stack([a, b])) for a, b in zip(sums_own, sums_far[0]))
        rate = params[:, 0]
        w = jnp.exp(-rate)
        r = r + w * h_in * k
        d = d + w * (h_in * k_d + k_in * (s_d + s)) + float(length) * jnp.exp(-rate * float(length + 1)) * h_in * k_in
        parts = jnp.stack([r, d], axis=1)
        parts = jnp.stack([jnp.where(core == 0, parts, 0.0), jnp.where(core == 1, parts, 0.0)], axis=1)
        parts = parts.reshape(groups, 2, modes, LANES).transpose(1, 2, 0, 3)
        parts = parts.reshape(2, modes, count, own_channels).transpose(2, 0, 1, 3)
        sums = lax.all_to_all(parts, "ctx", split_axis=0, concat_axis=0, tiled=True).sum(axis=0)
        root = scale * jnp.sqrt(decay_rate)
        residue_grad = root * sums[0].T
        log_grad = root * residue * (0.5 * sums[0].T - decay_rate * sums[1].T)
    return out[3], out[4], out[5], residue_grad, log_grad


def solution(mesh):
    in_specs = (P("ctx", "ch"),) * 4 + (P(("ch", "ctx"), None),) * 2
    out_specs = (P("ctx", "ch"),) * 3 + (P(("ch", "ctx"), None),) * 2
    return jax.shard_map(local, mesh=mesh, in_specs=in_specs, out_specs=out_specs, check_vma=False)
```

```python
import functools

import jax
import jax.numpy as jnp
from jax import lax
from jax.experimental import pallas as pl
from jax.experimental.pallas import tpu as pltpu
from jax.sharding import PartitionSpec as P

LANES = 128
SETS = 2
STRETCH = 8
WAYS = 4
HOPS = (3, 1, 2)
F32 = jnp.float32
BF16 = jnp.bfloat16
VMEM = pl.BlockSpec(memory_space=pltpu.VMEM)
SMEM = pl.BlockSpec(memory_space=pltpu.SMEM)
ANY = pl.BlockSpec(memory_space=pl.ANY)
HBM = pl.BlockSpec(memory_space=pltpu.HBM)


def total(terms):
    terms = list(terms)
    while len(terms) > 1:
        terms = [a + b for a, b in zip(terms[::2], terms[1::2])] + terms[len(terms) & ~1 :]
    return terms[0]


def set_columns(member, which):
    return pl.ds(pl.multiple_of((member * SETS + which) * LANES, LANES), LANES)


def gate_kernel(me_ref, q_hbm, k_hbm, v_hbm, u_hbm, own_ref, send_ref, stage_ref, sems, *, members, pieces):
    tokens = q_hbm.shape[0]
    core = me_ref[0] % SETS
    rows = tokens // pieces
    copies = []
    for piece in range(pieces):
        at = pl.ds(piece * rows, rows)
        for i, ref in enumerate((q_hbm, k_hbm, v_hbm, u_hbm)):
            copies.append(pltpu.make_async_copy(ref.at[at], stage_ref.at[i, at], sems.at[piece, i]))
            copies[-1].start()

    def body(tile, _):
        at = pl.ds(pl.multiple_of(tile * 16, 16), 16)
        for out_ref, which in ((own_ref, core), (send_ref, 1 - core)):
            for member in range(members):
                cols = set_columns(member, which)
                q, k, v, u = (stage_ref[i, at, cols].astype(F32) for i in range(4))
                out_ref[0, member, at, :] = (k * v).astype(BF16)
                out_ref[1, member, at, :] = (u * q).astype(BF16)
        return 0

    for piece in range(pieces):
        for copy in copies[piece * 4 : piece * 4 + 4]:
            copy.wait()
        lax.fori_loop(piece * rows // 16, (piece + 1) * rows // 16, body, 0)


def series_kernel(me_ref, own_ref, got_ref, x_ref, g_ref, lag_ref, *, tokens, members):
    core = me_ref[0] % SETS
    half = members // 2
    for ref, chunk in ((own_ref, core), (got_ref, 1 - core)):

        def body(tile, _):
            rows = pl.ds(pl.multiple_of(tile * 16, 16), 16)
            for member in range(members):
                for i, out_ref in enumerate((x_ref, g_ref)):
                    value = ref[i, member, rows, :].astype(F32)
                    for part in range(2):
                        start = (tile * 16 + part * 8) * members + chunk * half + member // 2
                        out_ref[member % 2, pl.ds(start, 8, stride=members), :] = value[part * 8 : part * 8 + 8]
            return 0

        lax.fori_loop(0, tokens // 16, body, 0)

    for side in range(2):

        def step(i, lags):
            x = [x_ref[side, pl.ds((i * STRETCH + t) * members, members), :] for t in range(STRETCH)]
            g = [g_ref[side, pl.ds((i * STRETCH + t) * members, members), :] for t in range(STRETCH)]
            return tuple(lags[j] + total([g[t] * x[t - j] for t in range(j, STRETCH)]) for j in range(STRETCH))

        zero = tuple(jnp.zeros((members, LANES), F32) for _ in range(STRETCH))
        lags = lax.fori_loop(0, tokens // STRETCH, step, zero)
        for j in range(STRETCH):
            lag_ref[side, j] = lags[j]


def param_rows(par_ref, param, mode, modes, members):
    return par_ref[pl.ds(param * modes + mode, members, stride=2 * modes), :]


def half_rows(par_ref, start, stride, members):
    rows = par_ref[pl.ds(start, members // 2, stride=stride), :]
    return jnp.concatenate([rows, rows], axis=0)


def chosen_half(me_ref, flip):
    side = (me_ref[0] // SETS) % 2
    return 1 - side if flip else side


def ranked(me_ref, rank, members):
    half = members // 2
    return rank % half * 2 + chosen_half(me_ref, rank >= half)


def state_kernel(me_ref, x_ref, g_ref, par_ref, sk_ref, hs_ref, ks_ref, xw_ref, gw_ref, *, tokens, modes, members, flip):
    side = chosen_half(me_ref, flip)
    half = members // 2
    w = [jnp.exp(-half_rows(par_ref, m, 2 * modes, members)) for m in range(modes)]
    stretches = tokens // STRETCH

    def step(i, carry):
        s, k = carry
        back = stretches - 1 - i
        for m in range(modes):
            hs_ref[i, m] = s[m]
        for t in range(STRETCH):
            at = pl.ds((i * STRETCH + t) * members, members)
            at_back = pl.ds((back * STRETCH + STRETCH - 1 - t) * members, members)
            x, g = x_ref[side, at, :], g_ref[side, at_back, :]
            xw_ref[at, :] = x * float(STRETCH - 1 - t)
            gw_ref[at_back, :] = g * float(STRETCH - 1 - t)
            s = tuple(w[m] * s[m] + x for m in range(modes))
            k = tuple(w[m] * k[m] + g for m in range(modes))
        for m in range(modes):
            ks_ref[back, m] = k[m]
        return s, k

    zero = tuple(jnp.zeros((members, LANES), F32) for _ in range(modes))
    for m in range(modes):
        ks_ref[stretches, m] = zero[m]
    s, k = lax.fori_loop(0, stretches, step, (zero, zero), unroll=2)
    for m in range(modes):
        at = pl.ds(m, half, stride=modes)
        for i, value in enumerate((s[m], k[m])):
            sk_ref[i, 0, at, :] = value[:half]
            sk_ref[i, 1, at, :] = value[half:]


def taps_kernel(me_ref, x_ref, g_ref, par_ref, y_ref, z_ref, *, tokens, modes, members):
    half = members // 2
    for flip in (0, 1):
        side = chosen_half(me_ref, flip)
        start = flip * half * 2 * modes
        rate = [half_rows(par_ref, start + m, 2 * modes, members) for m in range(modes)]
        w = [jnp.exp(-rate[m]) for m in range(modes)]
        power = [half_rows(par_ref, start + modes + m, 2 * modes, members) * jnp.sqrt(rate[m]) for m in range(modes)]
        taps = []
        for j in range(STRETCH):
            taps.append(total(power))
            power = [power[m] * w[m] for m in range(modes)]

        def within(i, _):
            at = [pl.ds((i * STRETCH + t) * members, members) for t in range(STRETCH)]
            x = [x_ref[side, at[t], :] for t in range(STRETCH)]
            g = [g_ref[side, at[t], :] for t in range(STRETCH)]
            for t in range(STRETCH):
                y = total([taps[j] * x[t - j] for j in range(t + 1)])
                z = total([taps[j] * g[t + j] for j in range(STRETCH - t)])
                for chunk in range(2):
                    to = pl.ds((chunk * tokens + i * STRETCH + t) * members + flip * half, half)
                    y_ref[to, :] = y[chunk * half : (chunk + 1) * half]
                    z_ref[to, :] = z[chunk * half : (chunk + 1) * half]
            return 0

        lax.fori_loop(0, tokens // STRETCH, within, 0, unroll=2)


def order_kernel(hs_own, ks_own, hs_far, ks_far, par_ref, hs_ref, ks_ref, const_ref, *, tokens, modes, members):
    half = members // 2
    for m in range(modes):
        rate = param_rows(par_ref, 0, m, modes, members)
        w = jnp.exp(-rate)
        const_ref[0, m] = w
        const_ref[1, m] = jnp.exp(rate * -float(STRETCH))
        const_ref[2, m] = param_rows(par_ref, 1, m, modes, members) * jnp.sqrt(rate) * w
    amp = []
    for flip in range(2):
        start = flip * half * 2 * modes
        rates = [half_rows(par_ref, start + m, 2 * modes, members) for m in range(modes)]
        residues = [half_rows(par_ref, start + modes + m, 2 * modes, members) for m in range(modes)]
        amp.append([residues[m] * jnp.sqrt(rates[m]) * jnp.exp(-rates[m]) for m in range(modes)])
    for src, out, count in ((0, hs_ref, tokens // STRETCH), (1, ks_ref, tokens // STRETCH + 1)):

        def body(i, _):
            for flip, ref in ((0, (hs_own, ks_own)[src]), (1, (hs_far, ks_far)[src])):
                for m in range(modes):
                    value = ref[i, m] * amp[flip][m]
                    for chunk in range(2):
                        out[chunk, i, pl.ds(m * members + flip * half, half), :] = value[chunk * half : (chunk + 1) * half]
            return 0

        lax.fori_loop(0, count, body, 0)


def flags(bit):
    bit = bit.astype(F32)
    return bit, 1.0 - bit


def put_states(refs, me, span, at, at_k, s, k, last):
    if last:
        place = me // span
        for hop, ref in zip(HOPS, refs):
            earlier, later = flags((place ^ hop) < place)
            ref[at, :] = (earlier * k + later * s).astype(BF16)
    else:
        refs[0][at, :] = s.astype(BF16)
        refs[0][at_k, :] = k.astype(BF16)


def blocks(rank, modes, members):
    return pl.ds(rank * modes, modes), pl.ds((members + rank) * modes, modes)


def sums_kernel(me_ref, x_ref, g_ref, lag_ref, hs_ref, ks_ref, sk_ref, par_ref, *refs, tokens, modes, members, part, unroll, flip, tree):
    if flip:
        sk_own, par_own, *sums_ref, tot_ref, message_ref, work_ref = refs
    else:
        *sums_ref, work_ref = refs
    side = chosen_half(me_ref, flip)
    half = members // 2
    stretches = tokens // STRETCH
    width = float(STRETCH)
    zero = jnp.zeros((members, LANES), F32)
    for first in range(0, modes, part):
        rate = [half_rows(par_ref, first + m, 2 * modes, members) for m in range(part)]
        w = [jnp.exp(-rate[m]) for m in range(part)]
        fade = [jnp.exp(rate[m] * -width) for m in range(part)]

        def step(i, carry):
            back = stretches - 1 - i
            x = [x_ref[pl.ds((i * STRETCH + t) * members, members), :] for t in range(STRETCH - 1)]
            g = [g_ref[pl.ds((back * STRETCH + t) * members, members), :] for t in range(STRETCH)]
            out = []
            for m in range(part):
                same, next_, b_k, b_s, sd, kd = carry[m]
                h, k = hs_ref[i, first + m], ks_ref[i, first + m]
                h_back = hs_ref[back, first + m]
                k_after, k_back = ks_ref[i + 1, first + m], ks_ref[back + 1, first + m]
                s_own = x[0]
                for t in range(1, STRETCH - 1):
                    s_own = s_own * w[m] + x[t]
                s_own = s_own * w[m]
                k_own = g[STRETCH - 1]
                for t in range(STRETCH - 2, 0, -1):
                    k_own = k_own * w[m] + g[t]
                k_own = k_own * w[m]
                out.append(
                    (
                        same + h * k,
                        next_ + h * k_after,
                        b_k + h_back * k_own,
                        b_s + k_after * s_own,
                        fade[m] * (sd + width * h) + s_own,
                        fade[m] * (kd + width * k_back) + k_own,
                    )
                )
            return tuple(out)

        sums = lax.fori_loop(0, stretches, step, ((zero,) * 6,) * part, unroll=unroll)
        lags = [lag_ref[side, j] for j in range(STRETCH)]
        for m in range(part):
            same, next_, b_k, b_s, sd, kd = sums[m]
            r, d = lags[STRETCH - 1], (width - 1.0) * lags[STRETCH - 1]
            for j in range(STRETCH - 2, -1, -1):
                r = r * w[m] + lags[j]
                d = d * w[m] + float(j) * lags[j]
            r = r + w[m] * (same - fade[m] * next_)
            d = d + w[m] * (b_k + b_s + same + (width - 1.0) * (fade[m] * next_))
            at = pl.ds(first + m, half, stride=modes)
            for i, value in enumerate((r, d, sd, kd)):
                work_ref[i, 0, at, :] = value[:half]
                work_ref[i, 1, at, :] = value[half:]

    me = me_ref[0]
    rows = members * modes
    for z in range(half):
        at = pl.ds(z * modes, modes)
        left, right = (tuple(work_ref[i, c, at, :] for i in range(4)) + (sk_ref[0, c, at, :], sk_ref[1, c, at, :]) for c in range(2))
        rate = par_ref[pl.ds(z * 2 * modes, modes), :]
        for i, value in enumerate(join(rate, left, right, float(tokens))):
            for ref in sums_ref:
                ref[i, at, :] = value
            if flip and tree:
                message_ref[pl.ds(rows * 2 + (i * half + z) * modes, modes), :] = value.astype(BF16)
        if flip:
            for ref, rank, par in ((sk_ref, half + z, par_ref), (sk_own, z, par_own)):
                fade = jnp.exp(par[pl.ds(z * 2 * modes, modes), :] * -float(tokens))
                s = fade * ref[0, 0, at, :] + ref[0, 1, at, :]
                k = ref[1, 0, at, :] + fade * ref[1, 1, at, :]
                to, to_k = blocks(rank, modes, members)
                tot_ref[0, to, :] = s
                tot_ref[1, to, :] = k
                put_states([message_ref], me, SETS, to, to_k, s, k, False)


def far_kernel(me_ref, x_ref, g_ref, lag_ref, par_ref, sk_own, par_own, sk_ref, hs_ref, ks_ref, *refs, tokens, modes, members, part, unroll, tree):
    *outs, xw_ref, gw_ref, work_ref = refs
    sizes = dict(tokens=tokens, modes=modes, members=members)
    state_kernel(me_ref, x_ref, g_ref, par_ref, sk_ref, hs_ref, ks_ref, xw_ref, gw_ref, flip=True, **sizes)
    sums_kernel(
        me_ref, xw_ref, gw_ref, lag_ref, hs_ref, ks_ref, sk_ref, par_ref, sk_own, par_own, *outs, work_ref,
        part=part, unroll=unroll, flip=True, tree=tree, **sizes,
    )


def join(rate, left, right, length):
    r_a, d_a, sd_a, kd_a, s_a, k_a = left
    r_b, d_b, sd_b, kd_b, s_b, k_b = right
    w = jnp.exp(-rate)
    fade = jnp.exp(rate * -length)
    r = r_a + r_b + w * (s_a * k_b)
    d = d_a + d_b + w * (s_a * kd_b + (sd_a + s_a) * k_b)
    sd = fade * (sd_a + length * s_a) + sd_b
    kd = kd_a + fade * (kd_b + length * k_b)
    return r, d, sd, kd


def level_kernel(
    me_ref, tot_ref, got_ref, enter_ref, par_ref, *refs, tokens, modes, members, span, last, tree
):
    refs = list(refs)
    if tree:
        kept_ref, work_ref, keep_ref = refs.pop(0), refs.pop(), refs.pop()
    out_ref = None if last else refs.pop(0)
    new_ref, *messages = refs
    me = me_ref[0]
    second = (me // span) % 2
    earlier, later = flags(second == 1)
    inside = (me // 2) % (span // 2) * 2
    gap = earlier * inside.astype(F32) + later * (span - 2 - inside).astype(F32)
    rows = members * modes
    half = members // 2

    def received(rank):
        at, at_k = blocks((rank + half) % members if span == 2 else rank, modes, members)
        return got_ref[at, :].astype(F32), got_ref[at_k, :].astype(F32)

    sums = []
    for rank in range(members):
        at, at_k = blocks(rank, modes, members)
        rate = par_ref[pl.ds(rank * 2 * modes, modes), :]
        far = jnp.exp(rate * -float(tokens * span))
        weight = jnp.exp(rate * (gap * -float(tokens)))
        s, k = tot_ref[0, at, :], tot_ref[1, at, :]
        gs, gk = received(rank)
        s_sum = earlier * (far * gs + s) + later * (far * s + gs)
        k_sum = earlier * (gk + far * k) + later * (k + far * gk)
        if not last:
            out_ref[0, at, :] = s_sum
            out_ref[1, at, :] = k_sum
        before = earlier * (weight * gs)
        after = later * (weight * gk)
        if span > 2:
            before += enter_ref[0, at, :]
            after += enter_ref[1, at, :]
        new_ref[0, at, :] = before
        new_ref[1, at, :] = after
        put_states(messages, me, span * 2, at, at_k, s_sum, k_sum, last)
        if tree and span == 2 and rank < half:
            block = pl.ds(rank * modes, modes)
            mine = tuple(kept_ref[i, block, :] for i in range(4)) + (s, k)
            theirs = tuple(got_ref[pl.ds(rows * 2 + (i * half + rank) * modes, modes), :].astype(F32) for i in range(4)) + (gs, gk)
            left = tuple(earlier * b + later * a for a, b in zip(mine, theirs))
            right = tuple(earlier * a + later * b for a, b in zip(mine, theirs))
            for i, value in enumerate(join(rate, left, right, float(tokens * span)) + (s_sum, k_sum)):
                work_ref[rank, i] = value
    if tree:
        place = me // (span * 2)
        keep_ref[...] = work_ref[place]
        for hop, ref in zip(HOPS, messages):
            for i in range(6):
                ref[pl.ds(rows + i * modes, modes), :] = work_ref[place ^ hop, i].astype(BF16)


def enter_kernel(me_ref, enter_ref, a_ref, b_ref, c_ref, par_ref, sk_own, sk_far, in_ref, *, tokens, modes, members, span):
    me = me_ref[0]
    place = me // span
    inside = (me // 2) % (span // 2) * 2
    partners = []
    for hop, ref in zip(HOPS, (a_ref, b_ref, c_ref)):
        partner = place ^ hop
        earlier, later = flags(partner < place)
        gap = earlier * (span * (place - partner - 1) + inside).astype(F32)
        gap += later * (span * (partner - place - 1) + (span - 2 - inside)).astype(F32)
        partners.append((ref, earlier, later, gap * -float(tokens)))
    for ref, flip in ((sk_own, 0), (sk_far, 1)):
        for z in range(members // 2):
            src = pl.ds(z * modes, modes)
            rank = flip * (members // 2) + z
            at, _ = blocks(rank, modes, members)
            rate = par_ref[pl.ds(rank * 2 * modes, modes), :]
            before, after = enter_ref[0, at, :], enter_ref[1, at, :]
            for got_ref, earlier, later, gap in partners:
                value = jnp.exp(rate * gap) * got_ref[at, :].astype(F32)
                before += earlier * value
                after += later * value
            fade = jnp.exp(rate * -float(tokens))
            in_ref[0, 0, at, :] = before
            in_ref[0, 1, at, :] = ref[1, 1, src, :] + fade * after
            in_ref[1, 0, at, :] = ref[0, 0, src, :] + fade * before
            in_ref[1, 1, at, :] = after


def finish_kernel(me_ref, y_ref, z_ref, hs_ref, ks_ref, const_ref, in_ref, *refs, tokens, modes, members, own):
    if own:
        k_ref, v_ref, u_ref, dq_ref, dk_ref, dv_ref, yo_ref, zo_ref = refs
    else:
        send_ref, yo_ref, zo_ref = refs
    core = me_ref[0] % SETS
    chunk = core if own else 1 - core
    stretches = tokens // STRETCH
    base = chunk * stretches
    w, fade, amp = ([const_ref[i, m] for m in range(modes)] for i in range(3))
    h = tuple(amp[m] * in_ref[chunk, 0, pl.ds(m, members, stride=modes), :] for m in range(modes))
    k = tuple(amp[m] * in_ref[chunk, 1, pl.ds(m, members, stride=modes), :] for m in range(modes))

    def forward(i, h):
        p = [h[m] + hs_ref[chunk, i, pl.ds(m * members, members), :] for m in range(modes)]
        for t in range(STRETCH):
            at = pl.ds((i * STRETCH + t) * members, members)
            yo_ref[at, :] = y_ref[pl.ds(((base + i) * STRETCH + t) * members, members), :] + total(p)
            if t < STRETCH - 1:
                p = [w[m] * p[m] for m in range(modes)]
        return tuple(fade[m] * h[m] for m in range(modes))

    def backward(i, k):
        back = stretches - 1 - i
        q = [k[m] + ks_ref[chunk, back + 1, pl.ds(m * members, members), :] for m in range(modes)]
        for t in range(STRETCH):
            row = back * STRETCH + STRETCH - 1 - t
            zo_ref[pl.ds(row * members, members), :] = z_ref[pl.ds((base * STRETCH + row) * members, members), :] + total(q)
            if t < STRETCH - 1:
                q = [w[m] * q[m] for m in range(modes)]
        return tuple(fade[m] * k[m] for m in range(modes))

    def put(source, store):
        for tile in range(tokens // 16):
            rows = pl.ds(tile * 16, 16)
            for member in range(members):
                halves = [pl.ds((tile * 16 + half * 8) * members + member, 8, stride=members) for half in range(2)]
                store(rows, member, jnp.concatenate([source[at, :] for at in halves], axis=0).astype(BF16))

    def store_y(rows, member, value):
        if own:
            cols = set_columns(ranked(me_ref, member, members), core)
            dq_ref[rows, cols] = (u_ref[rows, cols].astype(F32) * value.astype(F32)).astype(BF16)
        else:
            send_ref[0, member, rows, :] = value

    def store_z(rows, member, value):
        if own:
            cols = set_columns(ranked(me_ref, member, members), core)
            value = value.astype(F32)
            dk_ref[rows, cols] = (value * v_ref[rows, cols].astype(F32)).astype(BF16)
            dv_ref[rows, cols] = (value * k_ref[rows, cols].astype(F32)).astype(BF16)
        else:
            send_ref[1, member, rows, :] = value

    lax.fori_loop(0, stretches, forward, h, unroll=4)
    put(yo_ref, store_y)
    lax.fori_loop(0, stretches, backward, k, unroll=4)
    put(zo_ref, store_z)


def first_finish_kernel(
    me_ref, y_ref, z_ref, hs_ref, ks_ref, const_ref, enter_ref, a_ref, b_ref, c_ref, par_ref, sk_own, sk_far, send_ref, in_ref, *scratch,
    tokens, modes, members, span,
):
    sizes = dict(tokens=tokens, modes=modes, members=members)
    enter_kernel(me_ref, enter_ref, a_ref, b_ref, c_ref, par_ref, sk_own, sk_far, in_ref, span=span, **sizes)
    finish_kernel(me_ref, y_ref, z_ref, hs_ref, ks_ref, const_ref, in_ref, send_ref, *scratch, own=False, **sizes)


def last_kernel(me_ref, got_ref, k_ref, v_ref, u_ref, *refs, tokens, modes, members, span, scale, tree):
    refs = list(refs)
    if tree:
        kept_ref, a_ref, b_ref, c_ref, own_ref = refs[:5]
        refs = refs[5:]
    dq_ref, dk_ref, dv_ref, dq_hbm, dk_hbm, dv_hbm = refs[3:9]
    me = me_ref[0]
    core = me % SETS
    copies = []
    if tree:
        r_hbm, log_hbm, sems, par_sems, out_ref, group_ref = refs[9:]
        place = me // span
        group_ref[place] = kept_ref[...]
        for hop, ref in zip(HOPS, (a_ref, b_ref, c_ref)):
            for i in range(6):
                group_ref[place ^ hop, i] = ref[pl.ds((members + i) * modes, modes), :].astype(F32)
        rate, residue = own_ref[0], own_ref[1]
        w = jnp.exp(-rate)
        width = float(tokens * span)
        fade = jnp.exp(rate * -width)
        r, d, sd, _, s, _ = (group_ref[0, i] for i in range(6))
        for z in range(1, WAYS):
            r_b, d_b, sd_b, kd_b, s_b, k_b = (group_ref[z, i] for i in range(6))
            r = r + r_b + w * (s * k_b)
            d = d + d_b + w * (s * kd_b + (sd + s) * k_b)
            sd = fade * (sd + width * s) + sd_b
            s = fade * s + s_b
        root = jnp.sqrt(rate) * scale
        out_ref[0] = root * r
        out_ref[1] = root * residue * (0.5 * r - rate * d)
        for i, ref in enumerate((r_hbm, log_hbm)):
            copies.append(pltpu.make_async_copy(out_ref.at[i], ref, par_sems.at[i]))
            copies[-1].start()
    else:
        (sems,) = refs[9:]
    for tile in range(tokens // 16):
        rows = pl.ds(tile * 16, 16)
        for member in range(members):
            cols = set_columns(ranked(me_ref, member, members), 1 - core)
            y = got_ref[0, member, rows, :].astype(F32)
            z = got_ref[1, member, rows, :].astype(F32)
            dq_ref[rows, cols] = (u_ref[rows, cols].astype(F32) * y).astype(BF16)
            dk_ref[rows, cols] = (z * v_ref[rows, cols].astype(F32)).astype(BF16)
            dv_ref[rows, cols] = (z * k_ref[rows, cols].astype(F32)).astype(BF16)
        for i, (ref, out) in enumerate(((dq_ref, dq_hbm), (dk_ref, dk_hbm), (dv_ref, dv_hbm))):
            copies.append(pltpu.make_async_copy(ref.at[rows], out.at[rows], sems.at[i, tile]))
            copies[-1].start()
    for copy in copies:
        copy.wait()


def call(body, out_shape, in_specs, flops, out_specs=None, scratch=(), aliases=None):
    return pl.pallas_call(
        body,
        out_shape=out_shape,
        in_specs=in_specs,
        out_specs=jax.tree.map(lambda _: VMEM, out_shape) if out_specs is None else out_specs,
        scratch_shapes=scratch,
        input_output_aliases=aliases or {},
        compiler_params=pltpu.CompilerParams(vmem_limit_bytes=16 * 1024 * 1024),
        cost_estimate=pl.CostEstimate(flops=flops, bytes_accessed=1024 * 1024, transcendentals=0),
    )


def exchange(value, distance, count):
    return lax.ppermute(value, "ctx", [(i, i ^ distance) for i in range(count)])


def tie(*values):
    return lax.optimization_barrier(values)


def local(query_proj, key_proj, value_proj, output_grad, residue, decay_rate):
    tokens, channels = query_proj.shape
    own_channels, modes = residue.shape
    count = lax.axis_size("ctx")
    groups = channels // LANES
    members = groups // SETS
    rows = members * modes
    length = tokens * SETS
    top = count // WAYS
    tree = groups == count == SETS * 2 * WAYS and own_channels == LANES
    work = tokens * channels * modes
    index = lax.axis_index("ctx")
    core = index % SETS
    side = (index // SETS) % 2
    me = index.astype(jnp.int32).reshape(1)

    def shape(*dims, dtype=F32):
        return jax.ShapeDtypeStruct(dims, dtype)

    half = shape(2, members, tokens, LANES, dtype=BF16)
    series = shape(length * members, LANES)
    half_series = shape(tokens * members, LANES)
    pieces = 4
    pair = shape(2, rows, LANES)
    stretches = tokens // STRETCH
    sizes = dict(tokens=tokens, modes=modes, members=members)

    states = shape(2, 2, rows // 2, LANES), shape(stretches, modes, members, LANES), shape(stretches + 1, modes, members, LANES)

    def chip_states(gated, gate_grad, par):
        out = call(
            functools.partial(state_kernel, flip=False, **sizes), states + (half_series,) * 2, [SMEM] + [VMEM] * 3, work * 2
        )(me, gated, gate_grad, par)
        return list(out)

    own_gates, send_gates = call(
        functools.partial(gate_kernel, members=members, pieces=pieces),
        (half, half),
        [SMEM] + [HBM] * 4,
        work,
        scratch=(pltpu.VMEM((4, tokens, channels), BF16), pltpu.SemaphoreType.DMA((pieces, 4))),
    )(me, *(pltpu.with_memory_space_constraint(a, pltpu.HBM) for a in (query_proj, key_proj, value_proj, output_grad)))

    (own,) = tie(jnp.stack([decay_rate.T, residue.T]))
    params, axis = own, 0
    distance = count // 2
    while distance > (1 if tree else 0):
        other = exchange(params, distance, count)
        if axis == 0:
            other, own_gates, send_gates = tie(other, own_gates, send_gates)
            got_gates = exchange(send_gates, 1, count)
            gated, gate_grad, lags = call(
                functools.partial(series_kernel, tokens=tokens, members=members),
                (shape(2, tokens * members, LANES),) * 2 + (shape(2, STRETCH, members, LANES),),
                [SMEM] + [VMEM] * 2,
                work,
            )(me, own_gates, got_gates)
        if axis == 1:
            other, gated, gate_grad, lags = tie(other, gated, gate_grad, lags)
        if tree and distance == SETS:
            par_own, par_far = (a.reshape(rows, LANES) for a in (params, other))
            states_own = chip_states(gated, gate_grad, par_own)
            par_far, states_own[0] = tie(par_far, states_own[0])
            break
        upper = (index // distance) % 2 == 1
        params = jnp.stack([jnp.where(upper, other, params), jnp.where(upper, params, other)], axis=axis)
        distance //= 2
        axis += 1
    if not tree:
        params = params.reshape((count,) + own.shape).transpose(1, 2, 0, 3).reshape(2, modes, members, SETS, LANES)
        params = lax.dynamic_index_in_dim(params, core, 3, keepdims=False).transpose(2, 0, 1, 3)
        halves = params.reshape(members // 2, 2, 2, modes, LANES)
        par_own, par_far = (
            lax.dynamic_index_in_dim(halves, s, 1, keepdims=False).reshape(rows, LANES) for s in (side, 1 - side)
        )
        states_own = chip_states(gated, gate_grad, par_own)
    par = jnp.concatenate([par_own, par_far])

    sk_own, hs_own, ks_own, *weighted_own = states_own

    def message_shapes(span):
        if span == top:
            return (shape(rows + (6 * modes if tree else 0), LANES, dtype=BF16),) * (WAYS - 1)
        return (shape(rows * 2 + (4 * rows // span if tree else 0), LANES, dtype=BF16),)

    loops = dict(part=min(2, modes), unroll=16, tree=tree, **sizes)
    half_sums = shape(4, rows // 2, LANES)
    work_sums = pltpu.VMEM((4, 2, rows // 2, LANES), F32)
    weighted = pltpu.VMEM(half_series.shape, F32)
    sk_far, hs_far, ks_far, *sums_far, tot, message = call(
        functools.partial(far_kernel, **loops),
        states + (() if tree else (half_sums,)) + (pair, *message_shapes(SETS)),
        [SMEM] + [VMEM] * 6,
        work * 5,
        scratch=(weighted, weighted, work_sums),
    )(me, gated, gate_grad, lags, par_far, sk_own, par_own)
    messages = [message]
    tot, weighted_own[0] = tie(tot, weighted_own[0])
    (sums_own,) = call(
        functools.partial(sums_kernel, flip=False, **loops), (half_sums,), [SMEM] + [VMEM] * 7, work * 3, scratch=(work_sums,)
    )(me, *weighted_own, lags, hs_own, ks_own, sk_own, par_own)

    enter, span, pair_tot, kept = tot, SETS, tot, [sums_own] if tree else []
    while span < top:
        got = exchange(messages[0], span, count)
        last = span * 2 == top
        extra = (shape(6, modes, LANES) if last else shape(4, rows // span // 2, LANES),) if tree else ()
        out = call(
            functools.partial(level_kernel, span=span, last=last, tree=tree, **sizes),
            (pair,) * (1 if last else 2) + message_shapes(span * 2) + extra,
            [SMEM] + [VMEM] * (5 if tree else 4),
            rows,
            scratch=(pltpu.VMEM((members // 2, 6, modes, LANES), F32),) if tree else (),
        )(me, tot, got, enter, par, *kept)
        if not last:
            tot, *out = out
        enter, *messages = out
        if tree:
            kept = [messages.pop()]
        if span == SETS:
            enter, hs_own, gated, gate_grad = tie(enter, hs_own, gated, gate_grad)
        span *= 2
    far = [exchange(message, hop * top, count) for hop, message in zip(HOPS, messages)]
    hs, ks, const = call(
        functools.partial(order_kernel, **sizes),
        (
            shape(2, stretches, modes * members, LANES),
            shape(2, stretches + 1, modes * members, LANES),
            shape(3, modes, members, LANES),
        ),
        [VMEM] * 5,
        work,
    )(hs_own, ks_own, hs_far, ks_far, par)
    y, z = call(functools.partial(taps_kernel, **sizes), (series, series), [SMEM] + [VMEM] * 3, work)(
        me, gated, gate_grad, par
    )
    far[0], y, hs = tie(far[0], y, hs)
    scratch = (pltpu.VMEM((tokens * members, LANES), F32),) * 2
    finish = functools.partial(finish_kernel, tokens=tokens, modes=modes, members=members)
    send_conv, states_in = call(
        functools.partial(first_finish_kernel, span=top, **sizes),
        (half, shape(2, 2, rows, LANES)),
        [SMEM] + [VMEM] * 12,
        work * 2,
        scratch=scratch,
    )(me, y, z, hs, ks, const, enter, *far, par, sk_own, sk_far)
    got_conv = exchange(send_conv, 1, count)
    grads = (shape(tokens, channels, dtype=BF16),) * 3
    done = call(functools.partial(finish, own=True), grads, [SMEM] + [VMEM] * 9, work * 2, scratch=scratch)(
        me, y, z, hs, ks, const, states_in, key_proj, value_proj, output_grad
    )
    scale = float(tokens * count) ** (-0.5)
    extra = (*kept, *far, own) if tree else ()
    first = 5 + len(extra)
    out = call(
        functools.partial(last_kernel, tokens=tokens, modes=modes, members=members, span=top, scale=scale, tree=tree),
        grads + grads + ((shape(modes, LANES),) * 2 if tree else ()),
        [SMEM] + [VMEM] * (first + 2),
        work,
        (VMEM,) * 3 + (ANY,) * (5 if tree else 3),
        (pltpu.SemaphoreType.DMA((3, tokens // 16)),)
        + ((pltpu.SemaphoreType.DMA((2,)), pltpu.VMEM((2, modes, LANES), F32), pltpu.VMEM((WAYS, 6, modes, LANES), F32)) if tree else ()),
        {first: 0, first + 1: 1, first + 2: 2},
    )(me, got_conv, key_proj, value_proj, output_grad, *extra, *done)

    if tree:
        residue_grad, log_grad = out[6].T, out[7].T
    else:
        dims = (members, modes, LANES)

        def by_member(a):
            a = a.reshape(2, members // 2, modes, LANES)
            return jnp.where(side == 0, a, a[::-1]).transpose(1, 0, 2, 3).reshape(dims)

        h_in, k_in = by_member(states_in[0, 0]), by_member(states_in[1, 1])
        s, k = (by_member(a) for a in pair_tot)
        r, d, s_d, k_d = (by_member(jnp.stack([a, b])) for a, b in zip(sums_own, sums_far[0]))
        rate = params[:, 0]
        w = jnp.exp(-rate)
        r = r + w * h_in * k
        d = d + w * (h_in * k_d + k_in * (s_d + s)) + float(length) * jnp.exp(-rate * float(length + 1)) * h_in * k_in
        parts = jnp.stack([r, d], axis=1)
        parts = jnp.stack([jnp.where(core == 0, parts, 0.0), jnp.where(core == 1, parts, 0.0)], axis=1)
        parts = parts.reshape(groups, 2, modes, LANES).transpose(1, 2, 0, 3)
        parts = parts.reshape(2, modes, count, own_channels).transpose(2, 0, 1, 3)
        sums = lax.all_to_all(parts, "ctx", split_axis=0, concat_axis=0, tiled=True).sum(axis=0)
        root = scale * jnp.sqrt(decay_rate)
        residue_grad = root * sums[0].T
        log_grad = root * residue * (0.5 * sums[0].T - decay_rate * sums[1].T)
    return out[3], out[4], out[5], residue_grad, log_grad


def solution(mesh):
    in_specs = (P("ctx", "ch"),) * 4 + (P(("ch", "ctx"), None),) * 2
    out_specs = (P("ctx", "ch"),) * 3 + (P(("ch", "ctx"), None),) * 2
    return jax.shard_map(local, mesh=mesh, in_specs=in_specs, out_specs=out_specs, check_vma=False)
```

```python
import functools

import jax
import jax.numpy as jnp
from jax import lax
from jax.experimental import pallas as pl
from jax.experimental.pallas import tpu as pltpu
from jax.sharding import PartitionSpec as P

LANES = 128
SETS = 2
STRETCH = 8
WAYS = 4
HOPS = (3, 1, 2)
F32 = jnp.float32
BF16 = jnp.bfloat16
VMEM = pl.BlockSpec(memory_space=pltpu.VMEM)
SMEM = pl.BlockSpec(memory_space=pltpu.SMEM)
ANY = pl.BlockSpec(memory_space=pl.ANY)
HBM = pl.BlockSpec(memory_space=pltpu.HBM)


def total(terms):
    terms = list(terms)
    while len(terms) > 1:
        terms = [a + b for a, b in zip(terms[::2], terms[1::2])] + terms[len(terms) & ~1 :]
    return terms[0]


def set_columns(member, which):
    return pl.ds(pl.multiple_of((member * SETS + which) * LANES, LANES), LANES)


def gate_kernel(me_ref, q_hbm, k_hbm, v_hbm, u_hbm, own_ref, send_ref, stage_ref, sems, *, members, pieces):
    tokens = q_hbm.shape[0]
    core = me_ref[0] % SETS
    rows = tokens // pieces
    copies = []
    for piece in range(pieces):
        at = pl.ds(piece * rows, rows)
        for i, ref in enumerate((q_hbm, k_hbm, v_hbm, u_hbm)):
            copies.append(pltpu.make_async_copy(ref.at[at], stage_ref.at[i, at], sems.at[piece, i]))
            copies[-1].start()

    def body(tile, _):
        at = pl.ds(pl.multiple_of(tile * 16, 16), 16)
        for out_ref, which in ((own_ref, core), (send_ref, 1 - core)):
            for member in range(members):
                cols = set_columns(member, which)
                q, k, v, u = (stage_ref[i, at, cols].astype(F32) for i in range(4))
                out_ref[0, member, at, :] = (k * v).astype(BF16)
                out_ref[1, member, at, :] = (u * q).astype(BF16)
        return 0

    for piece in range(pieces):
        for copy in copies[piece * 4 : piece * 4 + 4]:
            copy.wait()
        lax.fori_loop(piece * rows // 16, (piece + 1) * rows // 16, body, 0)


def series_kernel(me_ref, own_ref, got_ref, x_ref, g_ref, lag_ref, *, tokens, members):
    core = me_ref[0] % SETS
    half = members // 2
    for ref, chunk in ((own_ref, core), (got_ref, 1 - core)):

        def body(tile, _):
            rows = pl.ds(pl.multiple_of(tile * 16, 16), 16)
            for member in range(members):
                for i, out_ref in enumerate((x_ref, g_ref)):
                    value = ref[i, member, rows, :].astype(F32)
                    for part in range(2):
                        start = (tile * 16 + part * 8) * members + chunk * half + member // 2
                        out_ref[member % 2, pl.ds(start, 8, stride=members), :] = value[part * 8 : part * 8 + 8]
            return 0

        lax.fori_loop(0, tokens // 16, body, 0)

    for side in range(2):

        def step(i, lags):
            x = [x_ref[side, pl.ds((i * STRETCH + t) * members, members), :] for t in range(STRETCH)]
            g = [g_ref[side, pl.ds((i * STRETCH + t) * members, members), :] for t in range(STRETCH)]
            return tuple(lags[j] + total([g[t] * x[t - j] for t in range(j, STRETCH)]) for j in range(STRETCH))

        zero = tuple(jnp.zeros((members, LANES), F32) for _ in range(STRETCH))
        lags = lax.fori_loop(0, tokens // STRETCH, step, zero)
        for j in range(STRETCH):
            lag_ref[side, j] = lags[j]


def param_rows(par_ref, param, mode, modes, members):
    return par_ref[pl.ds(param * modes + mode, members, stride=2 * modes), :]


def half_rows(par_ref, start, stride, members):
    rows = par_ref[pl.ds(start, members // 2, stride=stride), :]
    return jnp.concatenate([rows, rows], axis=0)


def chosen_half(me_ref, flip):
    side = (me_ref[0] // SETS) % 2
    return 1 - side if flip else side


def ranked(me_ref, rank, members):
    half = members // 2
    return rank % half * 2 + chosen_half(me_ref, rank >= half)


def state_kernel(me_ref, x_ref, g_ref, par_ref, sk_ref, hs_ref, ks_ref, xw_ref, gw_ref, *, tokens, modes, members, flip):
    side = chosen_half(me_ref, flip)
    half = members // 2
    w = [jnp.exp(-half_rows(par_ref, m, 2 * modes, members)) for m in range(modes)]
    stretches = tokens // STRETCH

    def step(i, carry):
        s, k = carry
        back = stretches - 1 - i
        for m in range(modes):
            hs_ref[i, m] = s[m]
        for t in range(STRETCH):
            at = pl.ds((i * STRETCH + t) * members, members)
            at_back = pl.ds((back * STRETCH + STRETCH - 1 - t) * members, members)
            x, g = x_ref[side, at, :], g_ref[side, at_back, :]
            xw_ref[at, :] = x * float(STRETCH - 1 - t)
            gw_ref[at_back, :] = g * float(STRETCH - 1 - t)
            s = tuple(w[m] * s[m] + x for m in range(modes))
            k = tuple(w[m] * k[m] + g for m in range(modes))
        for m in range(modes):
            ks_ref[back, m] = k[m]
        return s, k

    zero = tuple(jnp.zeros((members, LANES), F32) for _ in range(modes))
    for m in range(modes):
        ks_ref[stretches, m] = zero[m]
    s, k = lax.fori_loop(0, stretches, step, (zero, zero), unroll=2)
    for m in range(modes):
        at = pl.ds(m, half, stride=modes)
        for i, value in enumerate((s[m], k[m])):
            sk_ref[i, 0, at, :] = value[:half]
            sk_ref[i, 1, at, :] = value[half:]


def taps_kernel(me_ref, x_ref, g_ref, par_ref, y_ref, z_ref, *, tokens, modes, members):
    half = members // 2
    for flip in (0, 1):
        side = chosen_half(me_ref, flip)
        start = flip * half * 2 * modes
        rate = [half_rows(par_ref, start + m, 2 * modes, members) for m in range(modes)]
        w = [jnp.exp(-rate[m]) for m in range(modes)]
        power = [half_rows(par_ref, start + modes + m, 2 * modes, members) * jnp.sqrt(rate[m]) for m in range(modes)]
        taps = []
        for j in range(STRETCH):
            taps.append(total(power))
            power = [power[m] * w[m] for m in range(modes)]

        def within(i, _):
            at = [pl.ds((i * STRETCH + t) * members, members) for t in range(STRETCH)]
            x = [x_ref[side, at[t], :] for t in range(STRETCH)]
            g = [g_ref[side, at[t], :] for t in range(STRETCH)]
            for t in range(STRETCH):
                y = total([taps[j] * x[t - j] for j in range(t + 1)])
                z = total([taps[j] * g[t + j] for j in range(STRETCH - t)])
                for chunk in range(2):
                    to = pl.ds((chunk * tokens + i * STRETCH + t) * members + flip * half, half)
                    y_ref[to, :] = y[chunk * half : (chunk + 1) * half]
                    z_ref[to, :] = z[chunk * half : (chunk + 1) * half]
            return 0

        lax.fori_loop(0, tokens // STRETCH, within, 0, unroll=2)


def order_kernel(hs_own, ks_own, hs_far, ks_far, par_ref, hs_ref, ks_ref, const_ref, *, tokens, modes, members):
    half = members // 2
    for m in range(modes):
        rate = param_rows(par_ref, 0, m, modes, members)
        w = jnp.exp(-rate)
        const_ref[0, m] = w
        const_ref[1, m] = jnp.exp(rate * -float(STRETCH))
        const_ref[2, m] = param_rows(par_ref, 1, m, modes, members) * jnp.sqrt(rate) * w
    amp = []
    for flip in range(2):
        start = flip * half * 2 * modes
        rates = [half_rows(par_ref, start + m, 2 * modes, members) for m in range(modes)]
        residues = [half_rows(par_ref, start + modes + m, 2 * modes, members) for m in range(modes)]
        amp.append([residues[m] * jnp.sqrt(rates[m]) * jnp.exp(-rates[m]) for m in range(modes)])
    for src, out, count in ((0, hs_ref, tokens // STRETCH), (1, ks_ref, tokens // STRETCH + 1)):

        def body(i, _):
            for flip, ref in ((0, (hs_own, ks_own)[src]), (1, (hs_far, ks_far)[src])):
                for m in range(modes):
                    value = ref[i, m] * amp[flip][m]
                    for chunk in range(2):
                        out[chunk, i, pl.ds(m * members + flip * half, half), :] = value[chunk * half : (chunk + 1) * half]
            return 0

        lax.fori_loop(0, count, body, 0)


def flags(bit):
    bit = bit.astype(F32)
    return bit, 1.0 - bit


def put_states(refs, me, span, at, at_k, s, k, last):
    if last:
        place = me // span
        for hop, ref in zip(HOPS, refs):
            earlier, later = flags((place ^ hop) < place)
            ref[at, :] = (earlier * k + later * s).astype(BF16)
    else:
        refs[0][at, :] = s.astype(BF16)
        refs[0][at_k, :] = k.astype(BF16)


def blocks(rank, modes, members):
    return pl.ds(rank * modes, modes), pl.ds((members + rank) * modes, modes)


def sums_kernel(me_ref, x_ref, g_ref, lag_ref, hs_ref, ks_ref, sk_ref, par_ref, *refs, tokens, modes, members, part, unroll, flip, tree):
    if flip:
        sk_own, par_own, *sums_ref, tot_ref, message_ref, work_ref = refs
    else:
        *sums_ref, work_ref = refs
    side = chosen_half(me_ref, flip)
    half = members // 2
    stretches = tokens // STRETCH
    width = float(STRETCH)
    zero = jnp.zeros((members, LANES), F32)
    for first in range(0, modes, part):
        rate = [half_rows(par_ref, first + m, 2 * modes, members) for m in range(part)]
        w = [jnp.exp(-rate[m]) for m in range(part)]
        fade = [jnp.exp(rate[m] * -width) for m in range(part)]

        def step(i, carry):
            back = stretches - 1 - i
            x = [x_ref[pl.ds((i * STRETCH + t) * members, members), :] for t in range(STRETCH - 1)]
            g = [g_ref[pl.ds((back * STRETCH + t) * members, members), :] for t in range(STRETCH)]
            out = []
            for m in range(part):
                same, next_, b_k, b_s, sd, kd = carry[m]
                h, k = hs_ref[i, first + m], ks_ref[i, first + m]
                h_back = hs_ref[back, first + m]
                k_after, k_back = ks_ref[i + 1, first + m], ks_ref[back + 1, first + m]
                s_own = x[0]
                for t in range(1, STRETCH - 1):
                    s_own = s_own * w[m] + x[t]
                s_own = s_own * w[m]
                k_own = g[STRETCH - 1]
                for t in range(STRETCH - 2, 0, -1):
                    k_own = k_own * w[m] + g[t]
                k_own = k_own * w[m]
                out.append(
                    (
                        same + h * k,
                        next_ + h * k_after,
                        b_k + h_back * k_own,
                        b_s + k_after * s_own,
                        fade[m] * (sd + width * h) + s_own,
                        fade[m] * (kd + width * k_back) + k_own,
                    )
                )
            return tuple(out)

        sums = lax.fori_loop(0, stretches, step, ((zero,) * 6,) * part, unroll=unroll)
        lags = [lag_ref[side, j] for j in range(STRETCH)]
        for m in range(part):
            same, next_, b_k, b_s, sd, kd = sums[m]
            r, d = lags[STRETCH - 1], (width - 1.0) * lags[STRETCH - 1]
            for j in range(STRETCH - 2, -1, -1):
                r = r * w[m] + lags[j]
                d = d * w[m] + float(j) * lags[j]
            r = r + w[m] * (same - fade[m] * next_)
            d = d + w[m] * (b_k + b_s + same + (width - 1.0) * (fade[m] * next_))
            at = pl.ds(first + m, half, stride=modes)
            for i, value in enumerate((r, d, sd, kd)):
                work_ref[i, 0, at, :] = value[:half]
                work_ref[i, 1, at, :] = value[half:]

    me = me_ref[0]
    rows = members * modes
    for z in range(half):
        at = pl.ds(z * modes, modes)
        left, right = (tuple(work_ref[i, c, at, :] for i in range(4)) + (sk_ref[0, c, at, :], sk_ref[1, c, at, :]) for c in range(2))
        rate = par_ref[pl.ds(z * 2 * modes, modes), :]
        for i, value in enumerate(join(rate, left, right, float(tokens))):
            for ref in sums_ref:
                ref[i, at, :] = value
            if flip and tree:
                message_ref[pl.ds(rows * 2 + (i * half + z) * modes, modes), :] = value.astype(BF16)
        if flip:
            for ref, rank, par in ((sk_ref, half + z, par_ref), (sk_own, z, par_own)):
                fade = jnp.exp(par[pl.ds(z * 2 * modes, modes), :] * -float(tokens))
                s = fade * ref[0, 0, at, :] + ref[0, 1, at, :]
                k = ref[1, 0, at, :] + fade * ref[1, 1, at, :]
                to, to_k = blocks(rank, modes, members)
                tot_ref[0, to, :] = s
                tot_ref[1, to, :] = k
                put_states([message_ref], me, SETS, to, to_k, s, k, False)


def far_kernel(me_ref, x_ref, g_ref, lag_ref, par_ref, sk_own, par_own, sk_ref, hs_ref, ks_ref, *refs, tokens, modes, members, part, unroll, tree):
    *outs, xw_ref, gw_ref, work_ref = refs
    sizes = dict(tokens=tokens, modes=modes, members=members)
    state_kernel(me_ref, x_ref, g_ref, par_ref, sk_ref, hs_ref, ks_ref, xw_ref, gw_ref, flip=True, **sizes)
    sums_kernel(
        me_ref, xw_ref, gw_ref, lag_ref, hs_ref, ks_ref, sk_ref, par_ref, sk_own, par_own, *outs, work_ref,
        part=part, unroll=unroll, flip=True, tree=tree, **sizes,
    )


def join(rate, left, right, length):
    r_a, d_a, sd_a, kd_a, s_a, k_a = left
    r_b, d_b, sd_b, kd_b, s_b, k_b = right
    w = jnp.exp(-rate)
    fade = jnp.exp(rate * -length)
    r = r_a + r_b + w * (s_a * k_b)
    d = d_a + d_b + w * (s_a * kd_b + (sd_a + s_a) * k_b)
    sd = fade * (sd_a + length * s_a) + sd_b
    kd = kd_a + fade * (kd_b + length * k_b)
    return r, d, sd, kd


def level_kernel(
    me_ref, tot_ref, got_ref, enter_ref, par_ref, *refs, tokens, modes, members, span, last, tree
):
    refs = list(refs)
    if tree:
        kept_ref, work_ref, keep_ref = refs.pop(0), refs.pop(), refs.pop()
    out_ref = None if last else refs.pop(0)
    new_ref, *messages = refs
    me = me_ref[0]
    second = (me // span) % 2
    earlier, later = flags(second == 1)
    inside = (me // 2) % (span // 2) * 2
    gap = earlier * inside.astype(F32) + later * (span - 2 - inside).astype(F32)
    rows = members * modes
    half = members // 2

    def received(rank):
        at, at_k = blocks((rank + half) % members if span == 2 else rank, modes, members)
        return got_ref[at, :].astype(F32), got_ref[at_k, :].astype(F32)

    sums = []
    for rank in range(members):
        at, at_k = blocks(rank, modes, members)
        rate = par_ref[pl.ds(rank * 2 * modes, modes), :]
        far = jnp.exp(rate * -float(tokens * span))
        weight = jnp.exp(rate * (gap * -float(tokens)))
        s, k = tot_ref[0, at, :], tot_ref[1, at, :]
        gs, gk = received(rank)
        s_sum = earlier * (far * gs + s) + later * (far * s + gs)
        k_sum = earlier * (gk + far * k) + later * (k + far * gk)
        if not last:
            out_ref[0, at, :] = s_sum
            out_ref[1, at, :] = k_sum
        before = earlier * (weight * gs)
        after = later * (weight * gk)
        if span > 2:
            before += enter_ref[0, at, :]
            after += enter_ref[1, at, :]
        new_ref[0, at, :] = before
        new_ref[1, at, :] = after
        put_states(messages, me, span * 2, at, at_k, s_sum, k_sum, last)
        if tree and span == 2 and rank < half:
            block = pl.ds(rank * modes, modes)
            mine = tuple(kept_ref[i, block, :] for i in range(4)) + (s, k)
            theirs = tuple(got_ref[pl.ds(rows * 2 + (i * half + rank) * modes, modes), :].astype(F32) for i in range(4)) + (gs, gk)
            left = tuple(earlier * b + later * a for a, b in zip(mine, theirs))
            right = tuple(earlier * a + later * b for a, b in zip(mine, theirs))
            for i, value in enumerate(join(rate, left, right, float(tokens * span)) + (s_sum, k_sum)):
                work_ref[rank, i] = value
    if tree:
        place = me // (span * 2)
        keep_ref[...] = work_ref[place]
        for hop, ref in zip(HOPS, messages):
            for i in range(6):
                ref[pl.ds(rows + i * modes, modes), :] = work_ref[place ^ hop, i].astype(BF16)


def enter_kernel(me_ref, enter_ref, a_ref, b_ref, c_ref, par_ref, sk_own, sk_far, in_ref, *, tokens, modes, members, span):
    me = me_ref[0]
    place = me // span
    inside = (me // 2) % (span // 2) * 2
    partners = []
    for hop, ref in zip(HOPS, (a_ref, b_ref, c_ref)):
        partner = place ^ hop
        earlier, later = flags(partner < place)
        gap = earlier * (span * (place - partner - 1) + inside).astype(F32)
        gap += later * (span * (partner - place - 1) + (span - 2 - inside)).astype(F32)
        partners.append((ref, earlier, later, gap * -float(tokens)))
    for ref, flip in ((sk_own, 0), (sk_far, 1)):
        for z in range(members // 2):
            src = pl.ds(z * modes, modes)
            rank = flip * (members // 2) + z
            at, _ = blocks(rank, modes, members)
            rate = par_ref[pl.ds(rank * 2 * modes, modes), :]
            before, after = enter_ref[0, at, :], enter_ref[1, at, :]
            for got_ref, earlier, later, gap in partners:
                value = jnp.exp(rate * gap) * got_ref[at, :].astype(F32)
                before += earlier * value
                after += later * value
            fade = jnp.exp(rate * -float(tokens))
            in_ref[0, 0, at, :] = before
            in_ref[0, 1, at, :] = ref[1, 1, src, :] + fade * after
            in_ref[1, 0, at, :] = ref[0, 0, src, :] + fade * before
            in_ref[1, 1, at, :] = after


def finish_kernel(me_ref, y_ref, z_ref, hs_ref, ks_ref, const_ref, in_ref, *refs, tokens, modes, members, own):
    if own:
        k_ref, v_ref, u_ref, dq_ref, dk_ref, dv_ref, yo_ref, zo_ref = refs
    else:
        send_ref, yo_ref, zo_ref = refs
    core = me_ref[0] % SETS
    chunk = core if own else 1 - core
    stretches = tokens // STRETCH
    base = chunk * stretches
    w, fade, amp = ([const_ref[i, m] for m in range(modes)] for i in range(3))
    h = tuple(amp[m] * in_ref[chunk, 0, pl.ds(m, members, stride=modes), :] for m in range(modes))
    k = tuple(amp[m] * in_ref[chunk, 1, pl.ds(m, members, stride=modes), :] for m in range(modes))

    def forward(i, h):
        p = [h[m] + hs_ref[chunk, i, pl.ds(m * members, members), :] for m in range(modes)]
        for t in range(STRETCH):
            at = pl.ds((i * STRETCH + t) * members, members)
            yo_ref[at, :] = y_ref[pl.ds(((base + i) * STRETCH + t) * members, members), :] + total(p)
            if t < STRETCH - 1:
                p = [w[m] * p[m] for m in range(modes)]
        return tuple(fade[m] * h[m] for m in range(modes))

    def backward(i, k):
        back = stretches - 1 - i
        q = [k[m] + ks_ref[chunk, back + 1, pl.ds(m * members, members), :] for m in range(modes)]
        for t in range(STRETCH):
            row = back * STRETCH + STRETCH - 1 - t
            zo_ref[pl.ds(row * members, members), :] = z_ref[pl.ds((base * STRETCH + row) * members, members), :] + total(q)
            if t < STRETCH - 1:
                q = [w[m] * q[m] for m in range(modes)]
        return tuple(fade[m] * k[m] for m in range(modes))

    def put(source, store):
        for tile in range(tokens // 16):
            rows = pl.ds(tile * 16, 16)
            for member in range(members):
                halves = [pl.ds((tile * 16 + half * 8) * members + member, 8, stride=members) for half in range(2)]
                store(rows, member, jnp.concatenate([source[at, :] for at in halves], axis=0).astype(BF16))

    def store_y(rows, member, value):
        if own:
            cols = set_columns(ranked(me_ref, member, members), core)
            dq_ref[rows, cols] = (u_ref[rows, cols].astype(F32) * value.astype(F32)).astype(BF16)
        else:
            send_ref[0, member, rows, :] = value

    def store_z(rows, member, value):
        if own:
            cols = set_columns(ranked(me_ref, member, members), core)
            value = value.astype(F32)
            dk_ref[rows, cols] = (value * v_ref[rows, cols].astype(F32)).astype(BF16)
            dv_ref[rows, cols] = (value * k_ref[rows, cols].astype(F32)).astype(BF16)
        else:
            send_ref[1, member, rows, :] = value

    lax.fori_loop(0, stretches, forward, h, unroll=8)
    put(yo_ref, store_y)
    lax.fori_loop(0, stretches, backward, k, unroll=8)
    put(zo_ref, store_z)


def first_finish_kernel(
    me_ref, y_ref, z_ref, hs_ref, ks_ref, const_ref, enter_ref, a_ref, b_ref, c_ref, par_ref, sk_own, sk_far, send_ref, in_ref, *scratch,
    tokens, modes, members, span,
):
    sizes = dict(tokens=tokens, modes=modes, members=members)
    enter_kernel(me_ref, enter_ref, a_ref, b_ref, c_ref, par_ref, sk_own, sk_far, in_ref, span=span, **sizes)
    finish_kernel(me_ref, y_ref, z_ref, hs_ref, ks_ref, const_ref, in_ref, send_ref, *scratch, own=False, **sizes)


def last_kernel(me_ref, got_ref, k_ref, v_ref, u_ref, *refs, tokens, modes, members, span, scale, tree):
    refs = list(refs)
    if tree:
        kept_ref, a_ref, b_ref, c_ref, own_ref = refs[:5]
        refs = refs[5:]
    dq_ref, dk_ref, dv_ref, dq_hbm, dk_hbm, dv_hbm = refs[3:9]
    me = me_ref[0]
    core = me % SETS
    copies = []
    if tree:
        r_hbm, log_hbm, sems, par_sems, out_ref, group_ref = refs[9:]
        place = me // span
        group_ref[place] = kept_ref[...]
        for hop, ref in zip(HOPS, (a_ref, b_ref, c_ref)):
            for i in range(6):
                group_ref[place ^ hop, i] = ref[pl.ds((members + i) * modes, modes), :].astype(F32)
        rate, residue = own_ref[0], own_ref[1]
        w = jnp.exp(-rate)
        width = float(tokens * span)
        fade = jnp.exp(rate * -width)
        r, d, sd, _, s, _ = (group_ref[0, i] for i in range(6))
        for z in range(1, WAYS):
            r_b, d_b, sd_b, kd_b, s_b, k_b = (group_ref[z, i] for i in range(6))
            r = r + r_b + w * (s * k_b)
            d = d + d_b + w * (s * kd_b + (sd + s) * k_b)
            sd = fade * (sd + width * s) + sd_b
            s = fade * s + s_b
        root = jnp.sqrt(rate) * scale
        out_ref[0] = root * r
        out_ref[1] = root * residue * (0.5 * r - rate * d)
        for i, ref in enumerate((r_hbm, log_hbm)):
            copies.append(pltpu.make_async_copy(out_ref.at[i], ref, par_sems.at[i]))
            copies[-1].start()
    else:
        (sems,) = refs[9:]
    for tile in range(tokens // 16):
        rows = pl.ds(tile * 16, 16)
        for member in range(members):
            cols = set_columns(ranked(me_ref, member, members), 1 - core)
            y = got_ref[0, member, rows, :].astype(F32)
            z = got_ref[1, member, rows, :].astype(F32)
            dq_ref[rows, cols] = (u_ref[rows, cols].astype(F32) * y).astype(BF16)
            dk_ref[rows, cols] = (z * v_ref[rows, cols].astype(F32)).astype(BF16)
            dv_ref[rows, cols] = (z * k_ref[rows, cols].astype(F32)).astype(BF16)
        if tile % 2:
            rows = pl.ds(tile * 16 - 16, 32)
            for i, (ref, out) in enumerate(((dq_ref, dq_hbm), (dk_ref, dk_hbm), (dv_ref, dv_hbm))):
                copies.append(pltpu.make_async_copy(ref.at[rows], out.at[rows], sems.at[i, tile]))
                copies[-1].start()
    for copy in copies:
        copy.wait()


def call(body, out_shape, in_specs, flops, out_specs=None, scratch=(), aliases=None):
    return pl.pallas_call(
        body,
        out_shape=out_shape,
        in_specs=in_specs,
        out_specs=jax.tree.map(lambda _: VMEM, out_shape) if out_specs is None else out_specs,
        scratch_shapes=scratch,
        input_output_aliases=aliases or {},
        compiler_params=pltpu.CompilerParams(vmem_limit_bytes=16 * 1024 * 1024),
        cost_estimate=pl.CostEstimate(flops=flops, bytes_accessed=1024 * 1024, transcendentals=0),
    )


def exchange(value, distance, count):
    return lax.ppermute(value, "ctx", [(i, i ^ distance) for i in range(count)])


def tie(*values):
    return lax.optimization_barrier(values)


def local(query_proj, key_proj, value_proj, output_grad, residue, decay_rate):
    tokens, channels = query_proj.shape
    own_channels, modes = residue.shape
    count = lax.axis_size("ctx")
    groups = channels // LANES
    members = groups // SETS
    rows = members * modes
    length = tokens * SETS
    top = count // WAYS
    tree = groups == count == SETS * 2 * WAYS and own_channels == LANES
    work = tokens * channels * modes
    index = lax.axis_index("ctx")
    core = index % SETS
    side = (index // SETS) % 2
    me = index.astype(jnp.int32).reshape(1)

    def shape(*dims, dtype=F32):
        return jax.ShapeDtypeStruct(dims, dtype)

    half = shape(2, members, tokens, LANES, dtype=BF16)
    series = shape(length * members, LANES)
    half_series = shape(tokens * members, LANES)
    pieces = 4
    pair = shape(2, rows, LANES)
    stretches = tokens // STRETCH
    sizes = dict(tokens=tokens, modes=modes, members=members)

    states = shape(2, 2, rows // 2, LANES), shape(stretches, modes, members, LANES), shape(stretches + 1, modes, members, LANES)

    def chip_states(gated, gate_grad, par):
        out = call(
            functools.partial(state_kernel, flip=False, **sizes), states + (half_series,) * 2, [SMEM] + [VMEM] * 3, work * 2
        )(me, gated, gate_grad, par)
        return list(out)

    own_gates, send_gates = call(
        functools.partial(gate_kernel, members=members, pieces=pieces),
        (half, half),
        [SMEM] + [HBM] * 4,
        work,
        scratch=(pltpu.VMEM((4, tokens, channels), BF16), pltpu.SemaphoreType.DMA((pieces, 4))),
    )(me, *(pltpu.with_memory_space_constraint(a, pltpu.HBM) for a in (query_proj, key_proj, value_proj, output_grad)))

    (own,) = tie(jnp.stack([decay_rate.T, residue.T]))
    params, axis = own, 0
    distance = count // 2
    while distance > (1 if tree else 0):
        other = exchange(params, distance, count)
        if axis == 0:
            other, own_gates, send_gates = tie(other, own_gates, send_gates)
            got_gates = exchange(send_gates, 1, count)
            gated, gate_grad, lags = call(
                functools.partial(series_kernel, tokens=tokens, members=members),
                (shape(2, tokens * members, LANES),) * 2 + (shape(2, STRETCH, members, LANES),),
                [SMEM] + [VMEM] * 2,
                work,
            )(me, own_gates, got_gates)
        if axis == 1:
            other, gated, gate_grad, lags = tie(other, gated, gate_grad, lags)
        if tree and distance == SETS:
            par_own, par_far = (a.reshape(rows, LANES) for a in (params, other))
            states_own = chip_states(gated, gate_grad, par_own)
            par_far, states_own[0] = tie(par_far, states_own[0])
            break
        upper = (index // distance) % 2 == 1
        params = jnp.stack([jnp.where(upper, other, params), jnp.where(upper, params, other)], axis=axis)
        distance //= 2
        axis += 1
    if not tree:
        params = params.reshape((count,) + own.shape).transpose(1, 2, 0, 3).reshape(2, modes, members, SETS, LANES)
        params = lax.dynamic_index_in_dim(params, core, 3, keepdims=False).transpose(2, 0, 1, 3)
        halves = params.reshape(members // 2, 2, 2, modes, LANES)
        par_own, par_far = (
            lax.dynamic_index_in_dim(halves, s, 1, keepdims=False).reshape(rows, LANES) for s in (side, 1 - side)
        )
        states_own = chip_states(gated, gate_grad, par_own)
    par = jnp.concatenate([par_own, par_far])

    sk_own, hs_own, ks_own, *weighted_own = states_own

    def message_shapes(span):
        if span == top:
            return (shape(rows + (6 * modes if tree else 0), LANES, dtype=BF16),) * (WAYS - 1)
        return (shape(rows * 2 + (4 * rows // span if tree else 0), LANES, dtype=BF16),)

    loops = dict(part=min(2, modes), unroll=16, tree=tree, **sizes)
    half_sums = shape(4, rows // 2, LANES)
    work_sums = pltpu.VMEM((4, 2, rows // 2, LANES), F32)
    weighted = pltpu.VMEM(half_series.shape, F32)
    sk_far, hs_far, ks_far, *sums_far, tot, message = call(
        functools.partial(far_kernel, **loops),
        states + (() if tree else (half_sums,)) + (pair, *message_shapes(SETS)),
        [SMEM] + [VMEM] * 6,
        work * 5,
        scratch=(weighted, weighted, work_sums),
    )(me, gated, gate_grad, lags, par_far, sk_own, par_own)
    messages = [message]
    tot, weighted_own[0] = tie(tot, weighted_own[0])
    (sums_own,) = call(
        functools.partial(sums_kernel, flip=False, **loops), (half_sums,), [SMEM] + [VMEM] * 7, work * 3, scratch=(work_sums,)
    )(me, *weighted_own, lags, hs_own, ks_own, sk_own, par_own)

    enter, span, pair_tot, kept = tot, SETS, tot, [sums_own] if tree else []
    while span < top:
        got = exchange(messages[0], span, count)
        last = span * 2 == top
        extra = (shape(6, modes, LANES) if last else shape(4, rows // span // 2, LANES),) if tree else ()
        out = call(
            functools.partial(level_kernel, span=span, last=last, tree=tree, **sizes),
            (pair,) * (1 if last else 2) + message_shapes(span * 2) + extra,
            [SMEM] + [VMEM] * (5 if tree else 4),
            rows,
            scratch=(pltpu.VMEM((members // 2, 6, modes, LANES), F32),) if tree else (),
        )(me, tot, got, enter, par, *kept)
        if not last:
            tot, *out = out
        enter, *messages = out
        if tree:
            kept = [messages.pop()]
        if span == SETS:
            enter, hs_own, gated, gate_grad = tie(enter, hs_own, gated, gate_grad)
        span *= 2
    far = [exchange(message, hop * top, count) for hop, message in zip(HOPS, messages)]
    hs, ks, const = call(
        functools.partial(order_kernel, **sizes),
        (
            shape(2, stretches, modes * members, LANES),
            shape(2, stretches + 1, modes * members, LANES),
            shape(3, modes, members, LANES),
        ),
        [VMEM] * 5,
        work,
    )(hs_own, ks_own, hs_far, ks_far, par)
    y, z = call(functools.partial(taps_kernel, **sizes), (series, series), [SMEM] + [VMEM] * 3, work)(
        me, gated, gate_grad, par
    )
    far[0], y, hs = tie(far[0], y, hs)
    scratch = (pltpu.VMEM((tokens * members, LANES), F32),) * 2
    finish = functools.partial(finish_kernel, tokens=tokens, modes=modes, members=members)
    send_conv, states_in = call(
        functools.partial(first_finish_kernel, span=top, **sizes),
        (half, shape(2, 2, rows, LANES)),
        [SMEM] + [VMEM] * 12,
        work * 2,
        scratch=scratch,
    )(me, y, z, hs, ks, const, enter, *far, par, sk_own, sk_far)
    got_conv = exchange(send_conv, 1, count)
    grads = (shape(tokens, channels, dtype=BF16),) * 3
    done = call(functools.partial(finish, own=True), grads, [SMEM] + [VMEM] * 9, work * 2, scratch=scratch)(
        me, y, z, hs, ks, const, states_in, key_proj, value_proj, output_grad
    )
    scale = float(tokens * count) ** (-0.5)
    extra = (*kept, *far, own) if tree else ()
    first = 5 + len(extra)
    out = call(
        functools.partial(last_kernel, tokens=tokens, modes=modes, members=members, span=top, scale=scale, tree=tree),
        grads + grads + ((shape(modes, LANES),) * 2 if tree else ()),
        [SMEM] + [VMEM] * (first + 2),
        work,
        (VMEM,) * 3 + (ANY,) * (5 if tree else 3),
        (pltpu.SemaphoreType.DMA((3, tokens // 16)),)
        + ((pltpu.SemaphoreType.DMA((2,)), pltpu.VMEM((2, modes, LANES), F32), pltpu.VMEM((WAYS, 6, modes, LANES), F32)) if tree else ()),
        {first: 0, first + 1: 1, first + 2: 2},
    )(me, got_conv, key_proj, value_proj, output_grad, *extra, *done)

    if tree:
        residue_grad, log_grad = out[6].T, out[7].T
    else:
        dims = (members, modes, LANES)

        def by_member(a):
            a = a.reshape(2, members // 2, modes, LANES)
            return jnp.where(side == 0, a, a[::-1]).transpose(1, 0, 2, 3).reshape(dims)

        h_in, k_in = by_member(states_in[0, 0]), by_member(states_in[1, 1])
        s, k = (by_member(a) for a in pair_tot)
        r, d, s_d, k_d = (by_member(jnp.stack([a, b])) for a, b in zip(sums_own, sums_far[0]))
        rate = params[:, 0]
        w = jnp.exp(-rate)
        r = r + w * h_in * k
        d = d + w * (h_in * k_d + k_in * (s_d + s)) + float(length) * jnp.exp(-rate * float(length + 1)) * h_in * k_in
        parts = jnp.stack([r, d], axis=1)
        parts = jnp.stack([jnp.where(core == 0, parts, 0.0), jnp.where(core == 1, parts, 0.0)], axis=1)
        parts = parts.reshape(groups, 2, modes, LANES).transpose(1, 2, 0, 3)
        parts = parts.reshape(2, modes, count, own_channels).transpose(2, 0, 1, 3)
        sums = lax.all_to_all(parts, "ctx", split_axis=0, concat_axis=0, tiled=True).sum(axis=0)
        root = scale * jnp.sqrt(decay_rate)
        residue_grad = root * sums[0].T
        log_grad = root * residue * (0.5 * sums[0].T - decay_rate * sums[1].T)
    return out[3], out[4], out[5], residue_grad, log_grad


def solution(mesh):
    in_specs = (P("ctx", "ch"),) * 4 + (P(("ch", "ctx"), None),) * 2
    out_specs = (P("ctx", "ch"),) * 3 + (P(("ch", "ctx"), None),) * 2
    return jax.shard_map(local, mesh=mesh, in_specs=in_specs, out_specs=out_specs, check_vma=False)
```
